32 devices in a mesh: dp: 2 (over y), sp: 4 (over z), cp: 4 (over x, core).
Axes of the slice: x: 2, y: 2, z: 4, core: 2. Of those that a mesh axis runs over, the one named last changes fastest.
Arguments:
- tokens: bfloat16 [2, 4096, 1408], P('dp', ('sp', 'cp')), may hold values from -6 to 6
- skip_in: bfloat16 [2, 4096, 1408], P('dp', ('sp', 'cp')), may hold values from -6 to 6
- timestep: bfloat16 [2, 16, 1408], P('dp'), may hold values from -6 to 6
- captions: bfloat16 [2, 16, 333, 1024], P('dp', 'cp'), may hold values from -6 to 6
- null_mask: int32 [2, 16], P('dp'), may hold values 0 or 1
- lengths: int32 [2, 16], replicated, may hold values from 0 to 1024, as said below
- cotangent: bfloat16 [2, 4096, 1408], P('dp', ('sp', 'cp')), may hold values from -6 to 6
- skip_weight: bfloat16 [2816, 1408], P(('dp', 'sp', 'cp')), may hold values from -0.109375 to 0.109375
- shift_weight: bfloat16 [1408, 1408], P(('dp', 'sp', 'cp')), may hold values from -0.15625 to 0.15625
- self_input: bfloat16 [1408, 4224], P(('dp', 'sp', 'cp')), may hold values from -0.15625 to 0.15625
- self_output: bfloat16 [1408, 1408], P(('dp', 'sp', 'cp')), may hold values from -2.5 to 2.5
- cross_query: bfloat16 [1408, 1408], P(('dp', 'sp', 'cp')), may hold values from -0.15625 to 0.15625
- cross_pairs: bfloat16 [1024, 2816], P(('dp', 'sp', 'cp')), may hold values from -0.1875 to 0.1875
- cross_output: bfloat16 [1408, 1408], P(('dp', 'sp', 'cp')), may hold values from -2.5 to 2.5
- expand_weight: bfloat16 [1408, 6144], P(('dp', 'sp', 'cp')), may hold values from -0.15625 to 0.15625
- reduce_weight: bfloat16 [6144, 1408], P(None, ('dp', 'sp', 'cp')), may hold values from -0.078125 to 0.078125
- null_caption: bfloat16 [333, 1024], P(None, ('dp', 'sp', 'cp')), may hold values from -6 to 6
- norm_gains: bfloat16 [4, 1408], P(None, ('dp', 'sp', 'cp')), may hold values from 0.5 to 1.5
Outputs:
- block_out: bfloat16 [2, 4096, 1408], P('dp', ('sp', 'cp'))
- token_grad: bfloat16 [2, 4096, 1408], P('dp', ('sp', 'cp'))
- skip_grad: bfloat16 [2, 4096, 1408], P('dp', ('sp', 'cp'))
- skip_weight_grad: float32 [2816, 1408], P(('dp', 'sp', 'cp'))
- shift_weight_grad: float32 [1408, 1408], P(('dp', 'sp', 'cp'))
- self_input_grad: float32 [1408, 4224], P(('dp', 'sp', 'cp'))
- self_output_grad: float32 [1408, 1408], P(('dp', 'sp', 'cp'))
- cross_query_grad: float32 [1408, 1408], P(('dp', 'sp', 'cp'))
- cross_pairs_grad: float32 [1024, 2816], P(('dp', 'sp', 'cp'))
- cross_output_grad: float32 [1408, 1408], P(('dp', 'sp', 'cp'))
- expand_weight_grad: float32 [1408, 6144], P(('dp', 'sp', 'cp'))
- reduce_weight_grad: float32 [6144, 1408], P(None, ('dp', 'sp', 'cp'))
- null_caption_grad: float32 [333, 1024], P(None, ('dp', 'sp', 'cp'))
- norm_gains_grad: float32 [4, 1408], P(None, ('dp', 'sp', 'cp'))
The draws below stay inside these ranges and needn't reach their ends.
Inputs may be any that keep to these rules, and one draw needn't show every extreme that they name: `lengths`: row k lists the patch counts of the images of pack k in order, each 256 or 1024, followed by zeros; every pack has at least one image of 1024 patches and at least one zero; the tokens after the last image of a pack, if any, are padding.
All inputs are finite; a program needn't handle non-finite values. No bound on the sum of `null_mask` on one device may be relied on, other than what follows from the above.
Results may differ from the reference program's by a relative error of at most 0.022.
Values may be sent and summed in bfloat16 or wider, within the bound.
No kernel may reach another device: no remote copies, remote signals or barrier semaphores. Data moves between devices by JAX's collectives and lax.ppermute only.
A program may use at most 384 MiB of HBM per device.

```python
import math
import jax
import jax.numpy as jnp
from jax import lax

D = 1408
HEADS = 16
HEAD = 88
FF = 6144
DT = 1024
TEXT = 333
BIG_SIDE = 32
SMALL_SIDE = 16
PACK = 4096
ALLPACKS = 2
IMGS = 16


def draw_lengths(key, part):
    key = jax.random.fold_in(key, 7)
    big_cells = BIG_SIDE * BIG_SIDE
    small_cells = SMALL_SIDE * SMALL_SIDE

    def one_pack(pack_key):
        big_key, small_key, order_key = jax.random.split(pack_key, 3)
        big_count = jax.random.randint(big_key, (), 1, PACK // big_cells + 1)
        room = (PACK - big_count * big_cells) // small_cells
        small_count = jax.random.randint(small_key, (), 0, room + 1)
        image_count = big_count + small_count
        ranking = jax.random.permutation(order_key, IMGS)
        slot_ids = jnp.arange(IMGS)
        present = slot_ids < image_count
        ranks = jnp.sum((present[None, :] & (ranking[None, :] < ranking[:, None])).astype(jnp.int32), axis=1)
        return jnp.where(present, jnp.where(ranks < big_count, big_cells, small_cells), 0).astype(jnp.int32)
    return jax.vmap(one_pack)(jax.random.split(key, ALLPACKS))


def place_ends(values, rng, least, top_value):
    longest = values.shape.index(max(values.shape))
    spots = []
    for shift in (0, 1):
        where = [jax.random.randint(jax.random.fold_in(rng, axis), (), 0, length) for axis, length in enumerate(values.shape)]
        where[longest] = (where[longest] + shift) % values.shape[longest]
        spots.append(tuple(where))
    return values.at[spots[0]].set(least).at[spots[1]].set(top_value)


def block_levels(key, extent, shards, least, largest):
    def one(position, shards_of):
        draws = jax.random.uniform(jax.random.fold_in(jax.random.fold_in(key, 6), position), (shards_of,), jnp.float32, least / len(shards), largest / len(shards))
        return jnp.repeat(jnp.exp(draws), extent[position] // shards_of).reshape((-1,) + (1,) * (len(extent) - position - 1))

    loudness = one(*shards[0])
    for cut in shards[1:]:
        loudness = loudness * one(*cut)
    return loudness


def scatter_about(rng, shape, scale, reach, shards=(), kind=jnp.bfloat16):
    gain = block_levels(rng, shape, shards, -0.22, 0.18) if shards else 1.0
    array = jax.random.normal(rng, shape, jnp.float32) * scale * gain
    return jnp.minimum(jnp.maximum(array, -reach), reach).astype(kind)


def setup_inputs(seed: int = 0) -> dict:
    keys = jax.random.split(jax.random.key(seed), 19)
    tokens = scatter_about(keys[0], (ALLPACKS, PACK, D), 1.0, 6.0, ((0, 2), (1, 16)))
    skip_in = scatter_about(keys[1], (ALLPACKS, PACK, D), 1.0, 6.0, ((0, 2), (1, 16)))
    timestep = scatter_about(keys[2], (ALLPACKS, IMGS, D), 1.0, 6.0, ((0, 2),))
    captions = scatter_about(keys[3], (ALLPACKS, IMGS, TEXT, DT), 1.0, 6.0, ((0, 2), (1, 4)))
    null_mask = place_ends((jax.random.randint(keys[4], (ALLPACKS, IMGS), 0, 3) < 1).astype(jnp.int32), jax.random.fold_in(keys[4], 1), 0, 1)
    lengths = draw_lengths(jax.random.fold_in(keys[18], 71), 0)
    cotangent = scatter_about(keys[6], (ALLPACKS, PACK, D), 1.0, 6.0, ((0, 2), (1, 16)))
    skip_weight = scatter_about(keys[7], (2 * D, D), (2 * D) ** -0.5, 0.109375, ((0, 32),))
    shift_weight = scatter_about(keys[8], (D, D), D ** -0.5, 0.15625, ((0, 32),))
    self_input = scatter_about(keys[9], (D, 3 * D), D ** -0.5, 0.15625, ((0, 32),))
    self_output = scatter_about(keys[10], (D, D), (max(D // 256, 1)) ** -0.5, 2.5, ((0, 32),))
    cross_query = scatter_about(keys[11], (D, D), D ** -0.5, 0.15625, ((0, 32),))
    cross_pairs = scatter_about(keys[12], (DT, 2 * D), DT ** -0.5, 0.1875, ((0, 32),))
    cross_output = scatter_about(keys[13], (D, D), (max(D // 256, 1)) ** -0.5, 2.5, ((0, 32),))
    expand_weight = scatter_about(keys[14], (D, FF), D ** -0.5, 0.15625, ((0, 32),))
    reduce_weight = scatter_about(keys[15], (FF, D), FF ** -0.5, 0.078125, ((1, 32),))
    null_caption = scatter_about(keys[16], (TEXT, DT), 1.0, 6.0, ((1, 32),))
    norm_gains = jnp.clip(1.0 + 0.1 * jax.random.normal(keys[17], (4, D), jnp.float32), 0.5, 1.5).astype(jnp.bfloat16)
    return dict(tokens=tokens, skip_in=skip_in, timestep=timestep, captions=captions, null_mask=null_mask, lengths=lengths, cotangent=cotangent, skip_weight=skip_weight, shift_weight=shift_weight, self_input=self_input, self_output=self_output, cross_query=cross_query, cross_pairs=cross_pairs, cross_output=cross_output, expand_weight=expand_weight, reduce_weight=reduce_weight, null_caption=null_caption, norm_gains=norm_gains)


@jax.custom_vjp
def low(v):
    return lax.optimization_barrier(v.astype(jnp.bfloat16)).astype(jnp.float32)

@jax.custom_vjp
def low_back(v):
    return v

def low_keep(v):
    return (low(v), None)

def low_pass(kept, grad):
    return (grad,)

def back_keep(v):
    return (v, None)

def back_low(kept, grad):
    return (low(grad),)
low.defvjp(low_keep, low_pass)
low_back.defvjp(back_keep, back_low)
epsilon = 1e-06
highest = lax.Precision.HIGHEST

def matmul(left, right):
    return jnp.matmul(left, right, precision=highest)

def layer_norm(vector):
    centred = vector - lax.optimization_barrier(jnp.mean(vector, axis=-1, keepdims=True))
    return centred * lax.rsqrt(lax.optimization_barrier(jnp.mean(centred * centred, axis=-1, keepdims=True)) + epsilon)

def segment_info(lengths, positions):
    seg_ends = jnp.cumsum(lengths).astype(jnp.int32)
    starts = (seg_ends - lengths).astype(jnp.int32)
    present = lengths > 0
    slot_ids = jnp.arange(lengths.shape[0], dtype=jnp.int32)
    segment = lax.optimization_barrier(jnp.sum(((seg_ends[None, :] <= positions[:, None]) & present[None, :]).astype(jnp.int32), axis=1)).astype(jnp.int32)
    onehot = segment[:, None] == slot_ids[None, :]
    seg_start = lax.optimization_barrier(jnp.sum(jnp.where(onehot, starts[None, :], 0), axis=1)).astype(jnp.int32)
    seg_size = lax.optimization_barrier(jnp.sum(jnp.where(onehot, lengths[None, :], 0), axis=1)).astype(jnp.int32)
    side_len = jnp.where(seg_size == BIG_SIDE * BIG_SIDE, BIG_SIDE, SMALL_SIDE).astype(jnp.int32)
    offset = (positions - seg_start).astype(jnp.int32)
    images = jnp.sum(present.astype(jnp.int32)).astype(jnp.int32)
    return (segment, offset // side_len, offset % side_len, (segment < images).astype(jnp.float32))

def rope_tables(grid_row, grid_col):
    quarter = HEAD // 4
    frequency = jnp.exp(jnp.arange(quarter, dtype=jnp.float32) * (-math.log(10000.0) / quarter))
    angles = jnp.stack([grid_row.astype(jnp.float32)[:, None] * frequency, grid_col.astype(jnp.float32)[:, None] * frequency], axis=1)
    return (jnp.cos(angles), jnp.sin(angles))

def rotate(vector, cosine, sines):
    quarter = HEAD // 4
    split = vector.reshape(vector.shape[:-1] + (2, 2, quarter))
    former = split[..., 0, :]
    latter = split[..., 1, :]
    cosine = jnp.expand_dims(cosine, -3)
    sines = jnp.expand_dims(sines, -3)
    turned = jnp.stack([former * cosine - latter * sines, former * sines + latter * cosine], axis=-2)
    return turned.reshape(vector.shape)

def attend(query_rows, key_rows, value_rows, allowed):
    scores = low_back(jnp.einsum('nhe,mhe->hnm', query_rows, key_rows, precision=highest) * (1.0 / math.sqrt(HEAD)))
    weights = jnp.exp(scores) * allowed
    totals = lax.optimization_barrier(jnp.sum(weights, axis=-1))
    summed = low_back(jnp.einsum('hnm,mhe->nhe', low(weights), value_rows, precision=highest))
    return summed / jnp.transpose(totals)[:, :, None]

def self_attention(queries, key_rows, value_rows, segment):
    block_rows = min(512, PACK)

    def one_block(block_id):
        rows_query = lax.dynamic_slice_in_dim(queries, block_id * block_rows, block_rows, 0)
        rows_segment = lax.dynamic_slice_in_dim(segment, block_id * block_rows, block_rows, 0)
        allowed = (rows_segment[:, None] == segment[None, :]).astype(jnp.float32)[None]
        return attend(rows_query, key_rows, value_rows, allowed)
    blocks = lax.map(jax.checkpoint(one_block), jnp.arange(PACK // block_rows, dtype=jnp.int32))
    return blocks.reshape(PACK, HEADS, HEAD)

def cross_attention(queries, text_keys, text_values, segment):
    cell_rows = SMALL_SIDE * SMALL_SIDE

    def one_block(block_id):
        rows_query = lax.dynamic_slice_in_dim(queries, block_id * cell_rows, cell_rows, 0)
        image_id = lax.dynamic_slice_in_dim(segment, block_id * cell_rows, 1, 0)[0]
        keys_here = lax.dynamic_index_in_dim(text_keys, image_id, 0, keepdims=False)
        values_here = lax.dynamic_index_in_dim(text_values, image_id, 0, keepdims=False)
        return attend(rows_query, keys_here, values_here, 1.0)
    blocks = lax.map(jax.checkpoint(one_block), jnp.arange(PACK // cell_rows, dtype=jnp.int32))
    return blocks.reshape(PACK, HEADS, HEAD)

def pack_forward(weights, tokens, skip_in, timestep, captions, null_mask, lengths):
    skip_weight, shift_weight, self_input, self_output, cross_query, cross_pairs, cross_output, expand_weight, reduce_weight, null_caption, norm_gains = weights
    segment, grid_row, grid_col, valid_rows = segment_info(lengths, jnp.arange(PACK, dtype=jnp.int32))
    joined = jnp.concatenate([tokens, skip_in], axis=1)
    base_stream = layer_norm(low_back(matmul(joined, skip_weight))) * norm_gains[0]
    shift_table = matmul(low(jax.nn.silu(timestep)), shift_weight)
    onehot = (segment[:, None] == jnp.arange(IMGS, dtype=jnp.int32)[None, :]).astype(jnp.float32)
    normed_self = low(layer_norm(base_stream) * norm_gains[1] + matmul(onehot, shift_table))
    projected = low_back(matmul(normed_self, self_input)).reshape(PACK, 3, HEADS, HEAD)
    cosine, sines = rope_tables(grid_row, grid_col)
    queries = low_back(low(rotate(layer_norm(projected[:, 0]), cosine, sines)))
    key_rows = low_back(low(rotate(layer_norm(projected[:, 1]), cosine, sines)))
    value_rows = low_back(low(projected[:, 2]))
    attended = low_back(low(self_attention(queries, key_rows, value_rows, segment))).reshape(PACK, D)
    mid_stream = base_stream + low_back(matmul(attended, self_output))
    normed_cross = low(layer_norm(mid_stream) * norm_gains[2])
    cross_raw = low_back(matmul(normed_cross, cross_query)).reshape(PACK, HEADS, HEAD)
    cross_queries = low_back(low(layer_norm(cross_raw)))
    chosen = jnp.where(null_mask[:, None, None] > 0, null_caption[None], captions)
    paired = matmul(chosen, cross_pairs)
    text_raw = low_back(paired[..., :D]).reshape(IMGS, TEXT, HEADS, HEAD)
    text_keys = low_back(low(layer_norm(text_raw)))
    text_values = low_back(low(paired[..., D:])).reshape(IMGS, TEXT, HEADS, HEAD)
    crossed = low_back(low(cross_attention(cross_queries, text_keys, text_values, segment))).reshape(PACK, D)
    late_stream = mid_stream + low_back(matmul(crossed, cross_output))
    normed_ffn = low(layer_norm(late_stream) * norm_gains[3])
    hidden = low(jax.nn.gelu(low_back(matmul(normed_ffn, expand_weight)), approximate=True))
    return late_stream + low_back(matmul(hidden, reduce_weight))

def reference(tokens, skip_in, timestep, captions, null_mask, lengths, cotangent, skip_weight, shift_weight, self_input, self_output, cross_query, cross_pairs, cross_output, expand_weight, reduce_weight, null_caption, norm_gains):
    params = tuple((member.astype(jnp.float32) for member in (skip_weight, shift_weight, self_input, self_output, cross_query, cross_pairs, cross_output, expand_weight, reduce_weight, null_caption, norm_gains)))
    time_values = timestep.astype(jnp.float32)
    caption_values = captions.astype(jnp.float32)

    def forward(token_values, skip_values, weights):

        def one_pack(carried, member):
            return (carried, pack_forward(weights, *member))
        scanned = lax.scan(one_pack, None, (token_values, skip_values, time_values, caption_values, null_mask, lengths))
        return scanned[1]
    result, pull_back = jax.vjp(forward, tokens.astype(jnp.float32), skip_in.astype(jnp.float32), params)
    valid_rows = jax.vmap(lambda length_row: segment_info(length_row, jnp.arange(PACK, dtype=jnp.int32))[3])(lengths)
    token_part, skip_part, weight_grads = pull_back(cotangent.astype(jnp.float32) * valid_rows[:, :, None])
    factor = lengths.shape[0] * PACK / jnp.sum(lengths).astype(jnp.float32)
    return (result.astype(jnp.bfloat16), (token_part * factor).astype(jnp.bfloat16), (skip_part * factor).astype(jnp.bfloat16), weight_grads[0] * factor, weight_grads[1] * factor, weight_grads[2] * factor, weight_grads[3] * factor, weight_grads[4] * factor, weight_grads[5] * factor, weight_grads[6] * factor, weight_grads[7] * factor, weight_grads[8] * factor, weight_grads[9] * factor, weight_grads[10] * factor)
```

```python
import functools
import math

import jax
import jax.numpy as jnp
from jax import lax
from jax.experimental import pallas as pl
from jax.experimental.pallas import tpu as pltpu
from jax.sharding import PartitionSpec as P

D = 1408
HEADS = 16
HEAD = 88
DT = 1024
TEXT = 333
TEXT_PAD = 384
BIG_SIDE = 32
SMALL_SIDE = 16
PACK = 4096
IMGS = 16
CELL = 256
CELLS = PACK // CELL
SCALING = 1.0 / math.sqrt(HEAD)

epsilon = 1e-06
highest = lax.Precision.HIGHEST
bf16 = jnp.bfloat16
f32 = jnp.float32
GROUP = ("dp", "sp")
EVERY = ("dp", "sp", "cp")
HEAD_ORDER = ("cp", "sp")


def layer_norm(vector, axis=-1):
    centred = vector - jnp.mean(vector, axis=axis, keepdims=True)
    return centred * lax.rsqrt(jnp.mean(centred * centred, axis=axis, keepdims=True) + epsilon)


def head_norm(vector):
    return layer_norm(vector, -2)


def norm_gain(vector, gain):
    return layer_norm(vector) * gain


def dot(left, right, left_dim, right_dim):
    return lax.dot_general(
        left, right, (((left_dim,), (right_dim,)), ((), ())), preferred_element_type=f32
    )


def segment_info(lengths, positions):
    seg_ends = jnp.cumsum(lengths)
    starts = seg_ends - lengths
    present = lengths > 0
    slot_ids = jnp.arange(lengths.shape[0], dtype=jnp.int32)
    segment = jnp.sum(
        ((seg_ends[None, :] <= positions[:, None]) & present[None, :]).astype(jnp.int32), axis=1
    )
    onehot = segment[:, None] == slot_ids[None, :]
    seg_start = jnp.sum(jnp.where(onehot, starts[None, :], 0), axis=1)
    seg_size = jnp.sum(jnp.where(onehot, lengths[None, :], 0), axis=1)
    side_len = jnp.where(seg_size == BIG_SIDE * BIG_SIDE, BIG_SIDE, SMALL_SIDE).astype(jnp.int32)
    offset = positions - seg_start
    images = jnp.sum(present.astype(jnp.int32))
    return (segment, offset // side_len, offset % side_len, (segment < images).astype(f32))


def cell_ranges(lengths):
    positions = jnp.arange(CELLS, dtype=jnp.int32) * CELL
    seg_ends = jnp.cumsum(lengths)
    present = lengths > 0
    segment = jnp.sum(
        ((seg_ends[None, :] <= positions[:, None]) & present[None, :]).astype(jnp.int32), axis=1
    )
    same = segment[:, None] == segment[None, :]
    cells = jnp.arange(CELLS, dtype=jnp.int32)
    first = jnp.min(jnp.where(same, cells[None, :], CELLS), axis=1)
    last = jnp.max(jnp.where(same, cells[None, :] + 1, 0), axis=1)
    return (first, last, jnp.sum(lengths) // CELL)


def rope_tables(grid_row, grid_col):
    quarter = HEAD // 4
    frequency = jnp.exp(jnp.arange(quarter, dtype=f32) * (-math.log(10000.0) / quarter))
    angles = jnp.concatenate(
        [
            frequency[:, None] * grid_row.astype(f32)[None, :],
            frequency[:, None] * grid_col.astype(f32)[None, :],
        ],
        axis=0,
    )
    return (jnp.cos(angles), jnp.sin(angles))


def rotate(vector, cosine, sines):
    quarter = HEAD // 4
    one, two, three, four = (
        vector[..., k * quarter : (k + 1) * quarter, :] for k in range(4)
    )
    cos_row, cos_col = cosine[..., :quarter, :], cosine[..., quarter:, :]
    sin_row, sin_col = sines[..., :quarter, :], sines[..., quarter:, :]
    return jnp.concatenate(
        [
            one * cos_row - two * sin_row,
            one * sin_row + two * cos_row,
            three * cos_col - four * sin_col,
            three * sin_col + four * cos_col,
        ],
        axis=-2,
    )


def turn_norm(vector, cosine, sines):
    return rotate(head_norm(vector), cosine, sines)


def swap_core(value):
    return lax.ppermute(value, "cp", [(0, 1), (1, 0), (2, 3), (3, 2)])


def swap_chip(value):
    return lax.ppermute(value, "cp", [(0, 2), (2, 0), (1, 3), (3, 1)])


def gather_cp(value):
    count = lax.axis_size("cp")
    if count != 4:
        return lax.all_gather(value, "cp", axis=0, tiled=False)
    index = lax.axis_index("cp")
    chip, core = index // 2, index % 2
    other = swap_chip(value)
    pair = jnp.where(chip == 0, jnp.stack([value, other]), jnp.stack([other, value]))
    second = swap_core(pair)
    return jnp.where(
        core == 0, jnp.stack([pair, second], axis=1), jnp.stack([second, pair], axis=1)
    ).reshape((4,) + value.shape)


def scatter_cp(partial):
    count = lax.axis_size("cp")
    partial = partial.astype(bf16)
    if count != 4:
        return lax.psum_scatter(partial, "cp", scatter_dimension=0, tiled=False).astype(f32)
    index = lax.axis_index("cp")
    chip, core = index // 2, index % 2
    parts = partial.reshape((2, 2) + partial.shape[1:])
    keep = lax.dynamic_index_in_dim(parts, core, 1, keepdims=False)
    send = lax.dynamic_index_in_dim(parts, 1 - core, 1, keepdims=False)
    both = (keep.astype(f32) + swap_core(send).astype(f32)).astype(bf16)
    keep = lax.dynamic_index_in_dim(both, chip, 0, keepdims=False)
    send = lax.dynamic_index_in_dim(both, 1 - chip, 0, keepdims=False)
    return keep.astype(f32) + swap_chip(send).astype(f32)


def trade_cp(blocks):
    return lax.all_to_all(blocks, "cp", split_axis=0, concat_axis=0, tiled=True)


def flip(block):
    return jnp.transpose(block.astype(f32)).astype(bf16)


def kernel_dot(left, right, left_dim=1, right_dim=0):
    return lax.dot_general(
        left, right, (((left_dim,), (right_dim,)), ((), ())), preferred_element_type=f32
    )


def over_cells(first, last, step, carry):
    count = last - first
    fours = count // 4

    def four(turn, current):
        for k in range(4):
            current = step(first + turn * 4 + k, current)
        return current

    carry = lax.fori_loop(0, fours, four, carry)
    return lax.fori_loop(first + fours * 4, last, step, carry)


def self_forward_kernel(first_ref, last_ref, qkv_ref, out_ref, total_ref, keys):
    pair = pl.program_id(0)
    per = qkv_ref.shape[-1] // CELL

    def where(cell):
        return cell // per, pl.ds(pl.multiple_of((cell % per) * CELL, CELL), CELL)

    def turn_keys(cell, carry):
        chunk, lanes = where(cell)
        keys[cell] = flip(qkv_ref[chunk, 0, 1, :, lanes])
        return carry

    lax.fori_loop(0, CELLS, turn_keys, 0)

    def one_cell(cell, carry):
        chunk, lanes = where(cell)
        query = qkv_ref[chunk, 0, 0, :, lanes]

        def step(other, current):
            summed, totals = current
            key_chunk, key_lanes = where(other)
            weights = jnp.exp(kernel_dot(keys[other], query) * SCALING)
            totals = totals + jnp.sum(weights, axis=0, keepdims=True)
            summed = summed + kernel_dot(
                qkv_ref[key_chunk, 0, 2, :, key_lanes], weights.astype(bf16)
            )
            return (summed, totals)

        summed, totals = over_cells(
            first_ref[pair, cell],
            last_ref[pair, cell],
            step,
            (jnp.zeros((HEAD, CELL), f32), jnp.zeros((1, CELL), f32)),
        )
        out_ref[chunk, 0, :, lanes] = summed / totals
        total_ref[chunk, 0, :, lanes] = totals
        return carry

    lax.fori_loop(0, CELLS, one_cell, 0)


def self_backward_kernel(
    first_ref,
    last_ref,
    valid_ref,
    qkv_ref,
    grad_ref,
    out_ref,
    total_ref,
    result_ref,
    keys,
    values,
    key_sums,
    value_sums,
):
    pair = pl.program_id(0)
    per = qkv_ref.shape[-1] // CELL

    def where(cell):
        return cell // per, pl.ds(pl.multiple_of((cell % per) * CELL, CELL), CELL)

    def prepare(cell, carry):
        chunk, lanes = where(cell)
        keys[cell] = flip(qkv_ref[chunk, 0, 1, :, lanes])
        values[cell] = flip(qkv_ref[chunk, 0, 2, :, lanes])
        key_sums[cell] = jnp.zeros((HEAD, CELL), f32)
        value_sums[cell] = jnp.zeros((HEAD, CELL), f32)
        result_ref[chunk, 0, 0, :, lanes] = jnp.zeros((HEAD, CELL), bf16)
        return carry

    lax.fori_loop(0, CELLS, prepare, 0)

    def one_cell(cell, carry):
        chunk, lanes = where(cell)
        query = qkv_ref[chunk, 0, 0, :, lanes]
        grad = grad_ref[chunk, 0, :, lanes].astype(f32)
        inverse = 1.0 / total_ref[chunk, 0, :, lanes]
        scaled = (grad * inverse).astype(bf16)
        total_grad = (
            -jnp.sum(grad * out_ref[chunk, 0, :, lanes], axis=0, keepdims=True) * inverse
        )

        def step(other, query_sum):
            key_chunk, key_lanes = where(other)
            weights = jnp.exp(kernel_dot(keys[other], query) * SCALING)
            weight_grad = kernel_dot(values[other], scaled)
            score_grad = (weights * (weight_grad + total_grad)).astype(bf16)
            value_sums[other] += kernel_dot(scaled, weights.astype(bf16), 1, 1)
            key_sums[other] += kernel_dot(query, score_grad, 1, 1)
            return query_sum + kernel_dot(qkv_ref[key_chunk, 0, 1, :, key_lanes], score_grad)

        query_sum = over_cells(
            first_ref[pair, cell], last_ref[pair, cell], step, jnp.zeros((HEAD, CELL), f32)
        )
        result_ref[chunk, 0, 0, :, lanes] = (query_sum * SCALING).astype(bf16)
        return carry

    lax.fori_loop(0, valid_ref[pair], one_cell, 0)

    def finish(cell, carry):
        chunk, lanes = where(cell)
        result_ref[chunk, 0, 1, :, lanes] = (key_sums[cell] * SCALING).astype(bf16)
        result_ref[chunk, 0, 2, :, lanes] = value_sums[cell].astype(bf16)
        return carry

    lax.fori_loop(0, CELLS, finish, 0)


def pair_spec(shape):
    block = (shape[0], 1) + shape[2:]
    rest = (0,) * (len(shape) - 2)
    return pl.BlockSpec(block, lambda pair, *_: (0, pair) + rest)


VMEM_LIMIT = 40 * 1024 * 1024


def self_forward(qkv, first, last):
    chunks, pairs, _, _, columns = qkv.shape
    out_shape = (chunks, pairs, HEAD, columns)
    total_shape = (chunks, pairs, 1, columns)
    return pl.pallas_call(
        self_forward_kernel,
        out_shape=(
            jax.ShapeDtypeStruct(out_shape, f32),
            jax.ShapeDtypeStruct(total_shape, f32),
        ),
        grid_spec=pltpu.PrefetchScalarGridSpec(
            num_scalar_prefetch=2,
            grid=(pairs,),
            in_specs=[pair_spec(qkv.shape)],
            out_specs=[pair_spec(out_shape), pair_spec(total_shape)],
            scratch_shapes=[pltpu.VMEM((CELLS, CELL, HEAD), bf16)],
        ),
        compiler_params=pltpu.CompilerParams(vmem_limit_bytes=VMEM_LIMIT),
        name="self_forward",
    )(first, last, qkv)


def self_backward(qkv, grad, out, totals, first, last, valid):
    pairs = qkv.shape[1]
    return pl.pallas_call(
        self_backward_kernel,
        out_shape=jax.ShapeDtypeStruct(qkv.shape, bf16),
        grid_spec=pltpu.PrefetchScalarGridSpec(
            num_scalar_prefetch=3,
            grid=(pairs,),
            in_specs=[
                pair_spec(qkv.shape),
                pair_spec(grad.shape),
                pair_spec(out.shape),
                pair_spec(totals.shape),
            ],
            out_specs=pair_spec(qkv.shape),
            scratch_shapes=[
                pltpu.VMEM((CELLS, CELL, HEAD), bf16),
                pltpu.VMEM((CELLS, CELL, HEAD), bf16),
                pltpu.VMEM((CELLS, HEAD, CELL), f32),
                pltpu.VMEM((CELLS, HEAD, CELL), f32),
            ],
        ),
        compiler_params=pltpu.CompilerParams(vmem_limit_bytes=VMEM_LIMIT),
        name="self_backward",
    )(first, last, valid, qkv, grad, out, totals)


def text_weights(key_block, query):
    scores = kernel_dot(flip(key_block), query) * SCALING
    present = lax.broadcasted_iota(jnp.int32, scores.shape, 0) < TEXT
    return jnp.where(present, jnp.exp(scores), 0.0)


def cross_forward_kernel(query_ref, key_ref, value_ref, out_ref, total_ref):
    for head in range(query_ref.shape[0]):
        weights = text_weights(key_ref[head], query_ref[head])
        totals = jnp.sum(weights, axis=0, keepdims=True)
        out_ref[head] = kernel_dot(value_ref[head], weights.astype(bf16)) / totals
        total_ref[head] = totals


def cross_backward_kernel(
    query_ref,
    key_ref,
    value_ref,
    grad_ref,
    out_ref,
    total_ref,
    query_grad_ref,
    key_grad_ref,
    value_grad_ref,
):
    for head in range(query_ref.shape[0]):
        query, keys = query_ref[head], key_ref[head]
        grad = grad_ref[head].astype(f32)
        inverse = 1.0 / total_ref[head]
        scaled = (grad * inverse).astype(bf16)
        total_grad = -jnp.sum(grad * out_ref[head], axis=0, keepdims=True) * inverse
        weights = text_weights(keys, query)
        weight_grad = kernel_dot(flip(value_ref[head]), scaled)
        score_grad = (weights * (weight_grad + total_grad)).astype(bf16)
        query_grad_ref[head] = kernel_dot(keys, score_grad) * SCALING
        key_grad_ref[head] = kernel_dot(query, score_grad, 1, 1) * SCALING
        value_grad_ref[head] = kernel_dot(scaled, weights.astype(bf16), 1, 1)


HEADS_STEP = 4


def head_spec(shape):
    return pl.BlockSpec((HEADS_STEP,) + shape[1:], lambda step: (step, 0, 0))


def cross_forward(queries, keys, values):
    count, _, rows = queries.shape
    out_shape = (count, HEAD, rows)
    total_shape = (count, 1, rows)
    return pl.pallas_call(
        cross_forward_kernel,
        out_shape=(
            jax.ShapeDtypeStruct(out_shape, f32),
            jax.ShapeDtypeStruct(total_shape, f32),
        ),
        grid=(count // HEADS_STEP,),
        in_specs=[head_spec(queries.shape), head_spec(keys.shape), head_spec(values.shape)],
        out_specs=[head_spec(out_shape), head_spec(total_shape)],
        compiler_params=pltpu.CompilerParams(vmem_limit_bytes=VMEM_LIMIT),
        name="cross_forward",
    )(queries, keys, values)


def cross_backward(queries, keys, values, grad, out, totals):
    inputs = (queries, keys, values, grad, out, totals)
    return pl.pallas_call(
        cross_backward_kernel,
        out_shape=(
            jax.ShapeDtypeStruct(queries.shape, f32),
            jax.ShapeDtypeStruct(keys.shape, f32),
            jax.ShapeDtypeStruct(values.shape, f32),
        ),
        grid=(queries.shape[0] // HEADS_STEP,),
        in_specs=[head_spec(member.shape) for member in inputs],
        out_specs=[head_spec(queries.shape), head_spec(keys.shape), head_spec(values.shape)],
        compiler_params=pltpu.CompilerParams(vmem_limit_bytes=VMEM_LIMIT),
        name="cross_backward",
    )(*inputs)


def shards(
    tokens,
    skip_in,
    timestep,
    captions,
    null_mask,
    lengths,
    cotangent,
    skip_weight,
    shift_weight,
    self_input,
    self_output,
    cross_query,
    cross_pairs,
    cross_output,
    expand_weight,
    reduce_weight,
    null_caption,
    norm_gains,
):
    sp_count, cp_count = lax.axis_size("sp"), lax.axis_size("cp")
    dp_count = lax.axis_size("dp")
    dp_index, sp_index, cp_index = (lax.axis_index(name) for name in EVERY)
    place = (dp_index * sp_count + sp_index) * cp_count + cp_index
    packs, rows = tokens.shape[0], tokens.shape[1]
    held = packs * rows
    chunk = cp_count * rows
    group_heads = HEADS // cp_count
    pairs_dev = packs * group_heads // sp_count
    all_packs = lengths.shape[0]

    def split_columns(weight):
        columns = weight.shape[1] // cp_count
        blocks = jnp.swapaxes(weight.reshape(weight.shape[0], cp_count, columns), 0, 1)
        return trade_cp(blocks).reshape(cp_count * weight.shape[0], columns)

    def join_columns(part):
        count = part.shape[0] // cp_count
        blocks = trade_cp(part.reshape(cp_count, count, part.shape[1]))
        return jnp.swapaxes(blocks, 0, 1).reshape(count, cp_count * part.shape[1])

    def gather_part(weight):
        return lax.all_gather(split_columns(weight), GROUP, axis=0, tiled=True)

    def gather_whole(weight):
        return lax.all_gather(weight, EVERY, axis=0, tiled=True)

    def order_heads(weight):
        split = weight.reshape(weight.shape[0], 3, cp_count, -1)
        return jnp.swapaxes(split, 1, 2).reshape(weight.shape)

    def restore_heads(weight):
        split = weight.reshape(weight.shape[0], cp_count, 3, -1)
        return jnp.swapaxes(split, 1, 2).reshape(weight.shape)

    skip_full = gather_whole(skip_weight)
    input_part = gather_part(order_heads(self_input))
    output_full = gather_whole(self_output)
    query_full = gather_whole(cross_query)
    pairs_full = gather_whole(cross_pairs)
    cross_full = gather_whole(cross_output)
    expand_part = gather_part(expand_weight)
    reduce_part = gather_part(jnp.transpose(reduce_weight))
    gain_rows = lax.all_gather(norm_gains, EVERY, axis=1, tiled=True).astype(f32)
    caption_shard = jnp.pad(jnp.transpose(null_caption), ((0, 0), (0, TEXT_PAD - TEXT)))
    caption_full = jnp.transpose(gather_whole(caption_shard))

    own_lengths = lax.dynamic_slice_in_dim(lengths, dp_index * packs, packs, 0)
    describe = jax.vmap(segment_info, in_axes=(0, None))
    chunk_pos = sp_index * chunk + jnp.arange(chunk, dtype=jnp.int32)
    _, chunk_row, chunk_col, _ = describe(own_lengths, chunk_pos)
    block_pos = jnp.arange(sp_count * cp_count, dtype=jnp.int32) * rows
    all_segments, _, _, all_valid = describe(lengths, block_pos)
    own_segments = lax.dynamic_slice_in_dim(all_segments, dp_index * packs, packs, 0)
    own_valid = lax.dynamic_slice_in_dim(all_valid, dp_index * packs, packs, 0)
    block = sp_index * cp_count + cp_index
    block_image = lax.dynamic_index_in_dim(own_segments, block, 1, keepdims=False)
    block_valid = lax.dynamic_index_in_dim(own_valid, block, 1, keepdims=False)
    token_valid = jnp.broadcast_to(block_valid[:, None], (packs, rows)).reshape(held, 1)
    pair_pack = (sp_index * pairs_dev + jnp.arange(pairs_dev, dtype=jnp.int32)) // group_heads
    first_cells, last_cells, valid_cells = jax.vmap(cell_ranges)(own_lengths)
    first_cells = jnp.take(first_cells, pair_pack, axis=0)
    last_cells = jnp.take(last_cells, pair_pack, axis=0)
    valid_cells = jnp.take(valid_cells, pair_pack, axis=0)

    times = lax.all_gather(timestep, "dp", axis=0, tiled=True)
    silu_all = jax.nn.silu(times.astype(f32)).astype(bf16)
    shard_rows = shift_weight.shape[0]
    silu_own = lax.dynamic_slice_in_dim(silu_all, place * shard_rows, shard_rows, 2)
    shift_table = lax.psum(
        dot(silu_own.reshape(all_packs * IMGS, shard_rows), shift_weight, 1, 0), EVERY
    ).reshape(all_packs, IMGS, D)
    own_table = lax.dynamic_slice_in_dim(shift_table, dp_index * packs, packs, 0)
    slot_ids = jnp.arange(IMGS, dtype=jnp.int32)
    block_pick = (block_image[:, None] == slot_ids[None, :]).astype(f32)
    shifts = jnp.einsum("pi,pid->pd", block_pick, own_table, precision=highest)
    shift_rows = jnp.broadcast_to(shifts[:, None, :], (packs, rows, D)).reshape(held, D)

    image_dev = captions.shape[1]
    near = lax.dynamic_slice_in_dim(own_segments, sp_index * cp_count, cp_count, 1)
    local = jnp.clip(near - cp_index * image_dev, 0, image_dev - 1)
    offered = jnp.stack(
        [
            jnp.stack(
                [
                    lax.dynamic_index_in_dim(captions[p], local[p, k], 0, keepdims=False)
                    for p in range(packs)
                ]
            )
            for k in range(cp_count)
        ]
    )
    offered = jnp.pad(offered, ((0, 0), (0, 0), (0, TEXT_PAD - TEXT), (0, 0)))
    arrived = trade_cp(offered)
    own_null = jnp.take_along_axis(
        null_mask, block_image[:, None], axis=1
    )[:, 0]
    chosen = jnp.stack(
        [
            jnp.where(
                own_null[p] > 0,
                caption_full,
                lax.dynamic_index_in_dim(
                    arrived[:, p], block_image[p] // image_dev, 0, keepdims=False
                ),
            )
            for p in range(packs)
        ]
    )

    joined = jnp.concatenate([tokens.reshape(held, D), skip_in.reshape(held, D)], axis=1)
    mixed = dot(joined, skip_full, 1, 0)
    base_stream = norm_gain(mixed, gain_rows[0])
    normed_self = (norm_gain(base_stream, gain_rows[1]) + shift_rows).astype(bf16)
    normed_all = gather_cp(normed_self)
    projected = dot(input_part, normed_all.reshape(cp_count * held, D), 0, 1)
    projected = jnp.transpose(
        projected.reshape(3, group_heads, HEAD, cp_count, packs, rows), (4, 1, 0, 2, 3, 5)
    ).reshape(packs, group_heads, 3, HEAD, chunk)
    cosine, sines = jax.vmap(rope_tables)(chunk_row, chunk_col)
    cosine, sines = cosine[:, None], sines[:, None]
    query_raw, key_raw = projected[:, :, 0], projected[:, :, 1]
    queries = turn_norm(query_raw, cosine, sines).astype(bf16)
    key_rows = turn_norm(key_raw, cosine, sines).astype(bf16)
    value_rows = projected[:, :, 2].astype(bf16)
    qkv = jnp.stack([queries, key_rows, value_rows], axis=2)

    def to_heads(value):
        value = value.reshape((sp_count, pairs_dev) + value.shape[2:])
        return lax.all_to_all(value, "sp", split_axis=0, concat_axis=0, tiled=True)

    def from_heads(value):
        value = lax.all_to_all(value, "sp", split_axis=0, concat_axis=0, tiled=True)
        return value.reshape((packs, group_heads) + value.shape[2:])

    qkv = to_heads(qkv)
    out_self, totals_self = self_forward(qkv, first_cells, last_cells)

    def to_tokens(value):
        value = value.reshape(sp_count, pairs_dev, HEAD, cp_count, rows)
        value = jnp.transpose(value, (3, 0, 1, 2, 4))
        value = value.reshape(cp_count * sp_count, pairs_dev, HEAD, rows)
        value = lax.all_to_all(value, HEAD_ORDER, split_axis=0, concat_axis=0, tiled=True)
        value = value.reshape(cp_count, packs, group_heads, HEAD, rows)
        return jnp.transpose(value, (0, 2, 3, 1, 4)).reshape(D, held)

    def by_heads(value):
        value = value.reshape(cp_count, group_heads, HEAD, packs, rows)
        value = jnp.transpose(value, (0, 3, 1, 2, 4))
        value = value.reshape(cp_count * sp_count, pairs_dev, HEAD, rows)
        value = lax.all_to_all(value, HEAD_ORDER, split_axis=0, concat_axis=0, tiled=True)
        value = value.reshape(cp_count, sp_count, pairs_dev, HEAD, rows)
        return jnp.transpose(value, (1, 2, 3, 0, 4)).reshape(sp_count, pairs_dev, HEAD, chunk)

    def heads_of(value):
        value = value.reshape(HEADS, HEAD, packs, rows)
        return jnp.transpose(value, (2, 0, 1, 3)).reshape(packs * HEADS, HEAD, rows)

    def rows_of(value):
        value = value.reshape(packs, HEADS, HEAD, rows)
        return jnp.transpose(value, (1, 2, 0, 3)).reshape(D, held)

    attended = to_tokens(out_self.astype(bf16))
    mid_stream = base_stream + dot(attended, output_full, 0, 0)
    normed_cross = norm_gain(mid_stream, gain_rows[2]).astype(bf16)
    cross_raw = heads_of(dot(query_full, normed_cross, 0, 1))
    cross_queries = head_norm(cross_raw).astype(bf16)
    paired = jnp.einsum("cn,ptc->pnt", pairs_full, chosen, preferred_element_type=f32)
    paired = paired.reshape(packs, 2, HEADS, HEAD, TEXT_PAD)
    text_raw = paired[:, 0].reshape(packs * HEADS, HEAD, TEXT_PAD)
    text_keys = head_norm(text_raw).astype(bf16)
    text_values = paired[:, 1].reshape(packs * HEADS, HEAD, TEXT_PAD).astype(bf16)
    out_cross, totals_cross = cross_forward(cross_queries, text_keys, text_values)
    crossed = rows_of(out_cross.astype(bf16))
    late_stream = mid_stream + dot(crossed, cross_full, 0, 0)
    normed_ffn = norm_gain(late_stream, gain_rows[3]).astype(bf16)
    ffn_all = gather_cp(normed_ffn).reshape(cp_count * held, D)
    expanded = dot(ffn_all, expand_part, 1, 0)
    hidden = jax.nn.gelu(expanded, approximate=True).astype(bf16)
    reduced_part = dot(hidden, reduce_part, 1, 1)
    block_out = (
        late_stream + scatter_cp(reduced_part.reshape(cp_count, held, D))
    ).astype(bf16)

    out_grad = cotangent.reshape(held, D).astype(f32) * token_valid
    reduce_in = gather_cp(out_grad.astype(bf16)).reshape(cp_count * held, D)

    def add_group(partial):
        return lax.psum_scatter(partial.astype(bf16), GROUP, scatter_dimension=0, tiled=True)

    reduce_grad = add_group(dot(reduce_in, hidden, 0, 0))
    gelu_back = jax.vjp(lambda preact: jax.nn.gelu(preact, approximate=True), expanded)[1]
    expand_in = gelu_back(dot(reduce_in, reduce_part, 1, 0))[0].astype(bf16)
    expand_grad = add_group(dot(ffn_all, expand_in, 0, 0))
    ffn_back = jax.vjp(norm_gain, late_stream, gain_rows[3])[1]
    ffn_grad = scatter_cp(dot(expand_in, expand_part, 1, 1).reshape(cp_count, held, D))
    late_part, gain_ffn = ffn_back(ffn_grad)
    late_grad = out_grad + late_part

    def column_blocks(value):
        return jnp.swapaxes(value.reshape(value.shape[0], cp_count, -1), 0, 1)

    def row_blocks(value):
        return value.reshape((cp_count, value.shape[0] // cp_count) + value.shape[1:])

    cout_in = late_grad.astype(bf16)
    cross_out_grad = add_group(
        jnp.einsum(
            "skt,stn->kn",
            gather_cp(crossed),
            trade_cp(column_blocks(cout_in)),
            preferred_element_type=f32,
        )
    )
    crossed_grad = heads_of(dot(cross_full, cout_in, 1, 1).astype(bf16))
    cq_grad, ck_grad, cv_grad = cross_backward(
        cross_queries, text_keys, text_values, crossed_grad, out_cross, totals_cross
    )
    cq_grad = cq_grad.astype(bf16).astype(f32)
    cross_raw_grad = rows_of(jax.vjp(head_norm, cross_raw)[1](cq_grad)[0].astype(bf16))
    cross_query_grad = add_group(
        jnp.einsum(
            "stk,snt->kn",
            gather_cp(normed_cross),
            trade_cp(row_blocks(cross_raw_grad)),
            preferred_element_type=f32,
        )
    )
    cross_norm_back = jax.vjp(norm_gain, mid_stream, gain_rows[2])[1]
    mid_part, gain_cross = cross_norm_back(dot(cross_raw_grad, query_full, 0, 1))
    mid_grad = late_grad + mid_part
    self_in = mid_grad.astype(bf16)
    attended_grad = by_heads(dot(output_full, self_in, 1, 1).astype(bf16))
    self_out_grad = add_group(
        jnp.einsum(
            "skt,stn->kn",
            gather_cp(attended),
            trade_cp(column_blocks(self_in)),
            preferred_element_type=f32,
        )
    )
    qkv_grad = from_heads(
        self_backward(
            qkv, attended_grad, out_self, totals_self, first_cells, last_cells, valid_cells
        )
    )
    turn = functools.partial(turn_norm, cosine=cosine, sines=sines)
    query_raw_grad = jax.vjp(turn, query_raw)[1](qkv_grad[:, :, 0].astype(f32))[0].astype(bf16)
    key_raw_grad = jax.vjp(turn, key_raw)[1](qkv_grad[:, :, 1].astype(f32))[0].astype(bf16)
    projected_grad = jnp.stack([query_raw_grad, key_raw_grad, qkv_grad[:, :, 2]], axis=0)
    projected_grad = jnp.transpose(
        projected_grad.reshape(3, packs, group_heads, HEAD, cp_count, rows), (0, 2, 3, 4, 1, 5)
    ).reshape(3 * group_heads * HEAD, cp_count * held)
    self_input_grad = add_group(
        dot(normed_all.reshape(cp_count * held, D), projected_grad, 0, 1)
    )
    normed_self_grad = scatter_cp(
        dot(projected_grad, input_part, 0, 1).reshape(cp_count, held, D)
    )
    self_norm_back = jax.vjp(norm_gain, base_stream, gain_rows[1])[1]
    base_part, gain_self = self_norm_back(normed_self_grad)
    shift_grads = jnp.sum(normed_self_grad.reshape(packs, rows, D), axis=1)
    base_grad = mid_grad + base_part
    skip_norm_back = jax.vjp(norm_gain, mixed, gain_rows[0])[1]
    mixed_grad, gain_skip = skip_norm_back(base_grad)
    mixed_in = mixed_grad.astype(bf16)
    joined_grad = dot(mixed_in, skip_full, 1, 1)
    skip_weight_grad = add_group(
        jnp.einsum(
            "stk,stn->kn",
            gather_cp(joined),
            trade_cp(column_blocks(mixed_in)),
            preferred_element_type=f32,
        )
    )

    ck_grad = ck_grad.astype(bf16).astype(f32)
    text_raw_grad = jax.vjp(head_norm, text_raw)[1](ck_grad)[0].astype(bf16)
    paired_grad = jnp.stack(
        [
            text_raw_grad.reshape(packs, D, TEXT_PAD),
            cv_grad.reshape(packs, D, TEXT_PAD).astype(bf16),
        ],
        axis=1,
    ).reshape(packs, 2 * D, TEXT_PAD)
    pairs_grad = add_group(
        jnp.einsum(
            "sptc,snpt->cn",
            gather_cp(chosen),
            trade_cp(row_blocks(jnp.swapaxes(paired_grad, 0, 1))),
            preferred_element_type=f32,
        )
    )
    null_sum = jnp.einsum(
        "p,pnt->nt", own_null.astype(f32), paired_grad.astype(f32), precision=highest
    )
    caption_grad = dot(pairs_full, null_sum.astype(bf16), 1, 0)
    caption_grad = lax.psum_scatter(
        caption_grad.astype(bf16), EVERY, scatter_dimension=0, tiled=True
    )

    small = jnp.concatenate(
        [jnp.stack([gain_skip, gain_self, gain_cross, gain_ffn]), shift_grads], axis=0
    )
    small = lax.all_gather(small, EVERY, axis=0, tiled=False)
    gain_columns = norm_gains.shape[1]
    gains_grad = jnp.sum(
        lax.dynamic_slice_in_dim(small[:, :4], place * gain_columns, gain_columns, 2), axis=0
    )
    shift_all = small[:, 4:].reshape(dp_count, sp_count * cp_count, packs, D)
    shift_all = jnp.swapaxes(shift_all, 1, 2).reshape(all_packs * sp_count * cp_count, D)
    all_pick = (all_segments[:, :, None] == slot_ids).astype(f32)
    silu_blocks = jnp.einsum("pbi,pik->pbk", all_pick, silu_own.astype(f32), precision=highest)
    shift_weight_grad = lax.dot_general(
        silu_blocks.reshape(all_packs * sp_count * cp_count, shard_rows),
        shift_all,
        (((0,), (0,)), ((), ())),
        precision=highest,
        preferred_element_type=f32,
    )

    factor = all_packs * PACK / jnp.sum(lengths).astype(f32)

    def finish(part):
        return join_columns(part).astype(f32) * factor

    token_shape = (packs, rows, D)
    return (
        block_out.reshape(token_shape),
        (joined_grad[:, :D] * factor).astype(bf16).reshape(token_shape),
        (joined_grad[:, D:] * factor).astype(bf16).reshape(token_shape),
        finish(skip_weight_grad),
        shift_weight_grad * factor,
        restore_heads(join_columns(self_input_grad)).astype(f32) * factor,
        finish(self_out_grad),
        finish(cross_query_grad),
        finish(pairs_grad),
        finish(cross_out_grad),
        finish(expand_grad),
        jnp.transpose(join_columns(reduce_grad)).astype(f32) * factor,
        jnp.transpose(caption_grad)[:TEXT].astype(f32) * factor,
        gains_grad * factor,
    )


def solution(mesh):
    token_spec = P("dp", ("sp", "cp"), None)
    by_rows = P(EVERY, None)
    by_columns = P(None, EVERY)
    return jax.shard_map(
        shards,
        mesh=mesh,
        in_specs=(
            token_spec,
            token_spec,
            P("dp", None, None),
            P("dp", "cp", None, None),
            P("dp", None),
            P(),
            token_spec,
            by_rows,
            by_rows,
            by_rows,
            by_rows,
            by_rows,
            by_rows,
            by_rows,
            by_rows,
            by_columns,
            by_columns,
            by_columns,
        ),
        out_specs=(
            token_spec,
            token_spec,
            token_spec,
            by_rows,
            by_rows,
            by_rows,
            by_rows,
            by_rows,
            by_rows,
            by_rows,
            by_rows,
            by_columns,
            by_columns,
            by_columns,
        ),
        check_vma=False,
    )
```

```python
import functools
import math

import jax
import jax.numpy as jnp
from jax import lax
from jax.experimental import pallas as pl
from jax.experimental.pallas import tpu as pltpu
from jax.sharding import PartitionSpec as P

D = 1408
HEADS = 16
HEAD = 88
DT = 1024
TEXT = 333
TEXT_PAD = 384
BIG_SIDE = 32
SMALL_SIDE = 16
PACK = 4096
IMGS = 16
CELL = 256
CELLS = PACK // CELL
SCALING = 1.0 / math.sqrt(HEAD)

epsilon = 1e-06
highest = lax.Precision.HIGHEST
bf16 = jnp.bfloat16
f32 = jnp.float32
GROUP = ("dp", "sp")
EVERY = ("dp", "sp", "cp")
HEAD_ORDER = ("cp", "sp")


def layer_norm(vector, axis=-1):
    centred = vector - jnp.mean(vector, axis=axis, keepdims=True)
    return centred * lax.rsqrt(jnp.mean(centred * centred, axis=axis, keepdims=True) + epsilon)


def head_norm(vector):
    return layer_norm(vector, -2)


def norm_gain(vector, gain):
    return layer_norm(vector) * gain


def dot(left, right, left_dim, right_dim):
    return lax.dot_general(
        left, right, (((left_dim,), (right_dim,)), ((), ())), preferred_element_type=f32
    )


def segment_info(lengths, positions):
    seg_ends = jnp.cumsum(lengths)
    starts = seg_ends - lengths
    present = lengths > 0
    slot_ids = jnp.arange(lengths.shape[0], dtype=jnp.int32)
    segment = jnp.sum(
        ((seg_ends[None, :] <= positions[:, None]) & present[None, :]).astype(jnp.int32), axis=1
    )
    onehot = segment[:, None] == slot_ids[None, :]
    seg_start = jnp.sum(jnp.where(onehot, starts[None, :], 0), axis=1)
    seg_size = jnp.sum(jnp.where(onehot, lengths[None, :], 0), axis=1)
    side_len = jnp.where(seg_size == BIG_SIDE * BIG_SIDE, BIG_SIDE, SMALL_SIDE).astype(jnp.int32)
    offset = positions - seg_start
    images = jnp.sum(present.astype(jnp.int32))
    return (segment, offset // side_len, offset % side_len, (segment < images).astype(f32))


def cell_ranges(lengths):
    positions = jnp.arange(CELLS, dtype=jnp.int32) * CELL
    seg_ends = jnp.cumsum(lengths)
    present = lengths > 0
    segment = jnp.sum(
        ((seg_ends[None, :] <= positions[:, None]) & present[None, :]).astype(jnp.int32), axis=1
    )
    same = segment[:, None] == segment[None, :]
    cells = jnp.arange(CELLS, dtype=jnp.int32)
    first = jnp.min(jnp.where(same, cells[None, :], CELLS), axis=1)
    last = jnp.max(jnp.where(same, cells[None, :] + 1, 0), axis=1)
    return (first, last, jnp.sum(lengths) // CELL)


def rope_tables(grid_row, grid_col):
    quarter = HEAD // 4
    frequency = jnp.exp(jnp.arange(quarter, dtype=f32) * (-math.log(10000.0) / quarter))
    angles = jnp.concatenate(
        [
            frequency[:, None] * grid_row.astype(f32)[None, :],
            frequency[:, None] * grid_col.astype(f32)[None, :],
        ],
        axis=0,
    )
    return (jnp.cos(angles), jnp.sin(angles))


def rotate(vector, cosine, sines):
    quarter = HEAD // 4
    one, two, three, four = (
        vector[..., k * quarter : (k + 1) * quarter, :] for k in range(4)
    )
    cos_row, cos_col = cosine[..., :quarter, :], cosine[..., quarter:, :]
    sin_row, sin_col = sines[..., :quarter, :], sines[..., quarter:, :]
    return jnp.concatenate(
        [
            one * cos_row - two * sin_row,
            one * sin_row + two * cos_row,
            three * cos_col - four * sin_col,
            three * sin_col + four * cos_col,
        ],
        axis=-2,
    )


def turn_norm(vector, cosine, sines):
    return rotate(head_norm(vector), cosine, sines)


def trade_bit(value, axis, bit):
    count = lax.axis_size(axis)
    return lax.ppermute(value, axis, [(k, k ^ bit) for k in range(count)])


def bits_of(axis):
    count = lax.axis_size(axis)
    return [1 << k for k in range(count.bit_length() - 1)]


def has_bit(axis, bit):
    return (lax.axis_index(axis) // bit) % 2 == 1


def pieces_cp(value):
    pieces = [value]
    found = {0: value}
    for bit in reversed(bits_of("cp")):
        for key in list(found):
            found[key | bit] = trade_bit(found[key], "cp", bit)
    pieces = [found[key] for key in range(lax.axis_size("cp"))]
    return pieces


def reorder_cp(pieces):
    for bit in bits_of("cp"):
        high = has_bit("cp", bit)
        pieces = [
            jnp.where(high, pieces[key ^ bit], pieces[key]) for key in range(len(pieces))
        ]
    return pieces


def gather_cp(value):
    return jnp.stack(reorder_cp(pieces_cp(value)))


def scatter_cp(pieces):
    pieces = [piece.astype(bf16) for piece in pieces]
    for bit in bits_of("cp"):
        pieces = [
            (
                pieces[key].astype(f32) + trade_bit(pieces[key + 1], "cp", bit).astype(f32)
            ).astype(f32 if len(pieces) == 2 else bf16)
            for key in range(0, len(pieces), 2)
        ]
    return pieces[0]


def after(value, *others):
    for other in others:
        value = value + (other[(0,) * other.ndim].astype(f32) * 0.0).astype(value.dtype)
    return value


def exchange_cp(pieces):
    count = lax.axis_size("cp")
    return [pieces[0]] + [
        lax.ppermute(pieces[key], "cp", [(k, k ^ key) for k in range(count)])
        for key in range(1, count)
    ]


def trade_cp(blocks):
    return lax.all_to_all(blocks, "cp", split_axis=0, concat_axis=0, tiled=True)


def send_cp(blocks):
    return reorder_cp(exchange_cp(reorder_cp(blocks)))


def group_steps():
    steps = [("dp", bit, bit * lax.axis_size("sp")) for bit in bits_of("dp")]
    return steps + [("sp", bit, bit) for bit in bits_of("sp")]


def group_differences():
    differences = [0]
    for _, _, weight in reversed(group_steps()):
        differences = differences + [key ^ weight for key in differences]
    return differences


def scatter_group_halves(keep, send, waits):
    for step, (axis, bit, _) in enumerate(group_steps()):
        came = trade_bit(send, axis, bit).astype(f32)
        total = after(keep.astype(f32) + came, waits[step]).astype(bf16)
        half = total.shape[0] // 2
        keep, send = total[:half], total[half:]
        if step == len(group_steps()) - 1:
            return total
    return None


def gather_every(value):
    for axis in reversed(EVERY):
        for bit in bits_of(axis):
            other = trade_bit(value, axis, bit)
            value = jnp.where(
                has_bit(axis, bit), jnp.stack([other, value]), jnp.stack([value, other])
            )
    depth = sum(len(bits_of(axis)) for axis in EVERY)
    return value.reshape((-1,) + value.shape[depth:])


def scatter_every(value):
    for axis in EVERY:
        for bit in reversed(bits_of(axis)):
            halves = value.reshape((2, -1) + value.shape[1:])
            high = has_bit(axis, bit)
            keep = jnp.where(high, halves[1], halves[0])
            send = jnp.where(high, halves[0], halves[1])
            value = keep + trade_bit(send, axis, bit)
    return value[0]


def flip(block):
    if block.shape[0] % 128 == 0 and block.shape[1] % 128 == 0:
        return jnp.transpose(block)
    return jnp.transpose(block.astype(f32)).astype(bf16)


def kernel_dot(left, right, left_dim=1, right_dim=0):
    return lax.dot_general(
        left, right, (((left_dim,), (right_dim,)), ((), ())), preferred_element_type=f32
    )


def over_cells(first, last, step, carry):
    count = last - first
    fours = count // 4

    def four(turn, current):
        for k in range(4):
            current = step(first + turn * 4 + k, current)
        return current

    carry = lax.fori_loop(0, fours, four, carry)
    return lax.fori_loop(first + fours * 4, last, step, carry)


def self_forward_kernel(first_ref, last_ref, turned_ref, qkv_ref, *refs):
    out_ref, total_ref, keys = refs[-3:]
    pair = pl.program_id(0)
    per = qkv_ref.shape[-1] // CELL

    def where(cell):
        lanes = ((cell % per) ^ turned_ref[0]) * CELL
        return cell // per, pl.ds(pl.multiple_of(lanes, CELL), CELL)

    def turn_keys(cell, carry):
        chunk, lanes = where(cell)
        keys[cell] = flip(qkv_ref[chunk, 0, 1, :, lanes])
        return carry

    lax.fori_loop(0, CELLS, turn_keys, 0)

    def one_cell(cell, carry):
        chunk, lanes = where(cell)
        query = qkv_ref[chunk, 0, 0, :, lanes]

        def step(other, current):
            summed, totals = current
            key_chunk, key_lanes = where(other)
            weights = jnp.exp(kernel_dot(keys[other], query) * SCALING)
            totals = totals + jnp.sum(weights, axis=0, keepdims=True)
            summed = summed + kernel_dot(
                qkv_ref[key_chunk, 0, 2, :, key_lanes], weights.astype(bf16)
            )
            return (summed, totals)

        summed, totals = over_cells(
            first_ref[pair, cell],
            last_ref[pair, cell],
            step,
            (jnp.zeros((HEAD, CELL), f32), jnp.zeros((1, CELL), f32)),
        )
        out_ref[chunk, 0, :, lanes] = summed / totals
        total_ref[chunk, 0, :, lanes] = totals
        return carry

    lax.fori_loop(0, CELLS, one_cell, 0)


def self_backward_kernel(
    first_ref,
    last_ref,
    valid_ref,
    turned_ref,
    qkv_ref,
    grad_ref,
    out_ref,
    total_ref,
    *refs,
):
    result_ref, keys, values, key_sums, value_sums = refs[-5:]
    pair = pl.program_id(0)
    per = qkv_ref.shape[-1] // CELL

    def where(cell):
        lanes = ((cell % per) ^ turned_ref[0]) * CELL
        return cell // per, pl.ds(pl.multiple_of(lanes, CELL), CELL)

    def prepare(cell, carry):
        chunk, lanes = where(cell)
        keys[cell] = flip(qkv_ref[chunk, 0, 1, :, lanes])
        values[cell] = flip(qkv_ref[chunk, 0, 2, :, lanes])
        key_sums[cell] = jnp.zeros((HEAD, CELL), f32)
        value_sums[cell] = jnp.zeros((HEAD, CELL), f32)
        result_ref[chunk, 0, 0, :, lanes] = jnp.zeros((HEAD, CELL), bf16)
        return carry

    lax.fori_loop(0, CELLS, prepare, 0)

    def one_cell(cell, carry):
        chunk, lanes = where(cell)
        query = qkv_ref[chunk, 0, 0, :, lanes]
        grad = grad_ref[chunk, 0, :, lanes].astype(f32)
        inverse = 1.0 / total_ref[chunk, 0, :, lanes]
        scaled = (grad * inverse).astype(bf16)
        total_grad = (
            -jnp.sum(grad * out_ref[chunk, 0, :, lanes], axis=0, keepdims=True) * inverse
        )

        def step(other, query_sum):
            key_chunk, key_lanes = where(other)
            weights = jnp.exp(kernel_dot(keys[other], query) * SCALING)
            weight_grad = kernel_dot(values[other], scaled)
            score_grad = (weights * (weight_grad + total_grad)).astype(bf16)
            value_sums[other] += kernel_dot(scaled, weights.astype(bf16), 1, 1)
            key_sums[other] += kernel_dot(query, score_grad, 1, 1)
            return query_sum + kernel_dot(qkv_ref[key_chunk, 0, 1, :, key_lanes], score_grad)

        query_sum = over_cells(
            first_ref[pair, cell], last_ref[pair, cell], step, jnp.zeros((HEAD, CELL), f32)
        )
        result_ref[chunk, 0, 0, :, lanes] = (query_sum * SCALING).astype(bf16)
        return carry

    lax.fori_loop(0, valid_ref[pair], one_cell, 0)

    def finish(cell, carry):
        chunk, lanes = where(cell)
        result_ref[chunk, 0, 1, :, lanes] = (key_sums[cell] * SCALING).astype(bf16)
        result_ref[chunk, 0, 2, :, lanes] = value_sums[cell].astype(bf16)
        return carry

    lax.fori_loop(0, CELLS, finish, 0)


def pair_spec(shape):
    block = (shape[0], 1) + shape[2:]
    rest = (0,) * (len(shape) - 2)
    return pl.BlockSpec(block, lambda pair, *_: (0, pair) + rest)


VMEM_WHOLE = pl.BlockSpec(memory_space=pltpu.VMEM)
SMEM_WHOLE = pl.BlockSpec(memory_space=pltpu.SMEM)
ANY_WHOLE = pl.BlockSpec(memory_space=pl.ANY)
VMEM_LIMIT = 48 * 1024 * 1024


def self_forward(qkv, first, last, turned, stamps):
    chunks, pairs, _, _, columns = qkv.shape
    out_shape = (chunks, pairs, HEAD, columns)
    total_shape = (chunks, pairs, 1, columns)
    return pl.pallas_call(
        self_forward_kernel,
        out_shape=(
            jax.ShapeDtypeStruct(out_shape, f32),
            jax.ShapeDtypeStruct(total_shape, f32),
        ),
        grid_spec=pltpu.PrefetchScalarGridSpec(
            num_scalar_prefetch=3,
            grid=(pairs,),
            in_specs=[pair_spec(qkv.shape)] + [pl.BlockSpec(memory_space=pl.ANY)] * len(stamps),
            out_specs=[pair_spec(out_shape), pair_spec(total_shape)],
            scratch_shapes=[pltpu.VMEM((CELLS, CELL, HEAD), bf16)],
        ),
        compiler_params=pltpu.CompilerParams(vmem_limit_bytes=VMEM_LIMIT),
        cost_estimate=pl.CostEstimate(flops=10**10, bytes_accessed=8 << 20, transcendentals=0),
        name="self_forward",
    )(first, last, turned, qkv, *stamps)


def self_backward(qkv, grad, out, totals, first, last, valid, turned, stamps):
    pairs = qkv.shape[1]
    return pl.pallas_call(
        self_backward_kernel,
        out_shape=jax.ShapeDtypeStruct(qkv.shape, bf16),
        grid_spec=pltpu.PrefetchScalarGridSpec(
            num_scalar_prefetch=4,
            grid=(pairs,),
            in_specs=[
                pair_spec(qkv.shape),
                pair_spec(grad.shape),
                pair_spec(out.shape),
                pair_spec(totals.shape),
            ]
            + [pl.BlockSpec(memory_space=pl.ANY)] * len(stamps),
            out_specs=pair_spec(qkv.shape),
            scratch_shapes=[
                pltpu.VMEM((CELLS, CELL, HEAD), bf16),
                pltpu.VMEM((CELLS, CELL, HEAD), bf16),
                pltpu.VMEM((CELLS, HEAD, CELL), f32),
                pltpu.VMEM((CELLS, HEAD, CELL), f32),
            ],
        ),
        compiler_params=pltpu.CompilerParams(vmem_limit_bytes=VMEM_LIMIT),
        cost_estimate=pl.CostEstimate(flops=18 * 10**9, bytes_accessed=16 << 20, transcendentals=0),
        name="self_backward",
    )(first, last, valid, turned, qkv, grad, out, totals, *stamps)


def text_weights(key_block, query):
    scores = kernel_dot(flip(key_block), query) * SCALING
    present = lax.broadcasted_iota(jnp.int32, scores.shape, 0) < TEXT
    return jnp.where(present, jnp.exp(scores), 0.0)


def cross_forward_kernel(query_ref, key_ref, value_ref, out_ref, total_ref):
    for head in range(query_ref.shape[0]):
        weights = text_weights(key_ref[head], query_ref[head])
        totals = jnp.sum(weights, axis=0, keepdims=True)
        out_ref[head] = kernel_dot(value_ref[head], weights.astype(bf16)) / totals
        total_ref[head] = totals


def cross_backward_kernel(
    query_ref,
    key_ref,
    value_ref,
    grad_ref,
    out_ref,
    total_ref,
    query_grad_ref,
    key_grad_ref,
    value_grad_ref,
):
    for head in range(query_ref.shape[0]):
        query, keys = query_ref[head], key_ref[head]
        grad = grad_ref[head].astype(f32)
        inverse = 1.0 / total_ref[head]
        scaled = (grad * inverse).astype(bf16)
        total_grad = -jnp.sum(grad * out_ref[head], axis=0, keepdims=True) * inverse
        weights = text_weights(keys, query)
        weight_grad = kernel_dot(flip(value_ref[head]), scaled)
        score_grad = (weights * (weight_grad + total_grad)).astype(bf16)
        query_grad_ref[head] = kernel_dot(keys, score_grad) * SCALING
        key_grad_ref[head] = kernel_dot(query, score_grad, 1, 1) * SCALING
        value_grad_ref[head] = kernel_dot(scaled, weights.astype(bf16), 1, 1)


HEADS_STEP = 4


def head_spec(shape):
    return pl.BlockSpec((HEADS_STEP,) + shape[1:], lambda step: (step, 0, 0))


def cross_forward(queries, keys, values):
    count, _, rows = queries.shape
    out_shape = (count, HEAD, rows)
    total_shape = (count, 1, rows)
    return pl.pallas_call(
        cross_forward_kernel,
        out_shape=(
            jax.ShapeDtypeStruct(out_shape, f32),
            jax.ShapeDtypeStruct(total_shape, f32),
        ),
        grid=(count // HEADS_STEP,),
        in_specs=[head_spec(queries.shape), head_spec(keys.shape), head_spec(values.shape)],
        out_specs=[head_spec(out_shape), head_spec(total_shape)],
        compiler_params=pltpu.CompilerParams(vmem_limit_bytes=VMEM_LIMIT),
        name="cross_forward",
    )(queries, keys, values)


def cross_backward(queries, keys, values, grad, out, totals):
    inputs = (queries, keys, values, grad, out, totals)
    return pl.pallas_call(
        cross_backward_kernel,
        out_shape=(
            jax.ShapeDtypeStruct(queries.shape, f32),
            jax.ShapeDtypeStruct(keys.shape, f32),
            jax.ShapeDtypeStruct(values.shape, f32),
        ),
        grid=(queries.shape[0] // HEADS_STEP,),
        in_specs=[head_spec(member.shape) for member in inputs],
        out_specs=[head_spec(queries.shape), head_spec(keys.shape), head_spec(values.shape)],
        compiler_params=pltpu.CompilerParams(vmem_limit_bytes=VMEM_LIMIT),
        name="cross_backward",
    )(*inputs)


def unpack_kernel(width, text, bucket_ref, stamp_ref, *outs):
    padded = width + -width % 128
    for part in range(3):
        block = bucket_ref[:, part * padded : (part + 1) * padded]
        outs[part][...] = flip(block)[:width]
    rows = D * text // DT
    for group in range(DT // text):
        outs[3][group * text : (group + 1) * text, :] = bucket_ref[
            group * rows : group * rows + text, 3 * padded : 3 * padded + 2 * width
        ]


def unpack_mid(bucket, width, text, stamp):
    part = jax.ShapeDtypeStruct((width, D), bf16)
    return pl.pallas_call(
        functools.partial(unpack_kernel, width, text),
        out_shape=(part, part, part, jax.ShapeDtypeStruct((DT, 2 * width), bf16)),
        in_specs=[VMEM_WHOLE, ANY_WHOLE],
        out_specs=[VMEM_WHOLE] * 4,
        compiler_params=pltpu.CompilerParams(vmem_limit_bytes=VMEM_LIMIT),
        cost_estimate=pl.CostEstimate(flops=1, bytes_accessed=12 << 20, transcendentals=0),
        name="unpack_mid",
    )(bucket, stamp)


def turn_over_kernel(value_ref, out_ref):
    out_ref[...] = flip(value_ref[...])


def turn_over(value):
    return pl.pallas_call(
        turn_over_kernel,
        out_shape=jax.ShapeDtypeStruct(value.shape[::-1], value.dtype),
        in_specs=[pl.BlockSpec(memory_space=pltpu.VMEM)],
        out_specs=pl.BlockSpec(memory_space=pltpu.VMEM),
        compiler_params=pltpu.CompilerParams(vmem_limit_bytes=VMEM_LIMIT),
        cost_estimate=pl.CostEstimate(flops=1, bytes_accessed=2 << 20, transcendentals=0),
        name="turn_over",
    )(value)


def expand_grads_kernel(*refs):
    left = jnp.concatenate([ref[...] for ref in refs[:-2]], axis=1)
    refs[-1][...] = kernel_dot(left, refs[-2][...]).astype(bf16)


def expand_grads(pieces, right):
    steps = 4
    rows, width = D // steps, right.shape[1]
    return pl.pallas_call(
        expand_grads_kernel,
        out_shape=jax.ShapeDtypeStruct((D, width), bf16),
        grid=(steps,),
        in_specs=[pl.BlockSpec((rows, pieces[0].shape[1]), lambda g: (g, 0))] * len(pieces)
        + [pl.BlockSpec(right.shape, lambda g: (0, 0))],
        out_specs=pl.BlockSpec((rows, width), lambda g: (g, 0)),
        compiler_params=pltpu.CompilerParams(vmem_limit_bytes=VMEM_LIMIT),
        cost_estimate=pl.CostEstimate(
            flops=2 * D * right.shape[0] * width, bytes_accessed=12 << 20, transcendentals=0
        ),
        name="expand_grads",
    )(*pieces, right)


def reduce_grads_kernel(group_ref, *refs):
    pieces, (right_ref, keep_ref, send_ref) = refs[:-3], refs[-3:]
    step, steps = pl.program_id(0), pl.num_programs(0)
    left = jnp.concatenate([ref[...] for ref in pieces], axis=1)
    product = kernel_dot(left, right_ref[...]).astype(bf16)

    @pl.when(step < steps // 2)
    def _():
        keep_ref[...] = product

    @pl.when(step >= steps // 2)
    def _():
        send_ref[...] = product


def reduce_grads(pieces, right, groups):
    steps, width = groups.shape[0], right.shape[1]
    rows, half = D // steps, steps // 2
    shape = jax.ShapeDtypeStruct((D // 2, width), bf16)
    return pl.pallas_call(
        reduce_grads_kernel,
        out_shape=(shape, shape),
        grid_spec=pltpu.PrefetchScalarGridSpec(
            num_scalar_prefetch=1,
            grid=(steps,),
            in_specs=[
                pl.BlockSpec((rows, pieces[0].shape[1]), lambda g, group: (group[g], 0))
            ]
            * len(pieces)
            + [pl.BlockSpec(right.shape, lambda g, group: (0, 0))],
            out_specs=[
                pl.BlockSpec((rows, width), lambda g, group: (jnp.minimum(g, half - 1), 0)),
                pl.BlockSpec((rows, width), lambda g, group: (jnp.maximum(g - half, 0), 0)),
            ],
        ),
        compiler_params=pltpu.CompilerParams(vmem_limit_bytes=VMEM_LIMIT),
        cost_estimate=pl.CostEstimate(
            flops=2 * D * right.shape[0] * width, bytes_accessed=12 << 20, transcendentals=0
        ),
        name="reduce_grads",
    )(groups, *pieces, right)


def mid_grads_kernel(count, width, *refs):
    lefts, rights, texts, pairs = (refs[k * count : (k + 1) * count] for k in range(4))
    out_ref = refs[4 * count + 1]
    rows = out_ref.shape[0]
    padded = width + -width % 128
    for part in range(3):
        product = sum(
            kernel_dot(left[part], right[part], 1, 1) for left, right in zip(lefts, rights)
        )
        product = jnp.concatenate([product, jnp.zeros((rows, padded - width), f32)], axis=1)
        out_ref[:, part * padded : (part + 1) * padded] = product.astype(bf16)
    text = texts[0].shape[0]
    product = sum(kernel_dot(left[...], right[...], 1, 1) for left, right in zip(texts, pairs))
    rest = out_ref.shape[1] - 3 * padded
    product = jnp.concatenate([product, jnp.zeros((text, rest - 2 * width), f32)], axis=1)
    out_ref[:text, 3 * padded :] = product.astype(bf16)
    out_ref[text:, 3 * padded :] = jnp.zeros((rows - text, rest), bf16)


def mid_grads_bucket(lefts, rights, texts, pairs, stamp, groups):
    count, width = len(lefts), rights[0].shape[1]
    rows, text = D // groups, DT // groups
    columns = 3 * (width + -width % 128) + 2 * width + -2 * width % 128
    return pl.pallas_call(
        functools.partial(mid_grads_kernel, count, width),
        out_shape=jax.ShapeDtypeStruct((D, columns), bf16),
        grid=(groups,),
        in_specs=[pl.BlockSpec((3, rows, lefts[0].shape[2]), lambda g: (0, g, 0))] * count
        + [pl.BlockSpec(rights[0].shape, lambda g: (0, 0, 0))] * count
        + [pl.BlockSpec((text, texts[0].shape[1]), lambda g: (g, 0))] * count
        + [pl.BlockSpec(pairs[0].shape, lambda g: (0, 0))] * count
        + [ANY_WHOLE],
        out_specs=pl.BlockSpec((rows, columns), lambda g: (g, 0)),
        compiler_params=pltpu.CompilerParams(vmem_limit_bytes=VMEM_LIMIT),
        cost_estimate=pl.CostEstimate(
            flops=10 * D * D * width, bytes_accessed=24 << 20, transcendentals=0
        ),
        name="mid_grads",
    )(*lefts, *rights, *texts, *pairs, stamp)


def skip_grads_kernel(count, width, *refs):
    rights, lefts = refs[:count], refs[count : 2 * count]
    input_ref, out_ref = refs[2 * count :]
    product = sum(kernel_dot(left[...], right[...]) for left, right in zip(lefts, rights))
    padded = width + -width % 128
    quarter = width // (2 * count)
    product = jnp.transpose(product)
    group_rows = count * quarter
    fill = jnp.zeros((group_rows, padded - width), f32)
    for group in range(product.shape[0] // width):
        for part in range(2):
            starts = [
                group * width + (2 * k + part) * quarter for k in range(count)
            ]
            block = jnp.concatenate(
                [product[start : start + quarter] for start in starts], axis=0
            )
            out_ref[
                group * group_rows : (group + 1) * group_rows,
                part * padded : (part + 1) * padded,
            ] = jnp.concatenate([block, fill], axis=1).astype(bf16)
    out_ref[:, 2 * padded : 2 * padded + input_ref.shape[1]] = input_ref[...]
    rest = out_ref.shape[1] - 2 * padded - input_ref.shape[1]
    out_ref[:, 2 * padded + input_ref.shape[1] :] = jnp.zeros((out_ref.shape[0], rest), bf16)


def skip_grads_bucket(lefts, rights, inputs):
    count, width = len(lefts), lefts[0].shape[0]
    columns = 2 * (width + -width % 128) + inputs.shape[1] + -inputs.shape[1] % 128
    return pl.pallas_call(
        functools.partial(skip_grads_kernel, count, width),
        out_shape=jax.ShapeDtypeStruct((D, columns), bf16),
        grid=(2,),
        in_specs=[pl.BlockSpec((rights[0].shape[0], D), lambda g: (0, g))] * count
        + [pl.BlockSpec(lefts[0].shape, lambda g: (0, 0))] * count
        + [pl.BlockSpec((D // 2, inputs.shape[1]), lambda g: (g, 0))],
        out_specs=pl.BlockSpec((D // 2, columns), lambda g: (g, 0)),
        compiler_params=pltpu.CompilerParams(vmem_limit_bytes=VMEM_LIMIT),
        cost_estimate=pl.CostEstimate(
            flops=4 * D * width * count * 256, bytes_accessed=16 << 20, transcendentals=0
        ),
        name="skip_grads",
    )(*rights, *lefts, inputs)


def finish_kernel(factor_ref, blocks_ref, skip_ref, input_ref):
    factor = factor_ref[0, 0]
    count, shard, _ = blocks_ref.shape
    width = skip_ref.shape[1] // count
    padded = width + -width % 128
    blocks = [blocks_ref[k].astype(f32) * factor for k in range(count)]
    for part in range(2):
        skip_ref[part * shard : (part + 1) * shard, :] = jnp.concatenate(
            [block[:, part * padded : part * padded + width] for block in blocks], axis=1
        )
    input_ref[...] = jnp.concatenate(
        [
            block[:, 2 * padded + part * width : 2 * padded + (part + 1) * width]
            for part in range(3)
            for block in blocks
        ],
        axis=1,
    )


def finish_head(blocks, factor):
    count, shard, _ = blocks.shape
    return pl.pallas_call(
        finish_kernel,
        out_shape=(
            jax.ShapeDtypeStruct((2 * shard, D), f32),
            jax.ShapeDtypeStruct((shard, 3 * D), f32),
        ),
        in_specs=[pl.BlockSpec(memory_space=pltpu.SMEM), pl.BlockSpec(memory_space=pltpu.VMEM)],
        out_specs=[pl.BlockSpec(memory_space=pltpu.VMEM)] * 2,
        compiler_params=pltpu.CompilerParams(vmem_limit_bytes=VMEM_LIMIT),
        cost_estimate=pl.CostEstimate(flops=1, bytes_accessed=2 << 20, transcendentals=0),
        name="finish_head",
    )(factor.reshape(1, 1), blocks)


def norm_rows(value):
    centred = value - jnp.mean(value, axis=0, keepdims=True)
    scale = lax.rsqrt(jnp.mean(centred * centred, axis=0, keepdims=True) + epsilon)
    return centred * scale, scale


def norm_rows_back(normed, scale, grad):
    return scale * (
        grad
        - jnp.mean(grad, axis=0, keepdims=True)
        - normed * jnp.mean(grad * normed, axis=0, keepdims=True)
    )


def fetch(sources, targets, sems, base):
    copies = [
        pltpu.make_async_copy(source, target, sems.at[base + k])
        for k, (source, target) in enumerate(zip(sources, targets))
    ]
    for copy in copies:
        copy.start()
    return copies


def mix_kernel(count, padded, *refs):
    index_ref, bucket_ref = refs[:2]
    pieces = refs[2 : 2 + count]
    out_ref, weight = refs[2 + count :]
    width = weight.shape[1]
    half = width // 2
    for group in range(weight.shape[0] // width):
        for part in range(2):
            start = group * width + part * half
            weight[start : start + half, :] = bucket_ref[
                group * half : (group + 1) * half, part * padded : part * padded + width
            ]
    for piece in range(count):
        out_ref[piece ^ index_ref[0]] = kernel_dot(pieces[piece][...], weight[...]).astype(bf16)


def mix(index, bucket, pieces, width):
    count, padded = len(pieces), width + -width % 128
    rows = pieces[0].shape[0]
    return pl.pallas_call(
        functools.partial(mix_kernel, count, padded),
        out_shape=jax.ShapeDtypeStruct((count, rows, width), bf16),
        grid=(1,),
        in_specs=[SMEM_WHOLE, pl.BlockSpec((D, 2 * padded), lambda g: (0, 0))]
        + [pl.BlockSpec(pieces[0].shape, lambda g: (0, 0))] * count,
        out_specs=pl.BlockSpec((count, rows, width), lambda g: (0, 0, 0)),
        scratch_shapes=[pltpu.VMEM((2 * D, width), bf16)],
        compiler_params=pltpu.CompilerParams(vmem_limit_bytes=VMEM_LIMIT),
        cost_estimate=pl.CostEstimate(
            flops=4 * D * width * count * rows, bytes_accessed=8 << 20, transcendentals=0
        ),
        name="mix",
    )(index, bucket, *pieces)


def mixed_rows(blocks_ref, stage):
    width = blocks_ref.shape[2]
    for block in range(blocks_ref.shape[0]):
        turned = jnp.transpose(blocks_ref[block].astype(f32))
        stage[block * width : (block + 1) * width, :] = turned
    return stage[...]


def start_kernel(blocks_ref, gain_ref, shift_ref, base_ref, normed_ref, stage):
    base = norm_rows(mixed_rows(blocks_ref, stage))[0] * gain_ref[:, 0:1]
    base_ref[...] = base
    normed = norm_rows(base)[0] * gain_ref[:, 1:2] + shift_ref[...]
    normed_ref[...] = normed.astype(bf16)


def start_forward(blocks, gains, shift):
    tokens = blocks.shape[1]
    return pl.pallas_call(
        start_kernel,
        out_shape=(
            jax.ShapeDtypeStruct((D, tokens), f32),
            jax.ShapeDtypeStruct((D, tokens), bf16),
        ),
        in_specs=[VMEM_WHOLE] * 3,
        out_specs=[VMEM_WHOLE] * 2,
        scratch_shapes=[pltpu.VMEM((D, tokens), f32)],
        compiler_params=pltpu.CompilerParams(vmem_limit_bytes=VMEM_LIMIT),
        cost_estimate=pl.CostEstimate(flops=1, bytes_accessed=8 << 20, transcendentals=0),
        name="start_forward",
    )(blocks, gains, shift)


def start_back_kernel(
    blocks_ref, gain_ref, base_ref, mid_grad_ref, grad_ref, out_ref, sums_ref, stage
):
    normed, scale = norm_rows(base_ref[...])
    grad = grad_ref[...]
    sums_ref[:, 1:2] = jnp.sum(grad * normed, axis=1, keepdims=True)
    sums_ref[:, 2:3] = jnp.sum(grad, axis=1, keepdims=True)
    base_grad = mid_grad_ref[...] + norm_rows_back(normed, scale, grad * gain_ref[:, 1:2])
    normed, scale = norm_rows(mixed_rows(blocks_ref, stage))
    sums_ref[:, 0:1] = jnp.sum(base_grad * normed, axis=1, keepdims=True)
    mixed_grad = norm_rows_back(normed, scale, base_grad * gain_ref[:, 0:1]).astype(bf16)
    width = out_ref.shape[1]
    for block in range(out_ref.shape[0]):
        out_ref[block] = mixed_grad[block * width : (block + 1) * width]


def start_backward(blocks, gains, base, mid_grad, grad):
    count, tokens, width = blocks.shape
    return pl.pallas_call(
        start_back_kernel,
        out_shape=(
            jax.ShapeDtypeStruct((count, width, tokens), bf16),
            jax.ShapeDtypeStruct((D, 3), f32),
        ),
        in_specs=[VMEM_WHOLE] * 5,
        out_specs=[VMEM_WHOLE] * 2,
        scratch_shapes=[pltpu.VMEM((D, tokens), f32)],
        compiler_params=pltpu.CompilerParams(vmem_limit_bytes=VMEM_LIMIT),
        cost_estimate=pl.CostEstimate(flops=1, bytes_accessed=10 << 20, transcendentals=0),
        name="start_backward",
    )(blocks, gains, base, mid_grad, grad)


def middle_forward_kernel(count, *refs):
    index_ref, attended_ref, base_ref, gain_ref, key_ref, value_ref = refs[:6]
    sources = refs[6 : 6 + 3 * count]
    (
        mid_ref,
        late_ref,
        lefts_ref,
        raw_ref,
        query_ref,
        out_ref,
        total_ref,
        ffn_ref,
    ) = refs[6 + 3 * count : 14 + 3 * count]
    weights, sems = refs[14 + 3 * count :]
    copies = fetch(sources, [weights.at[k] for k in range(3 * count)], sems, 0)
    index = index_ref[0]
    width = D // count
    heads = HEADS // count

    def rows_of_piece(piece):
        return pl.ds(pl.multiple_of((piece ^ index) * width, 32), width)

    attended = attended_ref[...]
    for piece in range(count):
        copies[piece].wait()
        rows = rows_of_piece(piece)
        mid_ref[rows, :] = base_ref[rows, :] + kernel_dot(weights[piece], attended)
    normed = (norm_rows(mid_ref[...])[0] * gain_ref[:, 2:3]).astype(bf16)
    lefts_ref[0] = normed
    lefts_ref[2] = attended
    for piece in range(count):
        copies[count + piece].wait()
        product = kernel_dot(weights[count + piece], normed)
        for head in range(heads):
            raw_ref[(piece ^ index) * heads + head] = product[head * HEAD : (head + 1) * HEAD]
    for head in range(HEADS):
        query = norm_rows(raw_ref[head])[0].astype(bf16)
        query_ref[head] = query
        attention = text_weights(key_ref[head], query)
        totals = jnp.sum(attention, axis=0, keepdims=True)
        out = kernel_dot(value_ref[head], attention.astype(bf16)) / totals
        out_ref[head * HEAD : (head + 1) * HEAD, :] = out
        total_ref[head] = totals
    crossed = out_ref[...].astype(bf16)
    lefts_ref[1] = crossed
    for piece in range(count):
        copies[2 * count + piece].wait()
        rows = rows_of_piece(piece)
        late_ref[rows, :] = mid_ref[rows, :] + kernel_dot(weights[2 * count + piece], crossed)
    ffn_ref[...] = (norm_rows(late_ref[...])[0] * gain_ref[:, 3:4]).astype(bf16)


def middle_forward(index, attended, base, gains, keys, values, weights):
    count = len(weights) // 3
    tokens = attended.shape[1]
    stream = jax.ShapeDtypeStruct((D, tokens), f32)
    by_head = (HEADS, HEAD, tokens)
    return pl.pallas_call(
        functools.partial(middle_forward_kernel, count),
        out_shape=(
            stream,
            stream,
            jax.ShapeDtypeStruct((3, D, tokens), bf16),
            jax.ShapeDtypeStruct(by_head, f32),
            jax.ShapeDtypeStruct(by_head, bf16),
            stream,
            jax.ShapeDtypeStruct((HEADS, 1, tokens), f32),
            jax.ShapeDtypeStruct((D, tokens), bf16),
        ),
        in_specs=[SMEM_WHOLE] + [VMEM_WHOLE] * 5 + [ANY_WHOLE] * (3 * count),
        out_specs=[VMEM_WHOLE] * 8,
        scratch_shapes=[
            pltpu.VMEM((3 * count, D // count, D), bf16),
            pltpu.SemaphoreType.DMA((3 * count,)),
        ],
        compiler_params=pltpu.CompilerParams(vmem_limit_bytes=VMEM_LIMIT),
        cost_estimate=pl.CostEstimate(
            flops=10 * D * D * tokens, bytes_accessed=24 << 20, transcendentals=0
        ),
        name="middle_forward",
    )(index, attended, base, gains, keys, values, *weights)


def middle_backward_kernel(count, stamps, *refs):
    (
        index_ref,
        ffn_grad_ref,
        out_grad_ref,
        late_ref,
        mid_ref,
        gain_ref,
        query_ref,
        key_ref,
        value_ref,
        out_ref,
        total_ref,
        raw_ref,
    ) = refs[:12]
    sources = refs[12 : 12 + 3 * count]
    (
        late_grad_ref,
        raw_grad_ref,
        mid_grad_ref,
        mid_round_ref,
        attended_grad_ref,
        key_grad_ref,
        value_grad_ref,
        gain_grad_ref,
    ) = refs[12 + stamps + 3 * count : 20 + stamps + 3 * count]
    weights, stage, sems = refs[20 + stamps + 3 * count :]
    order = [2, 1, 0]
    copies = []
    for place in order:
        copies += fetch(
            sources[place * count : (place + 1) * count],
            [weights.at[place * count + k] for k in range(count)],
            sems,
            place * count,
        )
    index = index_ref[0]
    width = D // count

    def through(place, turn, source_ref):
        total = 0.0
        for piece in range(count):
            copies[turn * count + piece].wait()
            rows = pl.ds(pl.multiple_of((piece ^ index) * width, 32), width)
            total = total + kernel_dot(flip(source_ref[rows, :]), weights[place * count + piece])
        return jnp.transpose(total)

    normed, scale = norm_rows(late_ref[...])
    grad = ffn_grad_ref[...]
    gain_grad_ref[:, 1:2] = jnp.sum(grad * normed, axis=1, keepdims=True)
    late_grad = out_grad_ref[...].astype(f32) + norm_rows_back(
        normed, scale, grad * gain_ref[:, 3:4]
    )
    mid_grad_ref[...] = late_grad
    late_grad_ref[...] = late_grad.astype(bf16)
    stage[...] = through(2, 0, late_grad_ref).astype(bf16).astype(f32)
    for head in range(HEADS):
        rows = slice(head * HEAD, (head + 1) * HEAD)
        query, keys = query_ref[head], key_ref[head]
        grad = stage[rows, :]
        inverse = 1.0 / total_ref[head]
        scaled = (grad * inverse).astype(bf16)
        total_grad = -jnp.sum(grad * out_ref[rows, :], axis=0, keepdims=True) * inverse
        attention = text_weights(keys, query)
        weight_grad = kernel_dot(flip(value_ref[head]), scaled)
        score_grad = (attention * (weight_grad + total_grad)).astype(bf16)
        query_grad = (kernel_dot(keys, score_grad) * SCALING).astype(bf16).astype(f32)
        key_grad_ref[head] = kernel_dot(query, score_grad, 1, 1) * SCALING
        value_grad_ref[head] = kernel_dot(scaled, attention.astype(bf16), 1, 1)
        normed, scale = norm_rows(raw_ref[head])
        stage[rows, :] = norm_rows_back(normed, scale, query_grad)
    raw_grad_ref[...] = stage[...].astype(bf16)
    grad = through(1, 1, raw_grad_ref)
    normed, scale = norm_rows(mid_ref[...])
    gain_grad_ref[:, 0:1] = jnp.sum(grad * normed, axis=1, keepdims=True)
    mid_grad = mid_grad_ref[...] + norm_rows_back(normed, scale, grad * gain_ref[:, 2:3])
    mid_grad_ref[...] = mid_grad
    mid_round_ref[...] = mid_grad.astype(bf16)
    attended_grad_ref[...] = through(0, 2, mid_round_ref).astype(bf16)


def middle_backward(index, arrays, weights, stamps):
    count = len(weights) // 3
    tokens = arrays[0].shape[1]
    rounded = jax.ShapeDtypeStruct((D, tokens), bf16)
    texts = jax.ShapeDtypeStruct((HEADS, HEAD, TEXT_PAD), f32)
    return pl.pallas_call(
        functools.partial(middle_backward_kernel, count, len(stamps)),
        out_shape=(
            rounded,
            rounded,
            jax.ShapeDtypeStruct((D, tokens), f32),
            rounded,
            rounded,
            texts,
            texts,
            jax.ShapeDtypeStruct((D, 2), f32),
        ),
        in_specs=[SMEM_WHOLE]
        + [VMEM_WHOLE] * 11
        + [ANY_WHOLE] * (3 * count + len(stamps)),
        out_specs=[VMEM_WHOLE] * 8,
        scratch_shapes=[
            pltpu.VMEM((3 * count, D // count, D), bf16),
            pltpu.VMEM((D, tokens), f32),
            pltpu.SemaphoreType.DMA((3 * count,)),
        ],
        compiler_params=pltpu.CompilerParams(vmem_limit_bytes=VMEM_LIMIT),
        cost_estimate=pl.CostEstimate(
            flops=14 * D * D * tokens, bytes_accessed=30 << 20, transcendentals=0
        ),
        name="middle_backward",
    )(index, *arrays, *weights, *stamps)


GELU_SCALE = math.sqrt(2.0 / math.pi)


def ffn_kernel(count, *refs):
    inputs, grads = refs[:count], refs[count : 2 * count]
    expand_ref, reduce_ref, hidden_ref, expand_in_ref = refs[2 * count : 2 * count + 4]
    outputs = refs[2 * count + 4 :]
    back_refs, out_refs = outputs[:count], outputs[count : 2 * count]
    value_sc, grad_sc = outputs[2 * count :]
    step = pl.program_id(0)

    for piece in range(count):

        @pl.when(step == piece)
        def _():
            value_sc[...] = flip(inputs[piece][...])
            grad_sc[...] = flip(grads[piece][...])

    value, grad = value_sc[...], grad_sc[...]
    back, out = 0.0, 0.0
    width = expand_ref.shape[1]
    chunk = 512
    for start in range(0, width, chunk):
        cols = slice(start, start + chunk)
        weight, reduce = expand_ref[:, cols], reduce_ref[:, cols]
        plain = kernel_dot(value, weight)
        square = plain * plain
        curve = jnp.tanh(GELU_SCALE * (plain + 0.044715 * square * plain))
        hidden = (0.5 * plain * (1.0 + curve)).astype(bf16)
        slope = 0.5 * (1.0 + curve) + 0.5 * plain * (1.0 - curve * curve) * (
            GELU_SCALE * (1.0 + 3.0 * 0.044715 * square)
        )
        hidden_ref[:, cols] = hidden
        expand_in = (kernel_dot(grad, reduce) * slope).astype(bf16)
        expand_in_ref[:, cols] = expand_in
        back = back + kernel_dot(expand_in, weight, 1, 1)
        out = out + kernel_dot(hidden, reduce, 1, 1)
    back = jnp.transpose(back.astype(bf16))
    out = jnp.transpose(out.astype(bf16))
    for piece in range(count):

        @pl.when(step == piece)
        def _():
            back_refs[piece][...] = back
            out_refs[piece][...] = out


def feed_forward(inputs, grads, bucket):
    count = len(inputs)
    tokens, width = inputs[0].shape[1], bucket.shape[1] // 2
    by_hidden = jax.ShapeDtypeStruct((count * tokens, width), bf16)
    by_piece = jax.ShapeDtypeStruct((D, tokens), bf16)
    whole = pl.BlockSpec((D, tokens), lambda step: (0, 0))
    hidden_spec = pl.BlockSpec((tokens, width), lambda step: (step, 0))
    return pl.pallas_call(
        functools.partial(ffn_kernel, count),
        out_shape=(by_hidden, by_hidden) + (by_piece,) * (2 * count),
        grid=(count,),
        in_specs=[whole] * (2 * count)
        + [pl.BlockSpec((D, width), lambda step, k=k: (0, k)) for k in range(2)],
        out_specs=[hidden_spec, hidden_spec] + [whole] * (2 * count),
        scratch_shapes=[pltpu.VMEM((tokens, D), bf16), pltpu.VMEM((tokens, D), bf16)],
        compiler_params=pltpu.CompilerParams(vmem_limit_bytes=VMEM_LIMIT),
        cost_estimate=pl.CostEstimate(
            flops=8 * D * count * tokens * width,
            bytes_accessed=30 << 20,
            transcendentals=count * tokens * width,
        ),
        name="feed_forward",
    )(*inputs, *grads, bucket, bucket)


def project_kernel(count, heads, *refs):
    values = refs[:count]
    weights = refs[count : count + 3]
    cos_ref, sin_ref = refs[count + 3 : count + 5]
    qkv_ref, raw_ref = refs[-2:]
    quarter = HEAD // 4
    rows = values[0].shape[1]
    for piece in range(count):
        lanes = pl.ds(piece * rows, rows)
        value = flip(values[piece][...])
        product = jnp.concatenate(
            [jnp.transpose(kernel_dot(value, weight[...])) for weight in weights], axis=0
        )
        cosine, sines = cos_ref[:, lanes], sin_ref[:, lanes]
        cos_row, cos_col = cosine[:quarter], cosine[quarter:]
        sin_row, sin_col = sines[:quarter], sines[quarter:]
        for part in range(3):
            for head in range(heads):
                start = (part * heads + head) * HEAD
                raw = product[start : start + HEAD]
                if part == 2:
                    qkv_ref[head, part, :, lanes] = raw.astype(bf16)
                    continue
                raw_ref[head, part, :, lanes] = raw
                normed = head_norm(raw)
                one, two, three, four = (
                    normed[k * quarter : (k + 1) * quarter] for k in range(4)
                )
                turned = jnp.concatenate(
                    [
                        one * cos_row - two * sin_row,
                        one * sin_row + two * cos_row,
                        three * cos_col - four * sin_col,
                        three * sin_col + four * cos_col,
                    ],
                    axis=0,
                )
                qkv_ref[head, part, :, lanes] = turned.astype(bf16)


def project(values, bucket, offset, heads, cosine, sines, stamps):
    count, rows = len(values), values[0].shape[1]
    third = (3 * heads * HEAD + 383) // 384 * 128
    columns = count * rows
    full = [pl.BlockSpec(member.shape, lambda g: (0, 0)) for member in (*values, cosine, sines)]
    return pl.pallas_call(
        functools.partial(project_kernel, count, heads),
        out_shape=(
            jax.ShapeDtypeStruct((heads, 3, HEAD, columns), bf16),
            jax.ShapeDtypeStruct((heads, 2, HEAD, columns), f32),
        ),
        grid=(1,),
        in_specs=full[:count]
        + [
            pl.BlockSpec((D, third), lambda g, k=k: (0, offset // third + k)) for k in range(3)
        ]
        + full[count:]
        + [ANY_WHOLE] * len(stamps),
        out_specs=[
            pl.BlockSpec((heads, 3, HEAD, columns), lambda g: (0, 0, 0, 0)),
            pl.BlockSpec((heads, 2, HEAD, columns), lambda g: (0, 0, 0, 0)),
        ],
        compiler_params=pltpu.CompilerParams(vmem_limit_bytes=VMEM_LIMIT),
        cost_estimate=pl.CostEstimate(
            flops=6 * columns * D * heads * HEAD, bytes_accessed=12 << 20, transcendentals=0
        ),
        name="project",
    )(*values, bucket, bucket, bucket, cosine, sines, *stamps)


def shards(
    tokens,
    skip_in,
    timestep,
    captions,
    null_mask,
    lengths,
    cotangent,
    skip_weight,
    shift_weight,
    self_input,
    self_output,
    cross_query,
    cross_pairs,
    cross_output,
    expand_weight,
    reduce_weight,
    null_caption,
    norm_gains,
):
    sp_count, cp_count = lax.axis_size("sp"), lax.axis_size("cp")
    dp_count = lax.axis_size("dp")
    dp_index, sp_index, cp_index = (lax.axis_index(name) for name in EVERY)
    place = (dp_index * sp_count + sp_index) * cp_count + cp_index
    packs, rows = tokens.shape[0], tokens.shape[1]
    held = packs * rows
    chunk = cp_count * rows
    group_heads = HEADS // cp_count
    pairs_dev = packs * group_heads // sp_count
    all_packs = lengths.shape[0]

    def lanes(value):
        spare = -value.shape[-1] % 128
        return jnp.pad(value, [(0, 0)] * (value.ndim - 1) + [(0, spare)])

    def split_columns(weight):
        columns = weight.shape[1] // cp_count
        blocks = jnp.swapaxes(weight.reshape(weight.shape[0], cp_count, columns), 0, 1)
        return trade_cp(blocks).reshape(cp_count * weight.shape[0], columns)

    def send_columns(weights):
        blocks = [
            jnp.concatenate(
                [jnp.split(weight, cp_count, axis=1)[k] for weight in weights], axis=1
            )
            for k in range(cp_count)
        ]
        return jnp.concatenate(send_cp(blocks), axis=0)

    def order_heads(weight):
        split = weight.reshape(weight.shape[0], 3, cp_count, -1)
        return jnp.swapaxes(split, 1, 2).reshape(weight.shape)

    def restore_heads(weight):
        split = weight.reshape(weight.shape[0], cp_count, 3, -1)
        return jnp.swapaxes(split, 1, 2).reshape(weight.shape)

    def pack(parts):
        return jnp.concatenate([lanes(part) for part in parts], axis=1)

    def unpack(bucket, widths):
        start, parts = 0, []
        for width in widths:
            parts.append(bucket[:, start : start + width])
            start += width + -width % 128
        return parts

    width = D // cp_count
    ff_width = expand_weight.shape[1] // cp_count
    group_rows = cp_count * self_output.shape[0]
    group_text = cp_count * cross_pairs.shape[0]
    head_widths = (width, width, 3 * width)
    mid_widths = (width, width, width, 2 * width)

    def gather_group(bucket):
        return lax.all_gather(bucket, GROUP, axis=0, tiled=True)

    skip_cols = split_columns(skip_weight)
    gain_columns = norm_gains.shape[1]
    shard = self_output.shape[0]
    fill = -3 * width % 128
    input_blocks = order_heads(self_input).reshape(shard, cp_count, 3 * width)
    input_blocks = jnp.swapaxes(jnp.pad(input_blocks, ((0, 0), (0, 0), (0, fill))), 0, 1)
    spare = jnp.pad(jnp.transpose(norm_gains), ((0, 0), (3 * width, fill - 4)))
    input_blocks = trade_cp(input_blocks + spare)
    head_bucket = jnp.concatenate(
        [
            pack([skip_cols[:group_rows], skip_cols[group_rows:]]),
            input_blocks.reshape(group_rows, -1),
        ],
        axis=1,
    )
    three = send_columns(
        tuple(after(member, head_bucket) for member in (self_output, cross_query, cross_output))
    )
    expand_weight = after(expand_weight, head_bucket)
    reduce_weight = after(reduce_weight, head_bucket)
    pairs_cols = jnp.pad(
        send_columns((after(cross_pairs, head_bucket),)), ((0, group_rows - group_text), (0, 0))
    )
    mid_bucket = pack(
        [three[:, :width], three[:, width : 2 * width], three[:, 2 * width :], pairs_cols]
    )
    mid_gathered = gather_group(mid_bucket)
    plain = rows % 128 == 0 and packs == 1 and group_rows % 16 == 0
    ff_bucket = send_columns((expand_weight, jnp.transpose(reduce_weight)))
    ff_gathered = gather_group(ff_bucket)
    expand_part, reduce_part = unpack(ff_gathered, (ff_width, ff_width))

    head_gathered = gather_group(head_bucket)
    one, two, input_part = unpack(head_gathered, head_widths)
    skip_part = jnp.stack(
        [one.reshape(-1, group_rows, width), two.reshape(-1, group_rows, width)], axis=1
    ).reshape(2 * D, width)
    skip_part = after(skip_part, ff_bucket)
    gain_start = 2 * (width + -width % 128) + 3 * width
    gain_columns_t = head_gathered[:, gain_start : gain_start + 4].astype(f32)
    gain_rows = jnp.transpose(gain_columns_t)

    def times(left, full, left_dim):
        return jnp.concatenate(
            reorder_cp([dot(left, part, left_dim, 0) for part in full]), axis=1
        )

    def times_rows(full, right, right_dim):
        return jnp.concatenate(
            reorder_cp([dot(part, right, 0, right_dim) for part in full]), axis=0
        )

    def column_blocks(value):
        return jnp.split(value, cp_count, axis=1)

    def row_blocks(value):
        return jnp.split(value, cp_count, axis=0)

    def back_sum(left, full, left_dim):
        return sum(dot(block, part, left_dim, 1) for block, part in zip(left, full))

    def back_rows(full, right):
        return sum(dot(part, block, 1, 1) for part, block in zip(full, right))

    def traded(blocks):
        came = trade_cp(jnp.stack(blocks))
        return reorder_cp([came[k] for k in range(cp_count)])

    own_lengths = lax.dynamic_slice_in_dim(lengths, dp_index * packs, packs, 0)
    describe = jax.vmap(segment_info, in_axes=(0, None))
    chunk_block = jnp.arange(cp_count, dtype=jnp.int32) ^ cp_index
    chunk_pos = sp_index * chunk + (
        chunk_block[:, None] * rows + jnp.arange(rows, dtype=jnp.int32)[None, :]
    ).reshape(-1)
    turned = (cp_index * rows // CELL).reshape(1)
    _, chunk_row, chunk_col, _ = describe(own_lengths, chunk_pos)
    block_pos = jnp.arange(sp_count * cp_count, dtype=jnp.int32) * rows
    all_segments, _, _, all_valid = describe(lengths, block_pos)
    own_segments = lax.dynamic_slice_in_dim(all_segments, dp_index * packs, packs, 0)
    own_valid = lax.dynamic_slice_in_dim(all_valid, dp_index * packs, packs, 0)
    block = sp_index * cp_count + cp_index
    block_image = lax.dynamic_index_in_dim(own_segments, block, 1, keepdims=False)
    block_valid = lax.dynamic_index_in_dim(own_valid, block, 1, keepdims=False)
    token_valid = jnp.broadcast_to(block_valid[:, None], (packs, rows)).reshape(held, 1)
    pair_pack = (sp_index * pairs_dev + jnp.arange(pairs_dev, dtype=jnp.int32)) // group_heads
    first_cells, last_cells, valid_cells = jax.vmap(cell_ranges)(own_lengths)
    first_cells = jnp.take(first_cells, pair_pack, axis=0)
    last_cells = jnp.take(last_cells, pair_pack, axis=0)
    valid_cells = jnp.take(valid_cells, pair_pack, axis=0)

    times_all = after(timestep, head_bucket)
    for bit in bits_of("dp"):
        other = trade_bit(times_all, "dp", bit)
        times_all = jnp.where(
            has_bit("dp", bit),
            jnp.concatenate([other, times_all]),
            jnp.concatenate([times_all, other]),
        )
    silu_all = jax.nn.silu(times_all.astype(f32)).astype(bf16)
    shard_rows = shift_weight.shape[0]
    silu_own = lax.dynamic_slice_in_dim(silu_all, place * shard_rows, shard_rows, 2)
    slot_ids = jnp.arange(IMGS, dtype=jnp.int32)
    all_pick = (all_segments[:, :, None] == slot_ids).astype(f32)
    silu_blocks = jnp.einsum("pbi,pik->pbk", all_pick, silu_own.astype(f32), precision=highest)
    silu_blocks = jnp.swapaxes(
        silu_blocks.reshape(dp_count, packs, sp_count * cp_count, shard_rows), 1, 2
    ).reshape(-1, shard_rows)
    shifts = scatter_every(
        dot(silu_blocks.astype(bf16), shift_weight, 1, 0).reshape(-1, packs, D)
    )
    shift_rows = jnp.broadcast_to(shifts[:, None, :], (packs, rows, D)).reshape(held, D)

    image_dev = captions.shape[1]
    near = lax.dynamic_slice_in_dim(own_segments, sp_index * cp_count, cp_count, 1)
    local = jnp.clip(near - cp_index * image_dev, 0, image_dev - 1)
    joined = jnp.concatenate([tokens.reshape(held, D), skip_in.reshape(held, D)], axis=1)
    joined_all = pieces_cp(after(joined, head_bucket))
    piece_index = cp_index.reshape(1)
    if plain:
        mixed_blocks = trade_cp(mix(piece_index, head_gathered, joined_all, width))
        base_t, normed_self_t = start_forward(
            mixed_blocks, gain_columns_t, shifts.reshape(D, 1)
        )
        normed_all = pieces_cp(normed_self_t)
    else:
        mixed_all = [dot(piece, skip_part, 1, 0).astype(bf16) for piece in joined_all]
        mixed_blocks = trade_cp(jnp.stack(reorder_cp(mixed_all)))
        mixed = jnp.concatenate([mixed_blocks[k] for k in range(cp_count)], axis=1).astype(f32)
        base_stream = norm_gain(mixed, gain_rows[0])
        normed_self = (norm_gain(base_stream, gain_rows[1]) + shift_rows).astype(bf16)
        normed_all = pieces_cp(jnp.transpose(normed_self))
    cosine, sines = jax.vmap(rope_tables)(chunk_row, chunk_col)
    if plain:
        offset = 2 * (width + -width % 128)
        qkv, raw = project(
            normed_all,
            head_gathered,
            offset,
            group_heads,
            cosine[0],
            sines[0],
            (),
        )
        qkv, raw = qkv[None], raw[None]
        query_raw, key_raw = raw[:, :, 0], raw[:, :, 1]
    normed_all = jnp.concatenate(normed_all, axis=1)
    cosine, sines = cosine[:, None], sines[:, None]
    if not plain:
        projected = dot(input_part, normed_all, 0, 0)
        projected = jnp.transpose(
            projected.reshape(3, group_heads, HEAD, cp_count, packs, rows), (4, 1, 0, 2, 3, 5)
        ).reshape(packs, group_heads, 3, HEAD, chunk)
        query_raw, key_raw = projected[:, :, 0], projected[:, :, 1]
        queries = turn_norm(query_raw, cosine, sines).astype(bf16)
        key_rows = turn_norm(key_raw, cosine, sines).astype(bf16)
        value_rows = projected[:, :, 2].astype(bf16)
        qkv = jnp.stack([queries, key_rows, value_rows], axis=2)

    caption_shard = jnp.pad(
        jnp.transpose(after(null_caption, joined_all[-2])), ((0, 0), (0, TEXT_PAD - TEXT))
    )
    caption_rows = caption_shard.shape[0]
    caption_full = jnp.transpose(gather_every(caption_shard).reshape(DT, TEXT_PAD))
    local = local + (ff_bucket[0, 0].astype(f32) * 0.0).astype(jnp.int32)
    offered = jnp.stack(
        [
            jnp.stack(
                [
                    lax.dynamic_index_in_dim(captions[p], local[p, k], 0, keepdims=False)
                    for p in range(packs)
                ]
            )
            for k in range(cp_count)
        ]
    )
    offered = jnp.pad(offered, ((0, 0), (0, 0), (0, TEXT_PAD - TEXT), (0, 0)))
    arrived = jnp.stack(send_cp([offered[k] for k in range(cp_count)]))
    own_null = jnp.take_along_axis(
        null_mask, block_image[:, None], axis=1
    )[:, 0]
    chosen = jnp.stack(
        [
            jnp.where(
                own_null[p] > 0,
                caption_full,
                lax.dynamic_index_in_dim(
                    arrived[:, p], block_image[p] // image_dev, 0, keepdims=False
                ),
            )
            for p in range(packs)
        ]
    )

    out_grad = after(cotangent.reshape(held, D).astype(f32) * token_valid, joined_all[-2])
    out_turned = out_grad.astype(bf16)
    out_turned = turn_over(out_turned) if plain else jnp.transpose(out_turned)
    out_grad = jnp.transpose(out_turned).astype(f32)
    reduce_pieces = pieces_cp(out_turned)

    def to_heads(value):
        value = value.reshape((sp_count, pairs_dev) + value.shape[2:])
        return lax.all_to_all(value, "sp", split_axis=0, concat_axis=0, tiled=True)

    def from_heads(value):
        value = lax.all_to_all(value, "sp", split_axis=0, concat_axis=0, tiled=True)
        return value.reshape((packs, group_heads) + value.shape[2:])

    if plain:
        *mid_parts, pairs_part = unpack_mid(mid_gathered, width, group_text, qkv)
    else:
        output_part, query_part, cross_part, pairs_part = (
            after(part, qkv) for part in unpack(mid_gathered, mid_widths)
        )
        pairs_part = pairs_part.reshape(-1, group_rows, 2 * width)[:, :group_text].reshape(
            DT, 2 * width
        )
        mid_parts = (output_part, query_part, cross_part)
    pairs_full = pieces_cp(pairs_part)
    output_full, query_full, cross_full = (pieces_cp(part) for part in mid_parts)
    qkv = to_heads(qkv)
    out_self, totals_self = self_forward(
        qkv,
        first_cells,
        last_cells,
        turned,
        tuple(reduce_pieces) if plain else (),
    )

    def to_tokens(value):
        value = value.reshape(sp_count, pairs_dev, HEAD, cp_count, rows)
        value = jnp.stack(reorder_cp([value[:, :, :, k] for k in range(cp_count)]))
        value = value.reshape(cp_count * sp_count, pairs_dev, HEAD, rows)
        value = lax.all_to_all(value, HEAD_ORDER, split_axis=0, concat_axis=0, tiled=True)
        value = value.reshape(cp_count, packs, group_heads, HEAD, rows)
        return jnp.transpose(value, (0, 2, 3, 1, 4)).reshape(D, held)

    def by_heads(value):
        value = value.reshape(cp_count, group_heads, HEAD, packs, rows)
        value = jnp.transpose(value, (0, 3, 1, 2, 4))
        value = value.reshape(cp_count * sp_count, pairs_dev, HEAD, rows)
        value = lax.all_to_all(value, HEAD_ORDER, split_axis=0, concat_axis=0, tiled=True)
        value = value.reshape(cp_count, sp_count, pairs_dev, HEAD, rows)
        value = reorder_cp([value[k] for k in range(cp_count)])
        return jnp.concatenate(value, axis=-1)

    def heads_of(value):
        value = value.reshape(HEADS, HEAD, packs, rows)
        return jnp.transpose(value, (2, 0, 1, 3)).reshape(packs * HEADS, HEAD, rows)

    def rows_of(value):
        value = value.reshape(packs, HEADS, HEAD, rows)
        return jnp.transpose(value, (1, 2, 0, 3)).reshape(D, held)

    attended = to_tokens(out_self.astype(bf16))
    paired = times_rows(pairs_full, chosen.reshape(packs * TEXT_PAD, DT), 1)
    paired = jnp.moveaxis(paired.reshape(2, HEADS, HEAD, packs, TEXT_PAD), 3, 0)
    text_raw = paired[:, 0].reshape(packs * HEADS, HEAD, TEXT_PAD)
    text_keys = head_norm(text_raw).astype(bf16)
    text_values = paired[:, 1].reshape(packs * HEADS, HEAD, TEXT_PAD).astype(bf16)
    differences = jnp.array(group_differences(), jnp.int32)
    group_order = differences ^ (dp_index * sp_count + sp_index)
    if plain:
        mid_weights = (*output_full, *query_full, *cross_full)
        (
            mid_t,
            late_t,
            lefts,
            cross_raw,
            cross_queries,
            out_cross,
            totals_cross,
            normed_ffn_t,
        ) = middle_forward(
            piece_index,
            attended,
            base_t,
            gain_columns_t,
            text_keys,
            text_values,
            mid_weights,
        )
        ffn_pieces = pieces_cp(normed_ffn_t)
        hidden, expand_in, *parts = feed_forward(
            ffn_pieces, reduce_pieces, ff_gathered
        )
        ffn_part, block_part = parts[:cp_count], parts[cp_count:]
    else:
        mid_stream = base_stream + times(attended, output_full, 0)
        normed_cross = norm_gain(mid_stream, gain_rows[2]).astype(bf16)
        cross_raw = heads_of(times_rows(query_full, normed_cross, 1))
        cross_queries = head_norm(cross_raw).astype(bf16)
        out_cross, totals_cross = cross_forward(cross_queries, text_keys, text_values)
        crossed = rows_of(out_cross.astype(bf16))
        late_stream = mid_stream + times(crossed, cross_full, 0)
        normed_ffn = norm_gain(late_stream, gain_rows[3]).astype(bf16)
        ffn_pieces = pieces_cp(jnp.transpose(normed_ffn))
        expanded = dot(jnp.concatenate(ffn_pieces, axis=1), expand_part, 0, 0)
        hidden = jax.nn.gelu(expanded, approximate=True).astype(bf16)

    def by_piece(value):
        value = value.astype(bf16).reshape(cp_count, held, D)
        return [value[k] for k in range(cp_count)]

    def sum_group(bucket):
        return lax.psum_scatter(bucket, GROUP, scatter_dimension=0, tiled=True)

    if not plain:
        gelu_back = jax.vjp(lambda preact: jax.nn.gelu(preact, approximate=True), expanded)[1]
        reduce_in = jnp.concatenate(reduce_pieces, axis=1)
        expand_in = gelu_back(dot(reduce_in, reduce_part, 0, 0))[0].astype(bf16)
        ffn_part = dot(expand_in, expand_part, 1, 1).astype(bf16)
        ffn_part = by_piece(ffn_part)
        block_part = by_piece(dot(hidden, reduce_part, 1, 1))
    ff_out = expand_grads(ffn_pieces, expand_in)
    if plain:
        keep, send = reduce_grads(reduce_pieces, hidden, group_order)
        ff_grads = sum_group(ff_out)
    else:
        reduce_out = dot(reduce_in, hidden, 1, 0).astype(bf16)
        ff_grads = sum_group(jnp.concatenate([ff_out, reduce_out], axis=1))
        ff_grads, reduce_sums = ff_grads[:, :ff_width], ff_grads[:, ff_width:]
    ffn_grad = scatter_cp(ffn_part)
    if plain:
        lefts = pieces_cp(after(lefts, ffn_grad))
    texts = after(chosen, ffn_grad).reshape(packs * TEXT_PAD, DT)
    texts = pieces_cp(jnp.transpose(texts))
    if plain:
        (
            late_round,
            cross_raw_grad,
            mid_grad,
            mid_round,
            attended_grad,
            ck_grad,
            cv_grad,
            gain_pair,
        ) = middle_backward(
            piece_index,
            (
                ffn_grad,
                out_turned,
                late_t,
                mid_t,
                gain_columns_t,
                cross_queries,
                text_keys,
                text_values,
                out_cross,
                totals_cross,
                cross_raw,
            ),
            mid_weights,
            (ff_out, keep, send),
        )
        gain_cross, gain_ffn = gain_pair[:, 0], gain_pair[:, 1]
        cout_in, cross_raw_grad, self_in = (
            reorder_cp(row_blocks(member)) for member in (late_round, cross_raw_grad, mid_round)
        )
    else:
        ffn_back = jax.vjp(norm_gain, late_stream, gain_rows[3])[1]
        late_part, gain_ffn = ffn_back(ffn_grad)
        late_grad = out_grad + late_part

        cout_in = column_blocks(late_grad.astype(bf16))
        cout_in = reorder_cp(cout_in)
        crossed_grad = heads_of(back_rows(cross_full, cout_in).astype(bf16))
        cq_grad, ck_grad, cv_grad = cross_backward(
            cross_queries, text_keys, text_values, crossed_grad, out_cross, totals_cross
        )
        cq_grad = cq_grad.astype(bf16).astype(f32)
        cross_raw_grad = rows_of(jax.vjp(head_norm, cross_raw)[1](cq_grad)[0].astype(bf16))
        cross_raw_grad = reorder_cp(row_blocks(cross_raw_grad))
        cross_norm_back = jax.vjp(norm_gain, mid_stream, gain_rows[2])[1]
        mid_part, gain_cross = cross_norm_back(
            back_sum(cross_raw_grad, query_full, 0)
        )
        mid_grad = late_grad + mid_part
        self_in = reorder_cp(column_blocks(mid_grad.astype(bf16)))
        attended_grad = back_rows(output_full, self_in).astype(bf16)
        normed_cross_t = jnp.transpose(normed_cross)
        cout_in = [jnp.transpose(member) for member in cout_in]
        self_in = [jnp.transpose(member) for member in self_in]
    if not plain:
        lefts = pieces_cp(jnp.stack([normed_cross_t, crossed, attended]))
    rights = exchange_cp(
        [
            jnp.stack([cross, late, mid])
            for cross, late, mid in zip(cross_raw_grad, cout_in, self_in)
        ]
    )
    attended_grad = by_heads(attended_grad)
    qkv_grad = self_backward(
        qkv,
        attended_grad,
        out_self,
        totals_self,
        first_cells,
        last_cells,
        valid_cells,
        turned,
        (*lefts, *texts) if plain else (),
    )
    stamp = qkv_grad
    qkv_grad = from_heads(qkv_grad)
    if plain:
        block_out = jnp.transpose((late_t + scatter_cp(block_part)).astype(bf16))
    else:
        block_out = (late_stream + scatter_cp(block_part)).astype(bf16)

    ck_grad = ck_grad.astype(bf16).astype(f32)
    text_raw_grad = jax.vjp(head_norm, text_raw)[1](ck_grad)[0].astype(bf16)
    paired_grad = jnp.stack(
        [
            text_raw_grad.reshape(packs, D, TEXT_PAD),
            cv_grad.reshape(packs, D, TEXT_PAD).astype(bf16),
        ],
        axis=1,
    ).reshape(packs, 2 * D, TEXT_PAD)
    paired_rows = jnp.swapaxes(paired_grad, 0, 1).reshape(2 * D, packs * TEXT_PAD)
    paired_rows = reorder_cp(row_blocks(paired_rows))
    pairs = exchange_cp(paired_rows)
    if plain:
        mid_out = mid_grads_bucket(lefts, rights, texts, pairs, stamp, dp_count * sp_count)
    else:
        lefts = jnp.concatenate(lefts, axis=2)
        rights = jnp.concatenate(rights, axis=2)
        pairs_grad = dot(
            jnp.concatenate(texts, axis=1), jnp.concatenate(pairs, axis=1), 1, 1
        )
        pairs_grad = jnp.pad(
            pairs_grad.astype(bf16).reshape(-1, group_text, 2 * width),
            ((0, 0), (0, group_rows - group_text), (0, 0)),
        ).reshape(D, 2 * width)
        mid_out = pack(
            [dot(lefts[k], rights[k], 1, 1).astype(bf16) for k in range(3)] + [pairs_grad]
        )
    mid_grads = sum_group(mid_out)
    null_sum = jnp.einsum(
        "p,pnt->nt", own_null.astype(f32), paired_grad.astype(f32), precision=highest
    ).astype(bf16)
    caption_grad = sum(
        dot(part, block, 1, 0)
        for part, block in zip(pairs_full, reorder_cp(row_blocks(null_sum)))
    )
    caption_sum = caption_grad

    qkv_grad = after(qkv_grad, ff_grads)
    turn = functools.partial(turn_norm, cosine=cosine, sines=sines)
    query_raw_grad = jax.vjp(turn, query_raw)[1](qkv_grad[:, :, 0].astype(f32))[0].astype(bf16)
    key_raw_grad = jax.vjp(turn, key_raw)[1](qkv_grad[:, :, 1].astype(f32))[0].astype(bf16)
    projected_grad = jnp.stack([query_raw_grad, key_raw_grad, qkv_grad[:, :, 2]], axis=0)
    projected_grad = jnp.transpose(
        projected_grad.reshape(3, packs, group_heads, HEAD, cp_count, rows), (0, 2, 3, 4, 1, 5)
    ).reshape(3 * group_heads * HEAD, cp_count * held)
    if plain:
        normed_part = jnp.split(
            dot(input_part, projected_grad, 1, 0).astype(bf16), cp_count, axis=1
        )
    else:
        normed_part = dot(projected_grad, input_part, 0, 1).astype(bf16)
    self_input_grad = dot(normed_all, projected_grad, 1, 1).astype(bf16)
    if plain:
        mixed_grad, sums = start_backward(
            mixed_blocks,
            gain_columns_t,
            base_t,
            mid_grad,
            scatter_cp([normed_part[k] for k in range(cp_count)]),
        )
        gain_skip, gain_self = sums[:, 0], sums[:, 1]
        shift_grads = sums[:, 2][None]
        came = trade_cp(mixed_grad)
        mixed_pieces = reorder_cp([came[k] for k in range(cp_count)])
        head_out = skip_grads_bucket(mixed_pieces, joined_all, self_input_grad)
        joined_part = [dot(piece, skip_part, 0, 1).astype(bf16) for piece in mixed_pieces]
    else:
        normed_self_grad = scatter_cp(by_piece(normed_part))
        self_norm_back = jax.vjp(norm_gain, base_stream, gain_rows[1])[1]
        base_part, gain_self = self_norm_back(normed_self_grad)
        shift_grads = jnp.sum(normed_self_grad.reshape(packs, rows, D), axis=1)
        base_grad = mid_grad + base_part
        skip_norm_back = jax.vjp(norm_gain, mixed, gain_rows[0])[1]
        mixed_grad, gain_skip = skip_norm_back(base_grad)
        mixed_pieces = traded(column_blocks(mixed_grad.astype(bf16)))
        mixed_in = jnp.concatenate(mixed_pieces, axis=0)
        skip_out = dot(jnp.concatenate(joined_all, axis=0), mixed_in, 0, 0).astype(bf16)
        skip_out = skip_out.reshape(-1, 2, shard, width)
        head_out = pack(
            [
                skip_out[:, 0].reshape(D, width),
                skip_out[:, 1].reshape(D, width),
                self_input_grad,
            ]
        )
        joined_part = dot(mixed_in, skip_part, 1, 1).astype(bf16).reshape(cp_count, held, 2 * D)
        joined_part = [joined_part[k] for k in range(cp_count)]
    head_grads = sum_group(head_out)
    if plain:
        reduce_sums = scatter_group_halves(
            keep, send, (stamp, normed_part[0], head_out)
        )
    caption_grad = scatter_every(
        after(caption_sum, head_out).astype(bf16).reshape(-1, caption_rows, TEXT_PAD)
    )
    joined_grad = scatter_cp(joined_part)

    shift_grads = after(shift_grads, head_out)
    gains_part = after(jnp.stack([gain_skip, gain_self, gain_cross, gain_ffn]), head_out)
    gains_grad = scatter_every(jnp.swapaxes(gains_part.reshape(4, -1, gain_columns), 0, 1))
    shift_weight_grad = lax.dot_general(
        silu_blocks,
        gather_every(shift_grads).reshape(-1, D),
        (((0,), (0,)), ((), ())),
        precision=highest,
        preferred_element_type=f32,
    )

    factor = all_packs * PACK / jnp.sum(lengths).astype(f32)

    def join_columns(bucket, widths):
        blocks = jnp.stack(send_cp(jnp.split(bucket, cp_count, axis=0)))
        start, parts = 0, []
        for size in widths:
            part = jnp.swapaxes(blocks[:, :, start : start + size], 0, 1)
            parts.append(part.astype(f32) * factor)
            start += size + -size % 128
        return parts

    def whole(part):
        return part.reshape(part.shape[0], -1)

    mid_grads = after(mid_grads, head_out)
    (expand_out,) = join_columns(after(ff_grads, head_out), (ff_width,))
    (reduce_out,) = join_columns(reduce_sums, (ff_width,))
    cross_query_out, cross_out_out, self_out_out = join_columns(
        mid_grads[:, : 3 * (width + -width % 128)], (width, width, width)
    )
    (pairs_out,) = join_columns(
        mid_grads[:group_text, 3 * (width + -width % 128) :], (2 * width,)
    )
    if plain:
        skip_out, input_out = finish_head(
            trade_cp(head_grads.reshape(cp_count, shard, -1)), factor
        )
    else:
        one, two, input_out = join_columns(head_grads, head_widths)
        skip_out = jnp.concatenate([whole(one), whole(two)], axis=0)
        input_out = restore_heads(whole(input_out))

    token_shape = (packs, rows, D)
    return (
        block_out.reshape(token_shape),
        (joined_grad[:, :D] * factor).astype(bf16).reshape(token_shape),
        (joined_grad[:, D:] * factor).astype(bf16).reshape(token_shape),
        skip_out,
        shift_weight_grad * factor,
        input_out,
        whole(self_out_out),
        whole(cross_query_out),
        whole(pairs_out),
        whole(cross_out_out),
        whole(expand_out),
        jnp.transpose(whole(reduce_out)),
        jnp.transpose(caption_grad)[:TEXT].astype(f32) * factor,
        gains_grad * factor,
    )


def solution(mesh):
    token_spec = P("dp", ("sp", "cp"), None)
    by_rows = P(EVERY, None)
    by_columns = P(None, EVERY)
    return jax.shard_map(
        shards,
        mesh=mesh,
        in_specs=(
            token_spec,
            token_spec,
            P("dp", None, None),
            P("dp", "cp", None, None),
            P("dp", None),
            P(),
            token_spec,
            by_rows,
            by_rows,
            by_rows,
            by_rows,
            by_rows,
            by_rows,
            by_rows,
            by_rows,
            by_columns,
            by_columns,
            by_columns,
        ),
        out_specs=(
            token_spec,
            token_spec,
            token_spec,
            by_rows,
            by_rows,
            by_rows,
            by_rows,
            by_rows,
            by_rows,
            by_rows,
            by_rows,
            by_columns,
            by_columns,
            by_columns,
        ),
        check_vma=False,
    )
```

```python
import functools
import math

import jax
import jax.numpy as jnp
from jax import lax
from jax.experimental import pallas as pl
from jax.experimental.pallas import tpu as pltpu
from jax.sharding import PartitionSpec as P

D = 1408
HEADS = 16
HEAD = 88
DT = 1024
TEXT = 333
TEXT_PAD = 384
BIG_SIDE = 32
SMALL_SIDE = 16
PACK = 4096
IMGS = 16
CELL = 256
CELLS = PACK // CELL
SCALING = 1.0 / math.sqrt(HEAD)

epsilon = 1e-06
highest = lax.Precision.HIGHEST
bf16 = jnp.bfloat16
f32 = jnp.float32
GROUP = ("dp", "sp")
EVERY = ("dp", "sp", "cp")
HEAD_ORDER = ("cp", "sp")


def layer_norm(vector, axis=-1):
    centred = vector - jnp.mean(vector, axis=axis, keepdims=True)
    return centred * lax.rsqrt(jnp.mean(centred * centred, axis=axis, keepdims=True) + epsilon)


def head_norm(vector):
    return layer_norm(vector, -2)


def norm_gain(vector, gain):
    return layer_norm(vector) * gain


def dot(left, right, left_dim, right_dim):
    return lax.dot_general(
        left, right, (((left_dim,), (right_dim,)), ((), ())), preferred_element_type=f32
    )


def segment_info(lengths, positions):
    seg_ends = jnp.cumsum(lengths)
    starts = seg_ends - lengths
    present = lengths > 0
    slot_ids = jnp.arange(lengths.shape[0], dtype=jnp.int32)
    segment = jnp.sum(
        ((seg_ends[None, :] <= positions[:, None]) & present[None, :]).astype(jnp.int32), axis=1
    )
    onehot = segment[:, None] == slot_ids[None, :]
    seg_start = jnp.sum(jnp.where(onehot, starts[None, :], 0), axis=1)
    seg_size = jnp.sum(jnp.where(onehot, lengths[None, :], 0), axis=1)
    side_len = jnp.where(seg_size == BIG_SIDE * BIG_SIDE, BIG_SIDE, SMALL_SIDE).astype(jnp.int32)
    offset = positions - seg_start
    images = jnp.sum(present.astype(jnp.int32))
    return (segment, offset // side_len, offset % side_len, (segment < images).astype(f32))


def cell_ranges(lengths):
    positions = jnp.arange(CELLS, dtype=jnp.int32) * CELL
    seg_ends = jnp.cumsum(lengths)
    present = lengths > 0
    segment = jnp.sum(
        ((seg_ends[None, :] <= positions[:, None]) & present[None, :]).astype(jnp.int32), axis=1
    )
    same = segment[:, None] == segment[None, :]
    cells = jnp.arange(CELLS, dtype=jnp.int32)
    first = jnp.min(jnp.where(same, cells[None, :], CELLS), axis=1)
    last = jnp.max(jnp.where(same, cells[None, :] + 1, 0), axis=1)
    return (first, last, jnp.sum(lengths) // CELL)


def rope_tables(grid_row, grid_col):
    quarter = HEAD // 4
    frequency = jnp.exp(jnp.arange(quarter, dtype=f32) * (-math.log(10000.0) / quarter))
    angles = jnp.concatenate(
        [
            frequency[:, None] * grid_row.astype(f32)[None, :],
            frequency[:, None] * grid_col.astype(f32)[None, :],
        ],
        axis=0,
    )
    return (jnp.cos(angles), jnp.sin(angles))


def rotate(vector, cosine, sines):
    quarter = HEAD // 4
    one, two, three, four = (
        vector[..., k * quarter : (k + 1) * quarter, :] for k in range(4)
    )
    cos_row, cos_col = cosine[..., :quarter, :], cosine[..., quarter:, :]
    sin_row, sin_col = sines[..., :quarter, :], sines[..., quarter:, :]
    return jnp.concatenate(
        [
            one * cos_row - two * sin_row,
            one * sin_row + two * cos_row,
            three * cos_col - four * sin_col,
            three * sin_col + four * cos_col,
        ],
        axis=-2,
    )


def turn_norm(vector, cosine, sines):
    return rotate(head_norm(vector), cosine, sines)


def trade_bit(value, axis, bit):
    count = lax.axis_size(axis)
    return lax.ppermute(value, axis, [(k, k ^ bit) for k in range(count)])


def bits_of(axis):
    count = lax.axis_size(axis)
    return [1 << k for k in range(count.bit_length() - 1)]


def has_bit(axis, bit):
    return (lax.axis_index(axis) // bit) % 2 == 1


def pieces_cp(value):
    pieces = [value]
    found = {0: value}
    for bit in reversed(bits_of("cp")):
        for key in list(found):
            found[key | bit] = trade_bit(found[key], "cp", bit)
    pieces = [found[key] for key in range(lax.axis_size("cp"))]
    return pieces


def reorder_cp(pieces):
    for bit in bits_of("cp"):
        high = has_bit("cp", bit)
        pieces = [
            jnp.where(high, pieces[key ^ bit], pieces[key]) for key in range(len(pieces))
        ]
    return pieces


def gather_cp(value):
    return jnp.stack(reorder_cp(pieces_cp(value)))


def scatter_cp(pieces):
    pieces = [piece.astype(bf16) for piece in pieces]
    for bit in bits_of("cp"):
        pieces = [
            (
                pieces[key].astype(f32) + trade_bit(pieces[key + 1], "cp", bit).astype(f32)
            ).astype(f32 if len(pieces) == 2 else bf16)
            for key in range(0, len(pieces), 2)
        ]
    return pieces[0]


def after(value, *others):
    for other in others:
        value = value + (other[(0,) * other.ndim].astype(f32) * 0.0).astype(value.dtype)
    return value


def exchange_cp(pieces):
    count = lax.axis_size("cp")
    return [pieces[0]] + [
        lax.ppermute(pieces[key], "cp", [(k, k ^ key) for k in range(count)])
        for key in range(1, count)
    ]


def trade_cp(blocks):
    return lax.all_to_all(blocks, "cp", split_axis=0, concat_axis=0, tiled=True)


def send_cp(blocks):
    return reorder_cp(exchange_cp(reorder_cp(blocks)))


def group_steps():
    steps = [("dp", bit, bit * lax.axis_size("sp")) for bit in bits_of("dp")]
    return steps + [("sp", bit, bit) for bit in bits_of("sp")]


def group_differences():
    differences = [0]
    for _, _, weight in reversed(group_steps()):
        differences = differences + [key ^ weight for key in differences]
    return differences


def scatter_group_halves(keep, send, first, waits):
    for step, (axis, bit, _) in enumerate(group_steps()):
        came = (trade_bit(send, axis, bit) if step else first).astype(f32)
        total = after(keep.astype(f32) + came, waits[step]).astype(bf16)
        half = total.shape[0] // 2
        keep, send = total[:half], total[half:]
        if step == len(group_steps()) - 1:
            return total
    return None


def gather_every(value):
    dims = []
    for axis in ("dp", "sp", "cp"):
        for bit in reversed(bits_of(axis)):
            other = trade_bit(value, axis, bit)
            value = jnp.where(
                has_bit(axis, bit), jnp.stack([other, value]), jnp.stack([value, other])
            )
            dims.append((axis, bit))
    depth = len(dims)
    value = jnp.transpose(
        value, tuple(reversed(range(depth))) + tuple(range(depth, value.ndim))
    )
    return value.reshape((-1,) + value.shape[depth:])


def scatter_every(value):
    cp_count = lax.axis_size("cp")
    value = jnp.swapaxes(value.reshape((-1, cp_count) + value.shape[1:]), 0, 1)
    for axis in ("cp", "dp", "sp"):
        for bit in reversed(bits_of(axis)) if axis != "cp" else bits_of(axis):
            if axis == "cp":
                halves = value.reshape((-1, 2) + value.shape[1:])
                first, second = halves[:, 0], halves[:, 1]
            else:
                halves = value.reshape((2, -1) + value.shape[1:])
                first, second = halves[0], halves[1]
            high = has_bit(axis, bit)
            keep = jnp.where(high, second, first)
            send = jnp.where(high, first, second)
            value = keep + trade_bit(send, axis, bit)
        if axis == "cp":
            value = value[0]
    return value[0]


def send_every(value):
    count = lax.axis_size("dp") * lax.axis_size("sp") * lax.axis_size("cp")
    value = jnp.broadcast_to(value[None], (count,) + value.shape)
    return lax.all_to_all(value, EVERY, split_axis=0, concat_axis=0, tiled=True)


def sum_every(value):
    came = lax.all_to_all(value, EVERY, split_axis=0, concat_axis=0, tiled=True)
    return jnp.sum(came.astype(f32), axis=0)


def flip(block):
    if block.shape[0] % 128 == 0 and block.shape[1] % 128 == 0:
        return jnp.transpose(block)
    return jnp.transpose(block.astype(f32)).astype(bf16)


def kernel_dot(left, right, left_dim=1, right_dim=0):
    return lax.dot_general(
        left, right, (((left_dim,), (right_dim,)), ((), ())), preferred_element_type=f32
    )


def over_cells(first, last, step, carry):
    count = last - first
    fours = count // 4

    def four(turn, current):
        for k in range(4):
            current = step(first + turn * 4 + k, current)
        return current

    carry = lax.fori_loop(0, fours, four, carry)
    return lax.fori_loop(first + fours * 4, last, step, carry)


def self_forward_kernel(per_cell, first_ref, last_ref, turned_ref, qkv_ref, *refs):
    out_ref, total_ref, *sent_ref, keys = refs[-4:] if per_cell else refs[-3:]
    pair = pl.program_id(0)
    per = qkv_ref.shape[-1] // CELL

    def where(cell):
        lanes = ((cell % per) ^ turned_ref[0]) * CELL
        return cell // per, pl.ds(pl.multiple_of(lanes, CELL), CELL)

    def turn_keys(cell, carry):
        chunk, lanes = where(cell)
        keys[cell] = flip(qkv_ref[chunk, 0, 1, :, lanes])
        return carry

    lax.fori_loop(0, CELLS, turn_keys, 0)

    def one_cell(cell, carry):
        chunk, lanes = where(cell)
        query = qkv_ref[chunk, 0, 0, :, lanes]

        def step(other, current):
            summed, totals = current
            key_chunk, key_lanes = where(other)
            weights = jnp.exp(kernel_dot(keys[other], query) * SCALING)
            totals = totals + jnp.sum(weights, axis=0, keepdims=True)
            summed = summed + kernel_dot(
                qkv_ref[key_chunk, 0, 2, :, key_lanes], weights.astype(bf16)
            )
            return (summed, totals)

        summed, totals = over_cells(
            first_ref[pair, cell],
            last_ref[pair, cell],
            step,
            (jnp.zeros((HEAD, CELL), f32), jnp.zeros((1, CELL), f32)),
        )
        out = summed / totals
        out_ref[chunk, 0, :, lanes] = out
        if per_cell:
            sent_ref[0][cell % per, chunk, 0] = out.astype(bf16)
        total_ref[chunk, 0, :, lanes] = totals
        return carry

    lax.fori_loop(0, CELLS, one_cell, 0)


def self_backward_kernel(
    first_ref,
    last_ref,
    valid_ref,
    turned_ref,
    qkv_ref,
    grad_ref,
    out_ref,
    total_ref,
    *refs,
):
    result_ref, keys, values, key_sums, value_sums = refs[-5:]
    pair = pl.program_id(0)
    per = qkv_ref.shape[-1] // CELL

    def where(cell):
        lanes = ((cell % per) ^ turned_ref[0]) * CELL
        return cell // per, pl.ds(pl.multiple_of(lanes, CELL), CELL)

    def prepare(cell, carry):
        chunk, lanes = where(cell)
        keys[cell] = flip(qkv_ref[chunk, 0, 1, :, lanes])
        values[cell] = flip(qkv_ref[chunk, 0, 2, :, lanes])
        key_sums[cell] = jnp.zeros((HEAD, CELL), f32)
        value_sums[cell] = jnp.zeros((HEAD, CELL), f32)
        result_ref[chunk, 0, 0, :, lanes] = jnp.zeros((HEAD, CELL), bf16)
        return carry

    lax.fori_loop(0, CELLS, prepare, 0)

    def one_cell(cell, carry):
        chunk, lanes = where(cell)
        query = qkv_ref[chunk, 0, 0, :, lanes]
        if len(grad_ref.shape) == 5:
            grad = grad_ref[cell % per, chunk, 0].astype(f32)
        else:
            grad = grad_ref[chunk, 0, :, lanes].astype(f32)
        inverse = 1.0 / total_ref[chunk, 0, :, lanes]
        scaled = (grad * inverse).astype(bf16)
        total_grad = (
            -jnp.sum(grad * out_ref[chunk, 0, :, lanes], axis=0, keepdims=True) * inverse
        )

        def step(other, query_sum):
            key_chunk, key_lanes = where(other)
            weights = jnp.exp(kernel_dot(keys[other], query) * SCALING)
            weight_grad = kernel_dot(values[other], scaled)
            score_grad = (weights * (weight_grad + total_grad)).astype(bf16)
            value_sums[other] += kernel_dot(scaled, weights.astype(bf16), 1, 1)
            key_sums[other] += kernel_dot(query, score_grad, 1, 1)
            return query_sum + kernel_dot(qkv_ref[key_chunk, 0, 1, :, key_lanes], score_grad)

        query_sum = over_cells(
            first_ref[pair, cell], last_ref[pair, cell], step, jnp.zeros((HEAD, CELL), f32)
        )
        result_ref[chunk, 0, 0, :, lanes] = (query_sum * SCALING).astype(bf16)
        return carry

    lax.fori_loop(0, valid_ref[pair], one_cell, 0)

    def finish(cell, carry):
        chunk, lanes = where(cell)
        result_ref[chunk, 0, 1, :, lanes] = (key_sums[cell] * SCALING).astype(bf16)
        result_ref[chunk, 0, 2, :, lanes] = value_sums[cell].astype(bf16)
        return carry

    lax.fori_loop(0, CELLS, finish, 0)


def pair_spec(shape):
    block = (shape[0], 1) + shape[2:]
    rest = (0,) * (len(shape) - 2)
    return pl.BlockSpec(block, lambda pair, *_: (0, pair) + rest)


VMEM_WHOLE = pl.BlockSpec(memory_space=pltpu.VMEM)
SMEM_WHOLE = pl.BlockSpec(memory_space=pltpu.SMEM)
ANY_WHOLE = pl.BlockSpec(memory_space=pl.ANY)
VMEM_LIMIT = 48 * 1024 * 1024


def self_forward(qkv, first, last, turned, stamps, per_cell):
    chunks, pairs, _, _, columns = qkv.shape
    out_shape = (chunks, pairs, HEAD, columns)
    total_shape = (chunks, pairs, 1, columns)
    sent_shape = (columns // CELL, chunks, pairs, HEAD, CELL)
    sent_spec = pl.BlockSpec(
        sent_shape[:2] + (1,) + sent_shape[3:], lambda pair, *_: (0, 0, pair, 0, 0)
    )
    return pl.pallas_call(
        functools.partial(self_forward_kernel, per_cell),
        out_shape=(
            jax.ShapeDtypeStruct(out_shape, f32),
            jax.ShapeDtypeStruct(total_shape, f32),
        )
        + (jax.ShapeDtypeStruct(sent_shape, bf16),) * per_cell,
        grid_spec=pltpu.PrefetchScalarGridSpec(
            num_scalar_prefetch=3,
            grid=(pairs,),
            in_specs=[pair_spec(qkv.shape)] + [pl.BlockSpec(memory_space=pl.ANY)] * len(stamps),
            out_specs=[pair_spec(out_shape), pair_spec(total_shape)] + [sent_spec] * per_cell,
            scratch_shapes=[pltpu.VMEM((CELLS, CELL, HEAD), bf16)],
        ),
        compiler_params=pltpu.CompilerParams(vmem_limit_bytes=VMEM_LIMIT),
        cost_estimate=pl.CostEstimate(flops=10**10, bytes_accessed=8 << 20, transcendentals=0),
        name="self_forward",
    )(first, last, turned, qkv, *stamps)


def self_backward(qkv, grad, out, totals, first, last, valid, turned, stamps):
    pairs = qkv.shape[1]
    return pl.pallas_call(
        self_backward_kernel,
        out_shape=jax.ShapeDtypeStruct(qkv.shape, bf16),
        grid_spec=pltpu.PrefetchScalarGridSpec(
            num_scalar_prefetch=4,
            grid=(pairs,),
            in_specs=[
                pair_spec(qkv.shape),
                pair_spec(grad.shape)
                if grad.ndim == 4
                else pl.BlockSpec(
                    grad.shape[:2] + (1,) + grad.shape[3:], lambda pair, *_: (0, 0, pair, 0, 0)
                ),
                pair_spec(out.shape),
                pair_spec(totals.shape),
            ]
            + [pl.BlockSpec(memory_space=pl.ANY)] * len(stamps),
            out_specs=pair_spec(qkv.shape),
            scratch_shapes=[
                pltpu.VMEM((CELLS, CELL, HEAD), bf16),
                pltpu.VMEM((CELLS, CELL, HEAD), bf16),
                pltpu.VMEM((CELLS, HEAD, CELL), f32),
                pltpu.VMEM((CELLS, HEAD, CELL), f32),
            ],
        ),
        compiler_params=pltpu.CompilerParams(vmem_limit_bytes=VMEM_LIMIT),
        cost_estimate=pl.CostEstimate(flops=18 * 10**9, bytes_accessed=16 << 20, transcendentals=0),
        name="self_backward",
    )(first, last, valid, turned, qkv, grad, out, totals, *stamps)


def text_weights(key_block, query):
    scores = kernel_dot(flip(key_block), query) * SCALING
    present = lax.broadcasted_iota(jnp.int32, scores.shape, 0) < TEXT
    return jnp.where(present, jnp.exp(scores), 0.0)


def cross_forward_kernel(query_ref, key_ref, value_ref, out_ref, total_ref):
    for head in range(query_ref.shape[0]):
        weights = text_weights(key_ref[head], query_ref[head])
        totals = jnp.sum(weights, axis=0, keepdims=True)
        out_ref[head] = kernel_dot(value_ref[head], weights.astype(bf16)) / totals
        total_ref[head] = totals


def cross_backward_kernel(
    query_ref,
    key_ref,
    value_ref,
    grad_ref,
    out_ref,
    total_ref,
    query_grad_ref,
    key_grad_ref,
    value_grad_ref,
):
    for head in range(query_ref.shape[0]):
        query, keys = query_ref[head], key_ref[head]
        grad = grad_ref[head].astype(f32)
        inverse = 1.0 / total_ref[head]
        scaled = (grad * inverse).astype(bf16)
        total_grad = -jnp.sum(grad * out_ref[head], axis=0, keepdims=True) * inverse
        weights = text_weights(keys, query)
        weight_grad = kernel_dot(flip(value_ref[head]), scaled)
        score_grad = (weights * (weight_grad + total_grad)).astype(bf16)
        query_grad_ref[head] = kernel_dot(keys, score_grad) * SCALING
        key_grad_ref[head] = kernel_dot(query, score_grad, 1, 1) * SCALING
        value_grad_ref[head] = kernel_dot(scaled, weights.astype(bf16), 1, 1)


HEADS_STEP = 4


def head_spec(shape):
    return pl.BlockSpec((HEADS_STEP,) + shape[1:], lambda step: (step, 0, 0))


def cross_forward(queries, keys, values):
    count, _, rows = queries.shape
    out_shape = (count, HEAD, rows)
    total_shape = (count, 1, rows)
    return pl.pallas_call(
        cross_forward_kernel,
        out_shape=(
            jax.ShapeDtypeStruct(out_shape, f32),
            jax.ShapeDtypeStruct(total_shape, f32),
        ),
        grid=(count // HEADS_STEP,),
        in_specs=[head_spec(queries.shape), head_spec(keys.shape), head_spec(values.shape)],
        out_specs=[head_spec(out_shape), head_spec(total_shape)],
        compiler_params=pltpu.CompilerParams(vmem_limit_bytes=VMEM_LIMIT),
        name="cross_forward",
    )(queries, keys, values)


def cross_backward(queries, keys, values, grad, out, totals):
    inputs = (queries, keys, values, grad, out, totals)
    return pl.pallas_call(
        cross_backward_kernel,
        out_shape=(
            jax.ShapeDtypeStruct(queries.shape, f32),
            jax.ShapeDtypeStruct(keys.shape, f32),
            jax.ShapeDtypeStruct(values.shape, f32),
        ),
        grid=(queries.shape[0] // HEADS_STEP,),
        in_specs=[head_spec(member.shape) for member in inputs],
        out_specs=[head_spec(queries.shape), head_spec(keys.shape), head_spec(values.shape)],
        compiler_params=pltpu.CompilerParams(vmem_limit_bytes=VMEM_LIMIT),
        name="cross_backward",
    )(*inputs)


def unpack_kernel(width, text, bucket_ref, stamp_ref, *outs):
    padded = width + -width % 128
    for part in range(3):
        block = bucket_ref[:, part * padded : (part + 1) * padded]
        outs[part][...] = flip(block)[:width]
    rows = D * text // DT
    for group in range(DT // text):
        outs[3][group * text : (group + 1) * text, :] = bucket_ref[
            group * rows : group * rows + text, 3 * padded : 3 * padded + 2 * width
        ]


def unpack_mid(bucket, width, text, stamp):
    part = jax.ShapeDtypeStruct((width, D), bf16)
    return pl.pallas_call(
        functools.partial(unpack_kernel, width, text),
        out_shape=(part, part, part, jax.ShapeDtypeStruct((DT, 2 * width), bf16)),
        in_specs=[VMEM_WHOLE, ANY_WHOLE],
        out_specs=[VMEM_WHOLE] * 4,
        compiler_params=pltpu.CompilerParams(vmem_limit_bytes=VMEM_LIMIT),
        cost_estimate=pl.CostEstimate(flops=1, bytes_accessed=12 << 20, transcendentals=0),
        name="unpack_mid",
    )(bucket, stamp)


def offer_kernel(count, which_ref, captions_ref, *refs):
    outputs = refs[-2 - count : -2]
    stage, sems = refs[-2:]
    copies = [
        pltpu.make_async_copy(captions_ref.at[0, which_ref[k]], stage.at[k], sems.at[k])
        for k in range(count)
    ]
    for copy in copies:
        copy.start()
    for k in range(count):
        copies[k].wait()
        rest = jnp.zeros((TEXT_PAD - TEXT, stage.shape[2]), f32)
        outputs[k][...] = jnp.concatenate([stage[k].astype(f32), rest], axis=0).astype(bf16)


def offer(which, captions, stamps):
    count = which.shape[0]
    shape = jax.ShapeDtypeStruct((TEXT_PAD, captions.shape[3]), bf16)
    return pl.pallas_call(
        functools.partial(offer_kernel, count),
        out_shape=(shape,) * count,
        in_specs=[SMEM_WHOLE] + [ANY_WHOLE] * (1 + len(stamps)),
        out_specs=[VMEM_WHOLE] * count,
        scratch_shapes=[
            pltpu.VMEM((count, TEXT, captions.shape[3]), bf16),
            pltpu.SemaphoreType.DMA((count,)),
        ],
        compiler_params=pltpu.CompilerParams(vmem_limit_bytes=VMEM_LIMIT),
        cost_estimate=pl.CostEstimate(flops=1, bytes_accessed=8 << 20, transcendentals=0),
        name="offer",
    )(which, captions, *stamps)


def gate(values, stamps):
    def kernel(*refs):
        pass

    return pl.pallas_call(
        kernel,
        out_shape=tuple(jax.ShapeDtypeStruct(value.shape, value.dtype) for value in values),
        in_specs=[ANY_WHOLE] * (len(values) + len(stamps)),
        out_specs=[ANY_WHOLE] * len(values),
        input_output_aliases={k: k for k in range(len(values))},
        cost_estimate=pl.CostEstimate(flops=1, bytes_accessed=1, transcendentals=0),
        name="gate",
    )(*values, *stamps)


def turn_over_kernel(value_ref, *refs):
    out_ref = refs[-1]
    out_ref[...] = flip(value_ref[...])


def turn_over(value, stamps):
    return pl.pallas_call(
        turn_over_kernel,
        out_shape=jax.ShapeDtypeStruct(value.shape[::-1], value.dtype),
        in_specs=[VMEM_WHOLE] + [ANY_WHOLE] * len(stamps),
        out_specs=VMEM_WHOLE,
        compiler_params=pltpu.CompilerParams(vmem_limit_bytes=VMEM_LIMIT),
        cost_estimate=pl.CostEstimate(flops=1, bytes_accessed=2 << 20, transcendentals=0),
        name="turn_over",
    )(value, *stamps)


def expand_grads_kernel(count, *refs):
    left = jnp.concatenate([ref[...] for ref in refs[:count]], axis=1)
    refs[-1][...] = kernel_dot(left, refs[count][...]).astype(bf16)


def expand_grads(pieces, right, stamps):
    steps = 2
    rows, width = D // steps, right.shape[1]
    return pl.pallas_call(
        functools.partial(expand_grads_kernel, len(pieces)),
        out_shape=jax.ShapeDtypeStruct((D, width), bf16),
        grid=(steps,),
        in_specs=[pl.BlockSpec((rows, pieces[0].shape[1]), lambda g: (g, 0))] * len(pieces)
        + [pl.BlockSpec(right.shape, lambda g: (0, 0))]
        + [ANY_WHOLE] * len(stamps),
        out_specs=pl.BlockSpec((rows, width), lambda g: (g, 0)),
        compiler_params=pltpu.CompilerParams(vmem_limit_bytes=VMEM_LIMIT),
        cost_estimate=pl.CostEstimate(
            flops=2 * D * right.shape[0] * width, bytes_accessed=12 << 20, transcendentals=0
        ),
        name="expand_grads",
    )(*pieces, right, *stamps)


def reduce_grads_kernel(group_ref, *refs):
    pieces, (right_ref, keep_ref, send_ref) = refs[:-3], refs[-3:]
    step, steps = pl.program_id(0), pl.num_programs(0)
    left = jnp.concatenate([ref[...] for ref in pieces], axis=1)
    product = kernel_dot(left, right_ref[...]).astype(bf16)

    @pl.when(step < steps // 2)
    def _():
        keep_ref[...] = product

    @pl.when(step >= steps // 2)
    def _():
        send_ref[...] = product


def reduce_grads(pieces, right, groups):
    steps, width = groups.shape[0], right.shape[1]
    rows, half = D // steps, steps // 2
    shape = jax.ShapeDtypeStruct((D // 2, width), bf16)
    return pl.pallas_call(
        reduce_grads_kernel,
        out_shape=(shape, shape),
        grid_spec=pltpu.PrefetchScalarGridSpec(
            num_scalar_prefetch=1,
            grid=(steps,),
            in_specs=[
                pl.BlockSpec((rows, pieces[0].shape[1]), lambda g, group: (group[g], 0))
            ]
            * len(pieces)
            + [pl.BlockSpec(right.shape, lambda g, group: (0, 0))],
            out_specs=[
                pl.BlockSpec((rows, width), lambda g, group: (jnp.minimum(g, half - 1), 0)),
                pl.BlockSpec((rows, width), lambda g, group: (jnp.maximum(g - half, 0), 0)),
            ],
        ),
        compiler_params=pltpu.CompilerParams(vmem_limit_bytes=VMEM_LIMIT),
        cost_estimate=pl.CostEstimate(
            flops=2 * D * right.shape[0] * width, bytes_accessed=12 << 20, transcendentals=0
        ),
        name="reduce_grads",
    )(groups, *pieces, right)


def mid_grads_kernel(count, width, groups, *refs):
    lefts, third, rights, texts, pairs = (refs[k * count : (k + 1) * count] for k in range(5))
    out_ref = refs[5 * count + 1]
    rows = out_ref.shape[0] // groups
    padded = width + -width % 128
    for part in range(3):
        product = sum(
            kernel_dot(left[part] if part < 2 else last[...], right[part], 1, 1)
            for left, last, right in zip(lefts, third, rights)
        )
        product = jnp.concatenate(
            [product, jnp.zeros((product.shape[0], padded - width), f32)], axis=1
        )
        out_ref[:, part * padded : (part + 1) * padded] = product.astype(bf16)
    text = texts[0].shape[0] // groups
    product = sum(kernel_dot(left[...], right[...], 1, 1) for left, right in zip(texts, pairs))
    rest = out_ref.shape[1] - 3 * padded
    product = jnp.concatenate(
        [product, jnp.zeros((product.shape[0], rest - 2 * width), f32)], axis=1
    ).astype(bf16)
    for group in range(groups):
        start = group * rows
        out_ref[start : start + text, 3 * padded :] = product[group * text : (group + 1) * text]
        out_ref[start + text : start + rows, 3 * padded :] = jnp.zeros((rows - text, rest), bf16)


def mid_grads_bucket(lefts, third, rights, texts, pairs, stamp, groups):
    count, width = len(lefts), rights[0].shape[1]
    steps = 2
    rows, text = D // steps, DT // steps
    columns = 3 * (width + -width % 128) + 2 * width + -2 * width % 128
    return pl.pallas_call(
        functools.partial(mid_grads_kernel, count, width, groups // steps),
        out_shape=jax.ShapeDtypeStruct((D, columns), bf16),
        grid=(steps,),
        in_specs=[pl.BlockSpec((2, rows, lefts[0].shape[2]), lambda g: (0, g, 0))] * count
        + [pl.BlockSpec((rows, third[0].shape[1]), lambda g: (g, 0))] * count
        + [pl.BlockSpec(rights[0].shape, lambda g: (0, 0, 0))] * count
        + [pl.BlockSpec((text, texts[0].shape[1]), lambda g: (g, 0))] * count
        + [pl.BlockSpec(pairs[0].shape, lambda g: (0, 0))] * count
        + [ANY_WHOLE],
        out_specs=pl.BlockSpec((rows, columns), lambda g: (g, 0)),
        compiler_params=pltpu.CompilerParams(vmem_limit_bytes=VMEM_LIMIT),
        cost_estimate=pl.CostEstimate(
            flops=10 * D * D * width, bytes_accessed=24 << 20, transcendentals=0
        ),
        name="mid_grads",
    )(*lefts, *third, *rights, *texts, *pairs, stamp)


def skip_grads_kernel(count, width, *refs):
    rights, lefts = refs[:count], refs[count : 2 * count]
    input_ref, gain_ref, out_ref = refs[2 * count :]
    product = sum(kernel_dot(left[...], right[...]) for left, right in zip(lefts, rights))
    padded = width + -width % 128
    quarter = width // (2 * count)
    product = jnp.transpose(product)
    group_rows = count * quarter
    fill = jnp.zeros((group_rows, padded - width), f32)
    for group in range(product.shape[0] // width):
        for part in range(2):
            starts = [
                group * width + (2 * k + part) * quarter for k in range(count)
            ]
            block = jnp.concatenate(
                [product[start : start + quarter] for start in starts], axis=0
            )
            out_ref[
                group * group_rows : (group + 1) * group_rows,
                part * padded : (part + 1) * padded,
            ] = jnp.concatenate([block, fill], axis=1).astype(bf16)
    out_ref[:, 2 * padded : 2 * padded + input_ref.shape[1]] = input_ref[...]
    rest = out_ref.shape[1] - 2 * padded - input_ref.shape[1]
    gains = jnp.concatenate(
        [gain_ref[...], jnp.zeros((out_ref.shape[0], rest - gain_ref.shape[1]), f32)], axis=1
    )
    out_ref[:, 2 * padded + input_ref.shape[1] :] = gains.astype(bf16)


def skip_grads_bucket(lefts, rights, inputs, gains):
    count, width = len(lefts), lefts[0].shape[0]
    columns = 2 * (width + -width % 128) + inputs.shape[1] + -inputs.shape[1] % 128
    return pl.pallas_call(
        functools.partial(skip_grads_kernel, count, width),
        out_shape=jax.ShapeDtypeStruct((D, columns), bf16),
        grid=(2,),
        in_specs=[pl.BlockSpec((rights[0].shape[0], D), lambda g: (0, g))] * count
        + [pl.BlockSpec(lefts[0].shape, lambda g: (0, 0))] * count
        + [pl.BlockSpec((D // 2, member.shape[1]), lambda g: (g, 0)) for member in (inputs, gains)],
        out_specs=pl.BlockSpec((D // 2, columns), lambda g: (g, 0)),
        compiler_params=pltpu.CompilerParams(vmem_limit_bytes=VMEM_LIMIT),
        cost_estimate=pl.CostEstimate(
            flops=4 * D * width * count * 256, bytes_accessed=16 << 20, transcendentals=0
        ),
        name="skip_grads",
    )(*rights, *lefts, inputs, gains)


def finish_kernel(factor_ref, blocks_ref, skip_ref, input_ref, gain_ref):
    factor = factor_ref[0, 0]
    count, shard, _ = blocks_ref.shape
    width = skip_ref.shape[1] // count
    padded = width + -width % 128
    blocks = [blocks_ref[k].astype(f32) * factor for k in range(count)]
    for part in range(2):
        skip_ref[part * shard : (part + 1) * shard, :] = jnp.concatenate(
            [block[:, part * padded : part * padded + width] for block in blocks], axis=1
        )
    start = 2 * padded + 3 * width
    gain_ref[...] = sum(block[:, start : start + 4] for block in blocks)
    input_ref[...] = jnp.concatenate(
        [
            block[:, 2 * padded + part * width : 2 * padded + (part + 1) * width]
            for part in range(3)
            for block in blocks
        ],
        axis=1,
    )


def finish_head(blocks, factor):
    count, shard, _ = blocks.shape
    return pl.pallas_call(
        finish_kernel,
        out_shape=(
            jax.ShapeDtypeStruct((2 * shard, D), f32),
            jax.ShapeDtypeStruct((shard, 3 * D), f32),
            jax.ShapeDtypeStruct((shard, 4), f32),
        ),
        in_specs=[SMEM_WHOLE, VMEM_WHOLE],
        out_specs=[VMEM_WHOLE] * 3,
        compiler_params=pltpu.CompilerParams(vmem_limit_bytes=VMEM_LIMIT),
        cost_estimate=pl.CostEstimate(flops=1, bytes_accessed=2 << 20, transcendentals=0),
        name="finish_head",
    )(factor.reshape(1, 1), blocks)


def norm_rows(value):
    centred = value - jnp.mean(value, axis=0, keepdims=True)
    scale = lax.rsqrt(jnp.mean(centred * centred, axis=0, keepdims=True) + epsilon)
    return centred * scale, scale


def norm_rows_back(normed, scale, grad):
    return scale * (
        grad
        - jnp.mean(grad, axis=0, keepdims=True)
        - normed * jnp.mean(grad * normed, axis=0, keepdims=True)
    )


def fetch(sources, targets, sems, base):
    copies = [
        pltpu.make_async_copy(source, target, sems.at[base + k])
        for k, (source, target) in enumerate(zip(sources, targets))
    ]
    for copy in copies:
        copy.start()
    return copies


def mix_kernel(count, padded, *refs):
    index_ref, bucket_ref = refs[:2]
    pieces = refs[2 : 2 + count]
    out_ref, weight = refs[-2:]
    width = weight.shape[1]
    half = width // 2
    for group in range(weight.shape[0] // width):
        for part in range(2):
            start = group * width + part * half
            weight[start : start + half, :] = bucket_ref[
                group * half : (group + 1) * half, part * padded : part * padded + width
            ]
    for piece in range(count):
        out_ref[piece ^ index_ref[0]] = kernel_dot(pieces[piece][...], weight[...]).astype(bf16)


def mix(index, bucket, pieces, width, stamps):
    count, padded = len(pieces), width + -width % 128
    rows = pieces[0].shape[0]
    return pl.pallas_call(
        functools.partial(mix_kernel, count, padded),
        out_shape=jax.ShapeDtypeStruct((count, rows, width), bf16),
        grid=(1,),
        in_specs=[SMEM_WHOLE, pl.BlockSpec((D, 2 * padded), lambda g: (0, 0))]
        + [pl.BlockSpec(pieces[0].shape, lambda g: (0, 0))] * count
        + [ANY_WHOLE] * len(stamps),
        out_specs=pl.BlockSpec((count, rows, width), lambda g: (0, 0, 0)),
        scratch_shapes=[pltpu.VMEM((2 * D, width), bf16)],
        compiler_params=pltpu.CompilerParams(vmem_limit_bytes=VMEM_LIMIT),
        cost_estimate=pl.CostEstimate(
            flops=4 * D * width * count * rows, bytes_accessed=8 << 20, transcendentals=0
        ),
        name="mix",
    )(index, bucket, *pieces, *stamps)


def mixed_rows(blocks_ref, stage):
    width = blocks_ref.shape[2]
    for block in range(blocks_ref.shape[0]):
        turned = jnp.transpose(blocks_ref[block].astype(f32))
        stage[block * width : (block + 1) * width, :] = turned
    return stage[...]


def start_kernel(blocks_ref, gain_ref, shift_ref, base_ref, normed_ref, stage):
    base = norm_rows(mixed_rows(blocks_ref, stage))[0] * gain_ref[:, 0:1]
    base_ref[...] = base
    normed = norm_rows(base)[0] * gain_ref[:, 1:2] + shift_ref[...]
    normed_ref[...] = normed.astype(bf16)


def start_forward(blocks, gains, shift):
    tokens = blocks.shape[1]
    return pl.pallas_call(
        start_kernel,
        out_shape=(
            jax.ShapeDtypeStruct((D, tokens), f32),
            jax.ShapeDtypeStruct((D, tokens), bf16),
        ),
        in_specs=[VMEM_WHOLE] * 3,
        out_specs=[VMEM_WHOLE] * 2,
        scratch_shapes=[pltpu.VMEM((D, tokens), f32)],
        compiler_params=pltpu.CompilerParams(vmem_limit_bytes=VMEM_LIMIT),
        cost_estimate=pl.CostEstimate(flops=1, bytes_accessed=8 << 20, transcendentals=0),
        name="start_forward",
    )(blocks, gains, shift)


def start_back_kernel(
    blocks_ref, gain_ref, base_ref, mid_grad_ref, grad_ref, out_ref, sums_ref, stage
):
    normed, scale = norm_rows(base_ref[...])
    grad = grad_ref[...]
    sums_ref[:, 1:2] = jnp.sum(grad * normed, axis=1, keepdims=True)
    sums_ref[:, 2:3] = jnp.sum(grad, axis=1, keepdims=True)
    base_grad = mid_grad_ref[...] + norm_rows_back(normed, scale, grad * gain_ref[:, 1:2])
    normed, scale = norm_rows(mixed_rows(blocks_ref, stage))
    sums_ref[:, 0:1] = jnp.sum(base_grad * normed, axis=1, keepdims=True)
    mixed_grad = norm_rows_back(normed, scale, base_grad * gain_ref[:, 0:1]).astype(bf16)
    width = out_ref.shape[1]
    for block in range(out_ref.shape[0]):
        out_ref[block] = mixed_grad[block * width : (block + 1) * width]


def start_backward(blocks, gains, base, mid_grad, grad):
    count, tokens, width = blocks.shape
    return pl.pallas_call(
        start_back_kernel,
        out_shape=(
            jax.ShapeDtypeStruct((count, width, tokens), bf16),
            jax.ShapeDtypeStruct((D, 3), f32),
        ),
        in_specs=[VMEM_WHOLE] * 5,
        out_specs=[VMEM_WHOLE] * 2,
        scratch_shapes=[pltpu.VMEM((D, tokens), f32)],
        compiler_params=pltpu.CompilerParams(vmem_limit_bytes=VMEM_LIMIT),
        cost_estimate=pl.CostEstimate(flops=1, bytes_accessed=10 << 20, transcendentals=0),
        name="start_backward",
    )(blocks, gains, base, mid_grad, grad)


def middle_forward_kernel(count, *refs):
    index_ref, attended_ref, base_ref, gain_ref, key_ref, value_ref = refs[:6]
    sources = refs[6 : 6 + 3 * count]
    (
        mid_ref,
        late_ref,
        lefts_ref,
        raw_ref,
        query_ref,
        out_ref,
        total_ref,
        ffn_ref,
    ) = refs[6 + 3 * count : 14 + 3 * count]
    weights, sems = refs[14 + 3 * count :]
    copies = fetch(sources, [weights.at[k] for k in range(3 * count)], sems, 0)
    index = index_ref[0]
    width = D // count
    heads = HEADS // count

    def rows_of_piece(piece):
        return pl.ds(pl.multiple_of((piece ^ index) * width, 32), width)

    attended = attended_ref[...]
    for piece in range(count):
        copies[piece].wait()
        rows = rows_of_piece(piece)
        mid_ref[rows, :] = base_ref[rows, :] + kernel_dot(weights[piece], attended)
    normed = (norm_rows(mid_ref[...])[0] * gain_ref[:, 2:3]).astype(bf16)
    lefts_ref[0] = normed
    for piece in range(count):
        copies[count + piece].wait()
        product = kernel_dot(weights[count + piece], normed)
        for head in range(heads):
            raw_ref[(piece ^ index) * heads + head] = product[head * HEAD : (head + 1) * HEAD]
    for head in range(HEADS):
        query = norm_rows(raw_ref[head])[0].astype(bf16)
        query_ref[head] = query
        attention = text_weights(key_ref[head], query)
        totals = jnp.sum(attention, axis=0, keepdims=True)
        out = kernel_dot(value_ref[head], attention.astype(bf16)) / totals
        out_ref[head * HEAD : (head + 1) * HEAD, :] = out
        total_ref[head] = totals
    crossed = out_ref[...].astype(bf16)
    lefts_ref[1] = crossed
    for piece in range(count):
        copies[2 * count + piece].wait()
        rows = rows_of_piece(piece)
        late_ref[rows, :] = mid_ref[rows, :] + kernel_dot(weights[2 * count + piece], crossed)
    ffn_ref[...] = (norm_rows(late_ref[...])[0] * gain_ref[:, 3:4]).astype(bf16)


def middle_forward(index, attended, base, gains, keys, values, weights):
    count = len(weights) // 3
    tokens = attended.shape[1]
    stream = jax.ShapeDtypeStruct((D, tokens), f32)
    by_head = (HEADS, HEAD, tokens)
    return pl.pallas_call(
        functools.partial(middle_forward_kernel, count),
        out_shape=(
            stream,
            stream,
            jax.ShapeDtypeStruct((2, D, tokens), bf16),
            jax.ShapeDtypeStruct(by_head, f32),
            jax.ShapeDtypeStruct(by_head, bf16),
            stream,
            jax.ShapeDtypeStruct((HEADS, 1, tokens), f32),
            jax.ShapeDtypeStruct((D, tokens), bf16),
        ),
        in_specs=[SMEM_WHOLE] + [VMEM_WHOLE] * 5 + [ANY_WHOLE] * (3 * count),
        out_specs=[VMEM_WHOLE] * 8,
        scratch_shapes=[
            pltpu.VMEM((3 * count, D // count, D), bf16),
            pltpu.SemaphoreType.DMA((3 * count,)),
        ],
        compiler_params=pltpu.CompilerParams(vmem_limit_bytes=VMEM_LIMIT),
        cost_estimate=pl.CostEstimate(
            flops=10 * D * D * tokens, bytes_accessed=24 << 20, transcendentals=0
        ),
        name="middle_forward",
    )(index, attended, base, gains, keys, values, *weights)


def middle_backward_kernel(count, stamps, *refs):
    (
        index_ref,
        ffn_grad_ref,
        out_grad_ref,
        late_ref,
        mid_ref,
        gain_ref,
        query_ref,
        key_ref,
        value_ref,
        out_ref,
        total_ref,
        raw_ref,
    ) = refs[:12]
    sources = refs[12 : 12 + 3 * count]
    (
        late_grad_ref,
        raw_grad_ref,
        mid_grad_ref,
        mid_round_ref,
        attended_grad_ref,
        key_grad_ref,
        value_grad_ref,
        gain_grad_ref,
    ) = refs[12 + stamps + 3 * count : 20 + stamps + 3 * count]
    weights, stage, sems = refs[20 + stamps + 3 * count :]
    order = [2, 1, 0]
    copies = []
    for place in order:
        copies += fetch(
            sources[place * count : (place + 1) * count],
            [weights.at[place * count + k] for k in range(count)],
            sems,
            place * count,
        )
    index = index_ref[0]
    width = D // count

    def through(place, turn, source_ref):
        total = 0.0
        for piece in range(count):
            copies[turn * count + piece].wait()
            rows = pl.ds(pl.multiple_of((piece ^ index) * width, 32), width)
            total = total + kernel_dot(flip(source_ref[rows, :]), weights[place * count + piece])
        return jnp.transpose(total)

    normed, scale = norm_rows(late_ref[...])
    grad = ffn_grad_ref[...]
    gain_grad_ref[:, 1:2] = jnp.sum(grad * normed, axis=1, keepdims=True)
    late_grad = out_grad_ref[...].astype(f32) + norm_rows_back(
        normed, scale, grad * gain_ref[:, 3:4]
    )
    mid_grad_ref[...] = late_grad
    late_grad_ref[...] = late_grad.astype(bf16)
    stage[...] = through(2, 0, late_grad_ref).astype(bf16).astype(f32)
    for head in range(HEADS):
        rows = slice(head * HEAD, (head + 1) * HEAD)
        query, keys = query_ref[head], key_ref[head]
        grad = stage[rows, :]
        inverse = 1.0 / total_ref[head]
        scaled = (grad * inverse).astype(bf16)
        total_grad = -jnp.sum(grad * out_ref[rows, :], axis=0, keepdims=True) * inverse
        attention = text_weights(keys, query)
        weight_grad = kernel_dot(flip(value_ref[head]), scaled)
        score_grad = (attention * (weight_grad + total_grad)).astype(bf16)
        query_grad = (kernel_dot(keys, score_grad) * SCALING).astype(bf16).astype(f32)
        key_grad_ref[head] = kernel_dot(query, score_grad, 1, 1) * SCALING
        value_grad_ref[head] = kernel_dot(scaled, attention.astype(bf16), 1, 1)
        normed, scale = norm_rows(raw_ref[head])
        stage[rows, :] = norm_rows_back(normed, scale, query_grad)
    raw_grad_ref[...] = stage[...].astype(bf16)
    grad = through(1, 1, raw_grad_ref)
    normed, scale = norm_rows(mid_ref[...])
    gain_grad_ref[:, 0:1] = jnp.sum(grad * normed, axis=1, keepdims=True)
    mid_grad = mid_grad_ref[...] + norm_rows_back(normed, scale, grad * gain_ref[:, 2:3])
    mid_grad_ref[...] = mid_grad
    mid_round_ref[...] = mid_grad.astype(bf16)
    attended_grad_ref[...] = through(0, 2, mid_round_ref).astype(bf16)


def middle_backward(index, arrays, weights, stamps):
    count = len(weights) // 3
    tokens = arrays[0].shape[1]
    rounded = jax.ShapeDtypeStruct((D, tokens), bf16)
    texts = jax.ShapeDtypeStruct((HEADS, HEAD, TEXT_PAD), f32)
    return pl.pallas_call(
        functools.partial(middle_backward_kernel, count, len(stamps)),
        out_shape=(
            rounded,
            rounded,
            jax.ShapeDtypeStruct((D, tokens), f32),
            rounded,
            rounded,
            texts,
            texts,
            jax.ShapeDtypeStruct((D, 2), f32),
        ),
        in_specs=[SMEM_WHOLE]
        + [VMEM_WHOLE] * 11
        + [ANY_WHOLE] * (3 * count + len(stamps)),
        out_specs=[VMEM_WHOLE] * 8,
        scratch_shapes=[
            pltpu.VMEM((3 * count, D // count, D), bf16),
            pltpu.VMEM((D, tokens), f32),
            pltpu.SemaphoreType.DMA((3 * count,)),
        ],
        compiler_params=pltpu.CompilerParams(vmem_limit_bytes=VMEM_LIMIT),
        cost_estimate=pl.CostEstimate(
            flops=14 * D * D * tokens, bytes_accessed=30 << 20, transcendentals=0
        ),
        name="middle_backward",
    )(index, *arrays, *weights, *stamps)


GELU_SCALE = math.sqrt(2.0 / math.pi)


def ffn_kernel(count, stamps, *refs):
    inputs, grads = refs[:count], refs[count : 2 * count]
    expand_ref, reduce_ref = refs[2 * count : 2 * count + 2]
    hidden_ref, expand_in_ref, *outputs = refs[2 * count + 2 + stamps :]
    back_refs = outputs[:count]
    value_sc, grad_sc, back_sc = outputs[count:]
    step, steps = pl.program_id(0), pl.num_programs(0)
    tokens = inputs[0].shape[1]

    @pl.when(step == 0)
    def _():
        for piece in range(count):
            rows = slice(piece * tokens, (piece + 1) * tokens)
            value_sc[rows, :] = flip(inputs[piece][...])
            grad_sc[rows, :] = flip(grads[piece][...])

    weight = expand_ref[...]
    for half in range(2):
        rows = slice(half * count * tokens // 2, (half + 1) * count * tokens // 2)
        plain = kernel_dot(value_sc[rows, :], weight)
        square = plain * plain
        curve = jnp.tanh(plain * (GELU_SCALE + (GELU_SCALE * 0.044715) * square))
        above, half_plain = 1.0 + curve, 0.5 * plain
        hidden_ref[rows, :] = (half_plain * above).astype(bf16)
        steep = GELU_SCALE + (GELU_SCALE * 3.0 * 0.044715) * square
        slope = above * (0.5 + half_plain * (1.0 - curve) * steep)
        expand_in_ref[rows, :] = (kernel_dot(grad_sc[rows, :], reduce_ref[...]) * slope).astype(
            bf16
        )
    for piece in range(count):
        rows = slice(piece * tokens, (piece + 1) * tokens)
        part = kernel_dot(weight, expand_in_ref[rows, :], 1, 1)

        @pl.when(step == 0)
        def _():
            back_sc[piece] = part

        @pl.when((step > 0) & (step < steps - 1))
        def _():
            back_sc[piece] += part

        @pl.when(step == steps - 1)
        def _():
            back_refs[piece][...] = (back_sc[piece] + part).astype(bf16)


def feed_forward(inputs, grads, bucket, stamps):
    count = len(inputs)
    tokens, width = inputs[0].shape[1], bucket.shape[1] // 2
    steps = 3
    chunk = width // steps
    by_hidden = jax.ShapeDtypeStruct((count * tokens, width), bf16)
    by_piece = jax.ShapeDtypeStruct((D, tokens), bf16)
    whole = pl.BlockSpec((D, tokens), lambda step: (0, 0))
    hidden_spec = pl.BlockSpec((count * tokens, chunk), lambda step: (0, step))
    return pl.pallas_call(
        functools.partial(ffn_kernel, count, len(stamps)),
        out_shape=(by_hidden, by_hidden) + (by_piece,) * count,
        grid=(steps,),
        in_specs=[whole] * (2 * count)
        + [pl.BlockSpec((D, chunk), lambda step, k=k: (0, k * steps + step)) for k in range(2)]
        + [ANY_WHOLE] * len(stamps),
        out_specs=[hidden_spec, hidden_spec] + [whole] * count,
        scratch_shapes=[
            pltpu.VMEM((count * tokens, D), bf16),
            pltpu.VMEM((count * tokens, D), bf16),
            pltpu.VMEM((count, D, tokens), f32),
        ],
        compiler_params=pltpu.CompilerParams(vmem_limit_bytes=VMEM_LIMIT),
        cost_estimate=pl.CostEstimate(
            flops=6 * D * count * tokens * width,
            bytes_accessed=24 << 20,
            transcendentals=count * tokens * width,
        ),
        name="feed_forward",
    )(*inputs, *grads, bucket, bucket, *stamps)


def reduce_kernel(count, hidden_ref, reduce_ref, stamp_ref, *outputs):
    tokens = hidden_ref.shape[0] // count
    for piece in range(count):
        hidden = hidden_ref[piece * tokens : (piece + 1) * tokens, :]
        outputs[piece][...] = kernel_dot(reduce_ref[...], hidden, 1, 1).astype(bf16)


def reduce_parts(hidden, bucket, stamp, count):
    width = hidden.shape[1]
    tokens = hidden.shape[0] // count
    by_piece = jax.ShapeDtypeStruct((D, tokens), bf16)
    whole = pl.BlockSpec((D, tokens), lambda step: (0, 0))
    return pl.pallas_call(
        functools.partial(reduce_kernel, count),
        out_shape=(by_piece,) * count,
        grid=(1,),
        in_specs=[
            pl.BlockSpec(hidden.shape, lambda step: (0, 0)),
            pl.BlockSpec((D, width), lambda step: (0, 1)),
            ANY_WHOLE,
        ],
        out_specs=[whole] * count,
        compiler_params=pltpu.CompilerParams(vmem_limit_bytes=VMEM_LIMIT),
        cost_estimate=pl.CostEstimate(
            flops=2 * D * count * tokens * width, bytes_accessed=12 << 20, transcendentals=0
        ),
        name="reduce_parts",
    )(hidden, bucket, stamp)


def project_kernel(count, heads, *refs):
    values = refs[:count]
    weights = refs[count : count + 3]
    cos_ref, sin_ref = refs[count + 3 : count + 5]
    qkv_ref, raw_ref = refs[-2:]
    quarter = HEAD // 4
    rows = values[0].shape[1]
    for piece in range(count):
        lanes = pl.ds(piece * rows, rows)
        value = flip(values[piece][...])
        product = jnp.concatenate(
            [jnp.transpose(kernel_dot(value, weight[...])) for weight in weights], axis=0
        )
        cosine, sines = cos_ref[:, lanes], sin_ref[:, lanes]
        cos_row, cos_col = cosine[:quarter], cosine[quarter:]
        sin_row, sin_col = sines[:quarter], sines[quarter:]
        for part in range(3):
            for head in range(heads):
                start = (part * heads + head) * HEAD
                raw = product[start : start + HEAD]
                if part == 2:
                    qkv_ref[head, part, :, lanes] = raw.astype(bf16)
                    continue
                raw_ref[head, part, :, lanes] = raw
                normed = head_norm(raw)
                one, two, three, four = (
                    normed[k * quarter : (k + 1) * quarter] for k in range(4)
                )
                turned = jnp.concatenate(
                    [
                        one * cos_row - two * sin_row,
                        one * sin_row + two * cos_row,
                        three * cos_col - four * sin_col,
                        three * sin_col + four * cos_col,
                    ],
                    axis=0,
                )
                qkv_ref[head, part, :, lanes] = turned.astype(bf16)


def project(values, bucket, offset, heads, cosine, sines, stamps):
    count, rows = len(values), values[0].shape[1]
    third = (3 * heads * HEAD + 383) // 384 * 128
    columns = count * rows
    full = [pl.BlockSpec(member.shape, lambda g: (0, 0)) for member in (*values, cosine, sines)]
    return pl.pallas_call(
        functools.partial(project_kernel, count, heads),
        out_shape=(
            jax.ShapeDtypeStruct((heads, 3, HEAD, columns), bf16),
            jax.ShapeDtypeStruct((heads, 2, HEAD, columns), f32),
        ),
        grid=(1,),
        in_specs=full[:count]
        + [
            pl.BlockSpec((D, third), lambda g, k=k: (0, offset // third + k)) for k in range(3)
        ]
        + full[count:]
        + [ANY_WHOLE] * len(stamps),
        out_specs=[
            pl.BlockSpec((heads, 3, HEAD, columns), lambda g: (0, 0, 0, 0)),
            pl.BlockSpec((heads, 2, HEAD, columns), lambda g: (0, 0, 0, 0)),
        ],
        compiler_params=pltpu.CompilerParams(vmem_limit_bytes=VMEM_LIMIT),
        cost_estimate=pl.CostEstimate(
            flops=6 * columns * D * heads * HEAD, bytes_accessed=12 << 20, transcendentals=0
        ),
        name="project",
    )(*values, bucket, bucket, bucket, cosine, sines, *stamps)


def shards(
    tokens,
    skip_in,
    timestep,
    captions,
    null_mask,
    lengths,
    cotangent,
    skip_weight,
    shift_weight,
    self_input,
    self_output,
    cross_query,
    cross_pairs,
    cross_output,
    expand_weight,
    reduce_weight,
    null_caption,
    norm_gains,
):
    sp_count, cp_count = lax.axis_size("sp"), lax.axis_size("cp")
    dp_count = lax.axis_size("dp")
    dp_index, sp_index, cp_index = (lax.axis_index(name) for name in EVERY)
    place = (dp_index * sp_count + sp_index) * cp_count + cp_index
    packs, rows = tokens.shape[0], tokens.shape[1]
    held = packs * rows
    chunk = cp_count * rows
    group_heads = HEADS // cp_count
    pairs_dev = packs * group_heads // sp_count
    all_packs = lengths.shape[0]

    def lanes(value):
        spare = -value.shape[-1] % 128
        return jnp.pad(value, [(0, 0)] * (value.ndim - 1) + [(0, spare)])

    def split_columns(weight):
        columns = weight.shape[1] // cp_count
        blocks = jnp.swapaxes(weight.reshape(weight.shape[0], cp_count, columns), 0, 1)
        return trade_cp(blocks).reshape(cp_count * weight.shape[0], columns)

    def send_columns(weights):
        blocks = [
            jnp.concatenate(
                [jnp.split(weight, cp_count, axis=1)[k] for weight in weights], axis=1
            )
            for k in range(cp_count)
        ]
        return jnp.concatenate(send_cp(blocks), axis=0)

    def order_heads(weight):
        split = weight.reshape(weight.shape[0], 3, cp_count, -1)
        return jnp.swapaxes(split, 1, 2).reshape(weight.shape)

    def restore_heads(weight):
        split = weight.reshape(weight.shape[0], cp_count, 3, -1)
        return jnp.swapaxes(split, 1, 2).reshape(weight.shape)

    def pack(parts):
        return jnp.concatenate([lanes(part) for part in parts], axis=1)

    def unpack(bucket, widths):
        start, parts = 0, []
        for width in widths:
            parts.append(bucket[:, start : start + width])
            start += width + -width % 128
        return parts

    width = D // cp_count
    ff_width = expand_weight.shape[1] // cp_count
    group_rows = cp_count * self_output.shape[0]
    group_text = cp_count * cross_pairs.shape[0]
    head_widths = (width, width, 3 * width)
    mid_widths = (width, width, width, 2 * width)

    def gather_group(bucket):
        return lax.all_gather(bucket, GROUP, axis=0, tiled=True)

    skip_cols = split_columns(skip_weight)
    gain_columns = norm_gains.shape[1]
    shard = self_output.shape[0]
    fill = -3 * width % 128
    input_blocks = order_heads(self_input).reshape(shard, cp_count, 3 * width)
    input_blocks = jnp.swapaxes(jnp.pad(input_blocks, ((0, 0), (0, 0), (0, fill))), 0, 1)
    spare = jnp.pad(jnp.transpose(norm_gains), ((0, 0), (3 * width, fill - 4)))
    input_blocks = trade_cp(input_blocks + spare)
    head_bucket = jnp.concatenate(
        [
            pack([skip_cols[:group_rows], skip_cols[group_rows:]]),
            input_blocks.reshape(group_rows, -1),
        ],
        axis=1,
    )
    three = send_columns(
        tuple(after(member, head_bucket) for member in (self_output, cross_query, cross_output))
    )
    expand_weight = after(expand_weight, head_bucket)
    reduce_weight = after(reduce_weight, head_bucket)
    pairs_cols = jnp.pad(
        send_columns((after(cross_pairs, head_bucket),)), ((0, group_rows - group_text), (0, 0))
    )
    mid_bucket = pack(
        [three[:, :width], three[:, width : 2 * width], three[:, 2 * width :], pairs_cols]
    )
    mid_gathered = gather_group(mid_bucket)
    plain = rows == CELL and packs == 1 and group_rows % 16 == 0
    ff_bucket = send_columns((expand_weight, jnp.transpose(reduce_weight)))
    ff_gathered = gather_group(ff_bucket)
    expand_part, reduce_part = unpack(ff_gathered, (ff_width, ff_width))

    head_gathered = gather_group(head_bucket)
    one, two, input_part = unpack(head_gathered, head_widths)
    skip_part = jnp.stack(
        [one.reshape(-1, group_rows, width), two.reshape(-1, group_rows, width)], axis=1
    ).reshape(2 * D, width)
    skip_part = after(skip_part, ff_bucket)
    gain_start = 2 * (width + -width % 128) + 3 * width
    gain_columns_t = head_gathered[:, gain_start : gain_start + 4].astype(f32)
    gain_rows = jnp.transpose(gain_columns_t)

    def times(left, full, left_dim):
        return jnp.concatenate(
            reorder_cp([dot(left, part, left_dim, 0) for part in full]), axis=1
        )

    def times_rows(full, right, right_dim):
        return jnp.concatenate(
            reorder_cp([dot(part, right, 0, right_dim) for part in full]), axis=0
        )

    def column_blocks(value):
        return jnp.split(value, cp_count, axis=1)

    def row_blocks(value):
        return jnp.split(value, cp_count, axis=0)

    def back_sum(left, full, left_dim):
        return sum(dot(block, part, left_dim, 1) for block, part in zip(left, full))

    def back_rows(full, right):
        return sum(dot(part, block, 1, 1) for part, block in zip(full, right))

    def traded(blocks):
        came = trade_cp(jnp.stack(blocks))
        return reorder_cp([came[k] for k in range(cp_count)])

    own_lengths = lax.dynamic_slice_in_dim(lengths, dp_index * packs, packs, 0)
    describe = jax.vmap(segment_info, in_axes=(0, None))
    chunk_block = jnp.arange(cp_count, dtype=jnp.int32) ^ cp_index
    chunk_pos = sp_index * chunk + (
        chunk_block[:, None] * rows + jnp.arange(rows, dtype=jnp.int32)[None, :]
    ).reshape(-1)
    turned = (cp_index * rows // CELL).reshape(1)
    _, chunk_row, chunk_col, _ = describe(own_lengths, chunk_pos)
    block_pos = jnp.arange(sp_count * cp_count, dtype=jnp.int32) * rows
    all_segments, _, _, all_valid = describe(lengths, block_pos)
    own_segments = lax.dynamic_slice_in_dim(all_segments, dp_index * packs, packs, 0)
    own_valid = lax.dynamic_slice_in_dim(all_valid, dp_index * packs, packs, 0)
    block = sp_index * cp_count + cp_index
    block_image = lax.dynamic_index_in_dim(own_segments, block, 1, keepdims=False)
    block_valid = lax.dynamic_index_in_dim(own_valid, block, 1, keepdims=False)
    token_valid = jnp.broadcast_to(block_valid[:, None], (packs, rows)).reshape(held, 1)
    pair_pack = (sp_index * pairs_dev + jnp.arange(pairs_dev, dtype=jnp.int32)) // group_heads
    first_cells, last_cells, valid_cells = jax.vmap(cell_ranges)(own_lengths)
    first_cells = jnp.take(first_cells, pair_pack, axis=0)
    last_cells = jnp.take(last_cells, pair_pack, axis=0)
    valid_cells = jnp.take(valid_cells, pair_pack, axis=0)

    times_all = after(timestep, head_bucket)
    for bit in bits_of("dp"):
        other = trade_bit(times_all, "dp", bit)
        times_all = jnp.where(
            has_bit("dp", bit),
            jnp.concatenate([other, times_all]),
            jnp.concatenate([times_all, other]),
        )
    silu_all = jax.nn.silu(times_all.astype(f32)).astype(bf16)
    shard_rows = shift_weight.shape[0]
    silu_own = lax.dynamic_slice_in_dim(silu_all, place * shard_rows, shard_rows, 2)
    slot_ids = jnp.arange(IMGS, dtype=jnp.int32)
    all_pick = (all_segments[:, :, None] == slot_ids).astype(f32)
    silu_blocks = jnp.einsum("pbi,pik->pbk", all_pick, silu_own.astype(f32), precision=highest)
    silu_blocks = jnp.swapaxes(
        silu_blocks.reshape(dp_count, packs, sp_count * cp_count, shard_rows), 1, 2
    ).reshape(-1, shard_rows)
    shifts = scatter_every(
        dot(silu_blocks.astype(bf16), shift_weight, 1, 0).reshape(-1, packs, D)
    )
    shift_rows = jnp.broadcast_to(shifts[:, None, :], (packs, rows, D)).reshape(held, D)

    image_dev = captions.shape[1]
    near = lax.dynamic_slice_in_dim(own_segments, sp_index * cp_count, cp_count, 1)
    local = jnp.clip(near - cp_index * image_dev, 0, image_dev - 1)
    caption_shard = jnp.pad(
        jnp.transpose(after(null_caption, head_bucket)), ((0, 0), (0, TEXT_PAD - TEXT))
    )
    caption_rows = caption_shard.shape[0]
    caption_full = jnp.transpose(gather_every(caption_shard).reshape(DT, TEXT_PAD))
    joined = jnp.concatenate([tokens.reshape(held, D), skip_in.reshape(held, D)], axis=1)
    joined_all = pieces_cp(after(joined, head_bucket))
    piece_index = cp_index.reshape(1)
    if plain:
        mixed_blocks = trade_cp(mix(piece_index, head_gathered, joined_all, width, (caption_full,)))
        base_t, normed_self_t = start_forward(
            mixed_blocks, gain_columns_t, shifts.reshape(D, 1)
        )
        normed_all = pieces_cp(normed_self_t)
    else:
        mixed_all = [dot(piece, skip_part, 1, 0).astype(bf16) for piece in joined_all]
        mixed_blocks = trade_cp(jnp.stack(reorder_cp(mixed_all)))
        mixed = jnp.concatenate([mixed_blocks[k] for k in range(cp_count)], axis=1).astype(f32)
        base_stream = norm_gain(mixed, gain_rows[0])
        normed_self = (norm_gain(base_stream, gain_rows[1]) + shift_rows).astype(bf16)
        normed_all = pieces_cp(jnp.transpose(normed_self))
    cosine, sines = jax.vmap(rope_tables)(chunk_row, chunk_col)
    if plain:
        offset = 2 * (width + -width % 128)
        qkv, raw = project(
            normed_all,
            head_gathered,
            offset,
            group_heads,
            cosine[0],
            sines[0],
            (),
        )
        qkv, raw = qkv[None], raw[None]
        query_raw, key_raw = raw[:, :, 0], raw[:, :, 1]
    normed_all = jnp.concatenate(normed_all, axis=1)
    cosine, sines = cosine[:, None], sines[:, None]
    if not plain:
        projected = dot(input_part, normed_all, 0, 0)
        projected = jnp.transpose(
            projected.reshape(3, group_heads, HEAD, cp_count, packs, rows), (4, 1, 0, 2, 3, 5)
        ).reshape(packs, group_heads, 3, HEAD, chunk)
        query_raw, key_raw = projected[:, :, 0], projected[:, :, 1]
        queries = turn_norm(query_raw, cosine, sines).astype(bf16)
        key_rows = turn_norm(key_raw, cosine, sines).astype(bf16)
        value_rows = projected[:, :, 2].astype(bf16)
        qkv = jnp.stack([queries, key_rows, value_rows], axis=2)

    if plain:
        offered = offer(local[0, jnp.arange(cp_count) ^ cp_index], captions, (qkv,))
        arrived = jnp.stack(reorder_cp(exchange_cp(list(offered))))[:, None]
    else:
        offered = jnp.stack(
            [
                jnp.stack(
                    [
                        lax.dynamic_index_in_dim(captions[p], local[p, k], 0, keepdims=False)
                        for p in range(packs)
                    ]
                )
                for k in range(cp_count)
            ]
        )
        offered = jnp.pad(offered, ((0, 0), (0, 0), (0, TEXT_PAD - TEXT), (0, 0)))
        arrived = jnp.stack(send_cp([offered[k] for k in range(cp_count)]))
    own_null = jnp.take_along_axis(
        null_mask, block_image[:, None], axis=1
    )[:, 0]
    chosen = jnp.stack(
        [
            jnp.where(
                own_null[p] > 0,
                caption_full,
                lax.dynamic_index_in_dim(
                    arrived[:, p], block_image[p] // image_dev, 0, keepdims=False
                ),
            )
            for p in range(packs)
        ]
    )

    out_grad = cotangent.reshape(held, D).astype(f32) * token_valid
    out_turned = out_grad.astype(bf16)
    out_turned = turn_over(out_turned, (qkv,)) if plain else jnp.transpose(out_turned)
    out_grad = jnp.transpose(out_turned).astype(f32)
    reduce_pieces = pieces_cp(out_turned)

    def to_heads(value):
        value = value.reshape((sp_count, pairs_dev) + value.shape[2:])
        return lax.all_to_all(value, "sp", split_axis=0, concat_axis=0, tiled=True)

    def from_heads(value):
        value = lax.all_to_all(value, "sp", split_axis=0, concat_axis=0, tiled=True)
        return value.reshape((packs, group_heads) + value.shape[2:])

    if plain:
        *mid_parts, pairs_part = unpack_mid(
            mid_gathered, width, group_text, reduce_pieces[2]
        )
    else:
        output_part, query_part, cross_part, pairs_part = (
            after(part, qkv) for part in unpack(mid_gathered, mid_widths)
        )
        pairs_part = pairs_part.reshape(-1, group_rows, 2 * width)[:, :group_text].reshape(
            DT, 2 * width
        )
        mid_parts = (output_part, query_part, cross_part)
    pairs_full = pieces_cp(pairs_part)
    output_full, query_full, cross_full = (pieces_cp(part) for part in mid_parts)
    qkv = to_heads(qkv)
    out_self, totals_self, *sent = self_forward(
        qkv,
        first_cells,
        last_cells,
        turned,
        tuple(reduce_pieces) if plain else (),
        int(plain),
    )

    def to_tokens(value):
        value = value.reshape(sp_count, pairs_dev, HEAD, cp_count, rows)
        value = jnp.stack(reorder_cp([value[:, :, :, k] for k in range(cp_count)]))
        value = value.reshape(cp_count * sp_count, pairs_dev, HEAD, rows)
        value = lax.all_to_all(value, HEAD_ORDER, split_axis=0, concat_axis=0, tiled=True)
        value = value.reshape(cp_count, packs, group_heads, HEAD, rows)
        return jnp.transpose(value, (0, 2, 3, 1, 4)).reshape(D, held)

    def by_heads(value):
        value = value.reshape(cp_count, group_heads, HEAD, packs, rows)
        value = jnp.transpose(value, (0, 3, 1, 2, 4))
        value = value.reshape(cp_count * sp_count, pairs_dev, HEAD, rows)
        value = lax.all_to_all(value, HEAD_ORDER, split_axis=0, concat_axis=0, tiled=True)
        value = value.reshape(cp_count, sp_count, pairs_dev, HEAD, rows)
        value = reorder_cp([value[k] for k in range(cp_count)])
        return jnp.concatenate(value, axis=-1)

    def heads_of(value):
        value = value.reshape(HEADS, HEAD, packs, rows)
        return jnp.transpose(value, (2, 0, 1, 3)).reshape(packs * HEADS, HEAD, rows)

    def rows_of(value):
        value = value.reshape(packs, HEADS, HEAD, rows)
        return jnp.transpose(value, (1, 2, 0, 3)).reshape(D, held)

    if plain:
        attended = lax.all_to_all(
            sent[0].reshape(cp_count * sp_count, pairs_dev, HEAD, rows),
            HEAD_ORDER,
            split_axis=0,
            concat_axis=0,
            tiled=True,
        ).reshape(D, held)
    else:
        attended = to_tokens(out_self.astype(bf16))
    paired = times_rows(pairs_full, chosen.reshape(packs * TEXT_PAD, DT), 1)
    paired = jnp.moveaxis(paired.reshape(2, HEADS, HEAD, packs, TEXT_PAD), 3, 0)
    text_raw = paired[:, 0].reshape(packs * HEADS, HEAD, TEXT_PAD)
    text_keys = head_norm(text_raw).astype(bf16)
    text_values = paired[:, 1].reshape(packs * HEADS, HEAD, TEXT_PAD).astype(bf16)
    differences = jnp.array(group_differences(), jnp.int32)
    group_order = differences ^ (dp_index * sp_count + sp_index)
    if plain:
        mid_weights = (*output_full, *query_full, *cross_full)
        (
            mid_t,
            late_t,
            lefts,
            cross_raw,
            cross_queries,
            out_cross,
            totals_cross,
            normed_ffn_t,
        ) = middle_forward(
            piece_index,
            attended,
            base_t,
            gain_columns_t,
            text_keys,
            text_values,
            mid_weights,
        )
        ffn_pieces = pieces_cp(normed_ffn_t)
        (lefts,) = gate((lefts,), (ffn_pieces[2],))
        lefts_other = trade_bit(lefts, "cp", 2)
        hidden, expand_in, *ffn_part = feed_forward(
            ffn_pieces, reduce_pieces, ff_gathered, ()
        )
    else:
        mid_stream = base_stream + times(attended, output_full, 0)
        normed_cross = norm_gain(mid_stream, gain_rows[2]).astype(bf16)
        cross_raw = heads_of(times_rows(query_full, normed_cross, 1))
        cross_queries = head_norm(cross_raw).astype(bf16)
        out_cross, totals_cross = cross_forward(cross_queries, text_keys, text_values)
        crossed = rows_of(out_cross.astype(bf16))
        late_stream = mid_stream + times(crossed, cross_full, 0)
        normed_ffn = norm_gain(late_stream, gain_rows[3]).astype(bf16)
        ffn_pieces = pieces_cp(jnp.transpose(normed_ffn))
        expanded = dot(jnp.concatenate(ffn_pieces, axis=1), expand_part, 0, 0)
        hidden = jax.nn.gelu(expanded, approximate=True).astype(bf16)

    def by_piece(value):
        value = value.astype(bf16).reshape(cp_count, held, D)
        return [value[k] for k in range(cp_count)]

    def sum_group(bucket):
        return lax.psum_scatter(bucket, GROUP, scatter_dimension=0, tiled=True)

    if not plain:
        gelu_back = jax.vjp(lambda preact: jax.nn.gelu(preact, approximate=True), expanded)[1]
        reduce_in = jnp.concatenate(reduce_pieces, axis=1)
        expand_in = gelu_back(dot(reduce_in, reduce_part, 0, 0))[0].astype(bf16)
        ffn_part = dot(expand_in, expand_part, 1, 1).astype(bf16)
        ffn_part = by_piece(ffn_part)
        block_part = by_piece(dot(hidden, reduce_part, 1, 1))
    ff_out = expand_grads(ffn_pieces, expand_in, (lefts_other,) if plain else ())
    if plain:
        keep, send = reduce_grads(reduce_pieces, hidden, group_order)
        first_half = trade_bit(send, *group_steps()[0][:2])
        ff_grads = sum_group(ff_out)
    else:
        reduce_out = dot(reduce_in, hidden, 1, 0).astype(bf16)
        ff_grads = sum_group(jnp.concatenate([ff_out, reduce_out], axis=1))
        ff_grads, reduce_sums = ff_grads[:, :ff_width], ff_grads[:, ff_width:]
    ffn_grad = scatter_cp(ffn_part)
    texts = jnp.transpose(chosen.reshape(packs * TEXT_PAD, DT))
    if plain:
        attended, texts = gate((attended, texts), (ff_out,))
        attended_all = pieces_cp(attended)
        lefts = [lefts, trade_bit(lefts, "cp", 1), lefts_other, trade_bit(lefts_other, "cp", 1)]
    texts = pieces_cp(texts)
    if plain:
        (
            late_round,
            cross_raw_grad,
            mid_grad,
            mid_round,
            attended_grad,
            ck_grad,
            cv_grad,
            gain_pair,
        ) = middle_backward(
            piece_index,
            (
                ffn_grad,
                out_turned,
                late_t,
                mid_t,
                gain_columns_t,
                cross_queries,
                text_keys,
                text_values,
                out_cross,
                totals_cross,
                cross_raw,
            ),
            mid_weights,
            (ff_out,),
        )
        cout_in, cross_raw_grad, self_in = (
            reorder_cp(row_blocks(member)) for member in (late_round, cross_raw_grad, mid_round)
        )
    else:
        ffn_back = jax.vjp(norm_gain, late_stream, gain_rows[3])[1]
        late_part, gain_ffn = ffn_back(ffn_grad)
        late_grad = out_grad + late_part

        cout_in = column_blocks(late_grad.astype(bf16))
        cout_in = reorder_cp(cout_in)
        crossed_grad = heads_of(back_rows(cross_full, cout_in).astype(bf16))
        cq_grad, ck_grad, cv_grad = cross_backward(
            cross_queries, text_keys, text_values, crossed_grad, out_cross, totals_cross
        )
        cq_grad = cq_grad.astype(bf16).astype(f32)
        cross_raw_grad = rows_of(jax.vjp(head_norm, cross_raw)[1](cq_grad)[0].astype(bf16))
        cross_raw_grad = reorder_cp(row_blocks(cross_raw_grad))
        cross_norm_back = jax.vjp(norm_gain, mid_stream, gain_rows[2])[1]
        mid_part, gain_cross = cross_norm_back(
            back_sum(cross_raw_grad, query_full, 0)
        )
        mid_grad = late_grad + mid_part
        self_in = reorder_cp(column_blocks(mid_grad.astype(bf16)))
        attended_grad = back_rows(output_full, self_in).astype(bf16)
        normed_cross_t = jnp.transpose(normed_cross)
        cout_in = [jnp.transpose(member) for member in cout_in]
        self_in = [jnp.transpose(member) for member in self_in]
    if not plain:
        lefts = pieces_cp(jnp.stack([normed_cross_t, crossed]))
        attended_all = pieces_cp(attended)
    rights = exchange_cp(
        [
            jnp.stack([cross, late, mid])
            for cross, late, mid in zip(cross_raw_grad, cout_in, self_in)
        ]
    )
    if plain:
        attended_grad = lax.all_to_all(
            attended_grad.reshape(cp_count * sp_count, pairs_dev, HEAD, rows),
            HEAD_ORDER,
            split_axis=0,
            concat_axis=0,
            tiled=True,
        ).reshape(cp_count, sp_count, pairs_dev, HEAD, rows)
    else:
        attended_grad = by_heads(attended_grad)
    qkv_grad = self_backward(
        qkv,
        attended_grad,
        out_self,
        totals_self,
        first_cells,
        last_cells,
        valid_cells,
        turned,
        (first_half, *rights[1:]) if plain else (),
    )
    stamp = qkv_grad
    qkv_grad = from_heads(qkv_grad)
    if plain:
        block_part = reduce_parts(hidden, ff_gathered, stamp, cp_count)
        block_out = jnp.transpose((late_t + scatter_cp(block_part)).astype(bf16))
    else:
        block_out = (late_stream + scatter_cp(block_part)).astype(bf16)

    ck_grad = ck_grad.astype(bf16).astype(f32)
    text_raw_grad = jax.vjp(head_norm, text_raw)[1](ck_grad)[0].astype(bf16)
    paired_grad = jnp.stack(
        [
            text_raw_grad.reshape(packs, D, TEXT_PAD),
            cv_grad.reshape(packs, D, TEXT_PAD).astype(bf16),
        ],
        axis=1,
    ).reshape(packs, 2 * D, TEXT_PAD)
    paired_rows = jnp.swapaxes(paired_grad, 0, 1).reshape(2 * D, packs * TEXT_PAD)
    paired_rows = reorder_cp(row_blocks(paired_rows))
    pairs = exchange_cp(paired_rows)
    if plain:
        mid_out = mid_grads_bucket(
            lefts, attended_all, rights, texts, pairs, stamp, dp_count * sp_count
        )
    else:
        lefts = jnp.concatenate(lefts, axis=2)
        lefts = [lefts[0], lefts[1], jnp.concatenate(attended_all, axis=1)]
        rights = jnp.concatenate(rights, axis=2)
        pairs_grad = dot(
            jnp.concatenate(texts, axis=1), jnp.concatenate(pairs, axis=1), 1, 1
        )
        pairs_grad = jnp.pad(
            pairs_grad.astype(bf16).reshape(-1, group_text, 2 * width),
            ((0, 0), (0, group_rows - group_text), (0, 0)),
        ).reshape(D, 2 * width)
        mid_out = pack(
            [dot(lefts[k], rights[k], 1, 1).astype(bf16) for k in range(3)] + [pairs_grad]
        )
    mid_grads = sum_group(mid_out)
    if plain:
        near_null = jnp.take_along_axis(null_mask, near, axis=1)[0]
        near_null = near_null[jnp.arange(cp_count) ^ cp_index].astype(bf16)
        null_sum = sum(pairs[k].astype(f32) * near_null[k].astype(f32) for k in range(cp_count))
        caption_grad = dot(pairs_part, null_sum.astype(bf16), 1, 0)
    else:
        null_sum = jnp.einsum(
            "p,pnt->nt", own_null.astype(f32), paired_grad.astype(f32), precision=highest
        ).astype(bf16)
        caption_grad = sum(
            dot(part, block, 1, 0)
            for part, block in zip(pairs_full, reorder_cp(row_blocks(null_sum)))
        )
    caption_sum = caption_grad

    qkv_grad = after(qkv_grad, ff_grads)
    turn = functools.partial(turn_norm, cosine=cosine, sines=sines)
    query_raw_grad = jax.vjp(turn, query_raw)[1](qkv_grad[:, :, 0].astype(f32))[0].astype(bf16)
    key_raw_grad = jax.vjp(turn, key_raw)[1](qkv_grad[:, :, 1].astype(f32))[0].astype(bf16)
    projected_grad = jnp.stack([query_raw_grad, key_raw_grad, qkv_grad[:, :, 2]], axis=0)
    projected_grad = jnp.transpose(
        projected_grad.reshape(3, packs, group_heads, HEAD, cp_count, rows), (0, 2, 3, 4, 1, 5)
    ).reshape(3 * group_heads * HEAD, cp_count * held)
    if plain:
        normed_part = jnp.split(
            dot(input_part, projected_grad, 1, 0).astype(bf16), cp_count, axis=1
        )
    else:
        normed_part = dot(projected_grad, input_part, 0, 1).astype(bf16)
    self_input_grad = dot(normed_all, projected_grad, 1, 1).astype(bf16)
    if plain:
        mixed_grad, sums = start_backward(
            mixed_blocks,
            gain_columns_t,
            base_t,
            mid_grad,
            scatter_cp([normed_part[k] for k in range(cp_count)]),
        )
        shift_grads = sums[:, 2][None]
        came = trade_cp(mixed_grad)
        mixed_pieces = reorder_cp([came[k] for k in range(cp_count)])
        head_out = skip_grads_bucket(
            mixed_pieces,
            joined_all,
            self_input_grad,
            jnp.concatenate([sums[:, :2], gain_pair], axis=1),
        )
        joined_part = [dot(piece, skip_part, 0, 1).astype(bf16) for piece in mixed_pieces]
    else:
        normed_self_grad = scatter_cp(by_piece(normed_part))
        self_norm_back = jax.vjp(norm_gain, base_stream, gain_rows[1])[1]
        base_part, gain_self = self_norm_back(normed_self_grad)
        shift_grads = jnp.sum(normed_self_grad.reshape(packs, rows, D), axis=1)
        base_grad = mid_grad + base_part
        skip_norm_back = jax.vjp(norm_gain, mixed, gain_rows[0])[1]
        mixed_grad, gain_skip = skip_norm_back(base_grad)
        mixed_pieces = traded(column_blocks(mixed_grad.astype(bf16)))
        mixed_in = jnp.concatenate(mixed_pieces, axis=0)
        skip_out = dot(jnp.concatenate(joined_all, axis=0), mixed_in, 0, 0).astype(bf16)
        skip_out = skip_out.reshape(-1, 2, shard, width)
        head_out = pack(
            [
                skip_out[:, 0].reshape(D, width),
                skip_out[:, 1].reshape(D, width),
                self_input_grad,
            ]
        )
        joined_part = dot(mixed_in, skip_part, 1, 1).astype(bf16).reshape(cp_count, held, 2 * D)
        joined_part = [joined_part[k] for k in range(cp_count)]
    head_grads = sum_group(head_out)
    if plain:
        reduce_sums = scatter_group_halves(
            keep, send, first_half, (stamp, normed_part[0], head_out)
        )
    caption_grad = scatter_every(
        after(caption_sum, head_out).astype(bf16).reshape(-1, caption_rows, TEXT_PAD)
    )
    joined_grad = scatter_cp(joined_part)

    shift_grads = after(shift_grads, head_out)
    if not plain:
        gains_part = jnp.stack([gain_skip, gain_self, gain_cross, gain_ffn])
        gains_grad = scatter_every(jnp.swapaxes(gains_part.reshape(4, -1, gain_columns), 0, 1))
    shift_weight_grad = lax.dot_general(
        silu_blocks,
        send_every(shift_grads).reshape(-1, D),
        (((0,), (0,)), ((), ())),
        precision=highest,
        preferred_element_type=f32,
    )

    factor = all_packs * PACK / jnp.sum(lengths).astype(f32)

    def join_columns(bucket, widths):
        blocks = jnp.stack(send_cp(jnp.split(bucket, cp_count, axis=0)))
        start, parts = 0, []
        for size in widths:
            part = jnp.swapaxes(blocks[:, :, start : start + size], 0, 1)
            parts.append(part.astype(f32) * factor)
            start += size + -size % 128
        return parts

    def whole(part):
        return part.reshape(part.shape[0], -1)

    mid_grads = after(mid_grads, head_out)
    (expand_out,) = join_columns(after(ff_grads, head_out), (ff_width,))
    (reduce_out,) = join_columns(reduce_sums, (ff_width,))
    cross_query_out, cross_out_out, self_out_out = join_columns(
        mid_grads[:, : 3 * (width + -width % 128)], (width, width, width)
    )
    (pairs_out,) = join_columns(
        mid_grads[:group_text, 3 * (width + -width % 128) :], (2 * width,)
    )
    if plain:
        skip_out, input_out, gains_grad = finish_head(
            trade_cp(head_grads.reshape(cp_count, shard, -1)), factor
        )
        gains_grad = jnp.transpose(gains_grad)
    else:
        one, two, input_out = join_columns(head_grads, head_widths)
        skip_out = jnp.concatenate([whole(one), whole(two)], axis=0)
        input_out = restore_heads(whole(input_out))
        gains_grad = gains_grad * factor

    token_shape = (packs, rows, D)
    return (
        block_out.reshape(token_shape),
        (joined_grad[:, :D] * factor).astype(bf16).reshape(token_shape),
        (joined_grad[:, D:] * factor).astype(bf16).reshape(token_shape),
        skip_out,
        shift_weight_grad * factor,
        input_out,
        whole(self_out_out),
        whole(cross_query_out),
        whole(pairs_out),
        whole(cross_out_out),
        whole(expand_out),
        jnp.transpose(whole(reduce_out)),
        jnp.transpose(caption_grad)[:TEXT].astype(f32) * factor,
        gains_grad,
    )


def solution(mesh):
    token_spec = P("dp", ("sp", "cp"), None)
    by_rows = P(EVERY, None)
    by_columns = P(None, EVERY)
    return jax.shard_map(
        shards,
        mesh=mesh,
        in_specs=(
            token_spec,
            token_spec,
            P("dp", None, None),
            P("dp", "cp", None, None),
            P("dp", None),
            P(),
            token_spec,
            by_rows,
            by_rows,
            by_rows,
            by_rows,
            by_rows,
            by_rows,
            by_rows,
            by_rows,
            by_columns,
            by_columns,
            by_columns,
        ),
        out_specs=(
            token_spec,
            token_spec,
            token_spec,
            by_rows,
            by_rows,
            by_rows,
            by_rows,
            by_rows,
            by_rows,
            by_rows,
            by_rows,
            by_columns,
            by_columns,
            by_columns,
        ),
        check_vma=False,
    )
```

```python
import functools
import math

import jax
import jax.numpy as jnp
from jax import lax
from jax.experimental import pallas as pl
from jax.experimental.pallas import tpu as pltpu
from jax.sharding import PartitionSpec as P

D = 1408
HEADS = 16
HEAD = 88
DT = 1024
TEXT = 333
TEXT_PAD = 384
BIG_SIDE = 32
SMALL_SIDE = 16
PACK = 4096
IMGS = 16
CELL = 256
CELLS = PACK // CELL
SCALING = 1.0 / math.sqrt(HEAD)

epsilon = 1e-06
highest = lax.Precision.HIGHEST
bf16 = jnp.bfloat16
f32 = jnp.float32
GROUP = ("dp", "sp")
EVERY = ("dp", "sp", "cp")
HEAD_ORDER = ("cp", "sp")


def layer_norm(vector, axis=-1):
    centred = vector - jnp.mean(vector, axis=axis, keepdims=True)
    return centred * lax.rsqrt(jnp.mean(centred * centred, axis=axis, keepdims=True) + epsilon)


def head_norm(vector):
    return layer_norm(vector, -2)


def norm_gain(vector, gain):
    return layer_norm(vector) * gain


def dot(left, right, left_dim, right_dim):
    return lax.dot_general(
        left, right, (((left_dim,), (right_dim,)), ((), ())), preferred_element_type=f32
    )


def segment_info(lengths, positions):
    seg_ends = jnp.cumsum(lengths)
    starts = seg_ends - lengths
    present = lengths > 0
    slot_ids = jnp.arange(lengths.shape[0], dtype=jnp.int32)
    segment = jnp.sum(
        ((seg_ends[None, :] <= positions[:, None]) & present[None, :]).astype(jnp.int32), axis=1
    )
    onehot = segment[:, None] == slot_ids[None, :]
    seg_start = jnp.sum(jnp.where(onehot, starts[None, :], 0), axis=1)
    seg_size = jnp.sum(jnp.where(onehot, lengths[None, :], 0), axis=1)
    side_len = jnp.where(seg_size == BIG_SIDE * BIG_SIDE, BIG_SIDE, SMALL_SIDE).astype(jnp.int32)
    offset = positions - seg_start
    images = jnp.sum(present.astype(jnp.int32))
    return (segment, offset // side_len, offset % side_len, (segment < images).astype(f32))


def cell_ranges(lengths):
    positions = jnp.arange(CELLS, dtype=jnp.int32) * CELL
    seg_ends = jnp.cumsum(lengths)
    present = lengths > 0
    segment = jnp.sum(
        ((seg_ends[None, :] <= positions[:, None]) & present[None, :]).astype(jnp.int32), axis=1
    )
    same = segment[:, None] == segment[None, :]
    cells = jnp.arange(CELLS, dtype=jnp.int32)
    first = jnp.min(jnp.where(same, cells[None, :], CELLS), axis=1)
    last = jnp.max(jnp.where(same, cells[None, :] + 1, 0), axis=1)
    return (first, last, jnp.sum(lengths) // CELL)


def rope_tables(grid_row, grid_col):
    quarter = HEAD // 4
    frequency = jnp.exp(jnp.arange(quarter, dtype=f32) * (-math.log(10000.0) / quarter))
    angles = jnp.concatenate(
        [
            frequency[:, None] * grid_row.astype(f32)[None, :],
            frequency[:, None] * grid_col.astype(f32)[None, :],
        ],
        axis=0,
    )
    return (jnp.cos(angles), jnp.sin(angles))


def rotate(vector, cosine, sines):
    quarter = HEAD // 4
    one, two, three, four = (
        vector[..., k * quarter : (k + 1) * quarter, :] for k in range(4)
    )
    cos_row, cos_col = cosine[..., :quarter, :], cosine[..., quarter:, :]
    sin_row, sin_col = sines[..., :quarter, :], sines[..., quarter:, :]
    return jnp.concatenate(
        [
            one * cos_row - two * sin_row,
            one * sin_row + two * cos_row,
            three * cos_col - four * sin_col,
            three * sin_col + four * cos_col,
        ],
        axis=-2,
    )


def turn_norm(vector, cosine, sines):
    return rotate(head_norm(vector), cosine, sines)


def trade_bit(value, axis, bit):
    count = lax.axis_size(axis)
    return lax.ppermute(value, axis, [(k, k ^ bit) for k in range(count)])


def bits_of(axis):
    count = lax.axis_size(axis)
    return [1 << k for k in range(count.bit_length() - 1)]


def has_bit(axis, bit):
    return (lax.axis_index(axis) // bit) % 2 == 1


def pieces_cp(value):
    pieces = [value]
    found = {0: value}
    for bit in reversed(bits_of("cp")):
        for key in list(found):
            found[key | bit] = trade_bit(found[key], "cp", bit)
    pieces = [found[key] for key in range(lax.axis_size("cp"))]
    return pieces


def reorder_cp(pieces):
    for bit in bits_of("cp"):
        high = has_bit("cp", bit)
        pieces = [
            jnp.where(high, pieces[key ^ bit], pieces[key]) for key in range(len(pieces))
        ]
    return pieces


def gather_cp(value):
    return jnp.stack(reorder_cp(pieces_cp(value)))


def scatter_cp(pieces):
    pieces = [piece.astype(bf16) for piece in pieces]
    for bit in bits_of("cp"):
        pieces = [
            (
                pieces[key].astype(f32) + trade_bit(pieces[key + 1], "cp", bit).astype(f32)
            ).astype(f32 if len(pieces) == 2 else bf16)
            for key in range(0, len(pieces), 2)
        ]
    return pieces[0]


def after(value, *others):
    for other in others:
        value = value + (other[(0,) * other.ndim].astype(f32) * 0.0).astype(value.dtype)
    return value


def exchange_cp(pieces):
    count = lax.axis_size("cp")
    return [pieces[0]] + [
        lax.ppermute(pieces[key], "cp", [(k, k ^ key) for k in range(count)])
        for key in range(1, count)
    ]


def trade_cp(blocks):
    return lax.all_to_all(blocks, "cp", split_axis=0, concat_axis=0, tiled=True)


def send_cp(blocks):
    return reorder_cp(exchange_cp(reorder_cp(blocks)))


def group_steps():
    steps = [("dp", bit, bit * lax.axis_size("sp")) for bit in bits_of("dp")]
    return steps + [("sp", bit, bit) for bit in bits_of("sp")]


def group_differences():
    differences = [0]
    for _, _, weight in reversed(group_steps()):
        differences = differences + [key ^ weight for key in differences]
    return differences


def scatter_group_halves(keep, send, first, waits):
    for step, (axis, bit, _) in enumerate(group_steps()):
        came = (trade_bit(send, axis, bit) if step else first).astype(f32)
        total = after(keep.astype(f32) + came, waits[step]).astype(bf16)
        half = total.shape[0] // 2
        keep, send = total[:half], total[half:]
        if step == len(group_steps()) - 1:
            return total
    return None


def gather_every(value):
    dims = []
    for axis in ("dp", "sp", "cp"):
        for bit in reversed(bits_of(axis)):
            other = trade_bit(value, axis, bit)
            value = jnp.where(
                has_bit(axis, bit), jnp.stack([other, value]), jnp.stack([value, other])
            )
            dims.append((axis, bit))
    depth = len(dims)
    value = jnp.transpose(
        value, tuple(reversed(range(depth))) + tuple(range(depth, value.ndim))
    )
    return value.reshape((-1,) + value.shape[depth:])


def scatter_every(value):
    cp_count = lax.axis_size("cp")
    value = jnp.swapaxes(value.reshape((-1, cp_count) + value.shape[1:]), 0, 1)
    for axis in ("cp", "dp", "sp"):
        for bit in reversed(bits_of(axis)) if axis != "cp" else bits_of(axis):
            if axis == "cp":
                halves = value.reshape((-1, 2) + value.shape[1:])
                first, second = halves[:, 0], halves[:, 1]
            else:
                halves = value.reshape((2, -1) + value.shape[1:])
                first, second = halves[0], halves[1]
            high = has_bit(axis, bit)
            keep = jnp.where(high, second, first)
            send = jnp.where(high, first, second)
            value = keep + trade_bit(send, axis, bit)
        if axis == "cp":
            value = value[0]
    return value[0]


def send_every(value):
    count = lax.axis_size("dp") * lax.axis_size("sp") * lax.axis_size("cp")
    value = jnp.broadcast_to(value[None], (count,) + value.shape)
    return lax.all_to_all(value, EVERY, split_axis=0, concat_axis=0, tiled=True)


def sum_every(value):
    came = lax.all_to_all(value, EVERY, split_axis=0, concat_axis=0, tiled=True)
    return jnp.sum(came.astype(f32), axis=0)


def flip(block):
    if block.shape[0] % 128 == 0 and block.shape[1] % 128 == 0:
        return jnp.transpose(block)
    return jnp.transpose(block.astype(f32)).astype(bf16)


def kernel_dot(left, right, left_dim=1, right_dim=0):
    return lax.dot_general(
        left, right, (((left_dim,), (right_dim,)), ((), ())), preferred_element_type=f32
    )


def over_cells(first, last, step, carry):
    count = last - first
    fours = count // 4

    def four(turn, current):
        for k in range(4):
            current = step(first + turn * 4 + k, current)
        return current

    carry = lax.fori_loop(0, fours, four, carry)
    return lax.fori_loop(first + fours * 4, last, step, carry)


def self_forward_kernel(per_cell, first_ref, last_ref, turned_ref, qkv_ref, *refs):
    out_ref, total_ref, *sent_ref, keys = refs[-4:] if per_cell else refs[-3:]
    pair = pl.program_id(0)
    per = qkv_ref.shape[-1] // CELL

    def where(cell):
        lanes = ((cell % per) ^ turned_ref[0]) * CELL
        return cell // per, pl.ds(pl.multiple_of(lanes, CELL), CELL)

    def turn_keys(cell, carry):
        chunk, lanes = where(cell)
        keys[cell] = flip(qkv_ref[chunk, 0, 1, :, lanes])
        return carry

    lax.fori_loop(0, CELLS, turn_keys, 0)

    def one_cell(cell, carry):
        chunk, lanes = where(cell)
        query = qkv_ref[chunk, 0, 0, :, lanes]

        def step(other, current):
            summed, totals = current
            key_chunk, key_lanes = where(other)
            weights = jnp.exp(kernel_dot(keys[other], query) * SCALING)
            totals = totals + jnp.sum(weights, axis=0, keepdims=True)
            summed = summed + kernel_dot(
                qkv_ref[key_chunk, 0, 2, :, key_lanes], weights.astype(bf16)
            )
            return (summed, totals)

        summed, totals = over_cells(
            first_ref[pair, cell],
            last_ref[pair, cell],
            step,
            (jnp.zeros((HEAD, CELL), f32), jnp.zeros((1, CELL), f32)),
        )
        out = summed / totals
        out_ref[chunk, 0, :, lanes] = out
        if per_cell:
            sent_ref[0][cell % per, chunk, 0] = out.astype(bf16)
        total_ref[chunk, 0, :, lanes] = totals
        return carry

    lax.fori_loop(0, CELLS, one_cell, 0)


def self_backward_kernel(
    first_ref,
    last_ref,
    valid_ref,
    turned_ref,
    qkv_ref,
    grad_ref,
    out_ref,
    total_ref,
    *refs,
):
    result_ref, keys, values, key_sums, value_sums = refs[-5:]
    pair = pl.program_id(0)
    per = qkv_ref.shape[-1] // CELL

    def where(cell):
        lanes = ((cell % per) ^ turned_ref[0]) * CELL
        return cell // per, pl.ds(pl.multiple_of(lanes, CELL), CELL)

    def prepare(cell, carry):
        chunk, lanes = where(cell)
        keys[cell] = flip(qkv_ref[chunk, 0, 1, :, lanes])
        values[cell] = flip(qkv_ref[chunk, 0, 2, :, lanes])
        key_sums[cell] = jnp.zeros((HEAD, CELL), f32)
        value_sums[cell] = jnp.zeros((HEAD, CELL), f32)
        result_ref[chunk, 0, 0, :, lanes] = jnp.zeros((HEAD, CELL), bf16)
        return carry

    lax.fori_loop(0, CELLS, prepare, 0)

    def one_cell(cell, carry):
        chunk, lanes = where(cell)
        query = qkv_ref[chunk, 0, 0, :, lanes]
        if len(grad_ref.shape) == 5:
            grad = grad_ref[cell % per, chunk, 0].astype(f32)
        else:
            grad = grad_ref[chunk, 0, :, lanes].astype(f32)
        inverse = 1.0 / total_ref[chunk, 0, :, lanes]
        scaled = (grad * inverse).astype(bf16)
        total_grad = (
            -jnp.sum(grad * out_ref[chunk, 0, :, lanes], axis=0, keepdims=True) * inverse
        )

        def step(other, query_sum):
            key_chunk, key_lanes = where(other)
            weights = jnp.exp(kernel_dot(keys[other], query) * SCALING)
            weight_grad = kernel_dot(values[other], scaled)
            score_grad = (weights * (weight_grad + total_grad)).astype(bf16)
            value_sums[other] += kernel_dot(scaled, weights.astype(bf16), 1, 1)
            key_sums[other] += kernel_dot(query, score_grad, 1, 1)
            return query_sum + kernel_dot(qkv_ref[key_chunk, 0, 1, :, key_lanes], score_grad)

        query_sum = over_cells(
            first_ref[pair, cell], last_ref[pair, cell], step, jnp.zeros((HEAD, CELL), f32)
        )
        result_ref[chunk, 0, 0, :, lanes] = (query_sum * SCALING).astype(bf16)
        return carry

    lax.fori_loop(0, valid_ref[pair], one_cell, 0)

    def finish(cell, carry):
        chunk, lanes = where(cell)
        result_ref[chunk, 0, 1, :, lanes] = (key_sums[cell] * SCALING).astype(bf16)
        result_ref[chunk, 0, 2, :, lanes] = value_sums[cell].astype(bf16)
        return carry

    lax.fori_loop(0, CELLS, finish, 0)


def pair_spec(shape):
    block = (shape[0], 1) + shape[2:]
    rest = (0,) * (len(shape) - 2)
    return pl.BlockSpec(block, lambda pair, *_: (0, pair) + rest)


VMEM_WHOLE = pl.BlockSpec(memory_space=pltpu.VMEM)
SMEM_WHOLE = pl.BlockSpec(memory_space=pltpu.SMEM)
ANY_WHOLE = pl.BlockSpec(memory_space=pl.ANY)
VMEM_LIMIT = 48 * 1024 * 1024


def self_forward(qkv, first, last, turned, stamps, per_cell):
    chunks, pairs, _, _, columns = qkv.shape
    out_shape = (chunks, pairs, HEAD, columns)
    total_shape = (chunks, pairs, 1, columns)
    sent_shape = (columns // CELL, chunks, pairs, HEAD, CELL)
    sent_spec = pl.BlockSpec(
        sent_shape[:2] + (1,) + sent_shape[3:], lambda pair, *_: (0, 0, pair, 0, 0)
    )
    return pl.pallas_call(
        functools.partial(self_forward_kernel, per_cell),
        out_shape=(
            jax.ShapeDtypeStruct(out_shape, f32),
            jax.ShapeDtypeStruct(total_shape, f32),
        )
        + (jax.ShapeDtypeStruct(sent_shape, bf16),) * per_cell,
        grid_spec=pltpu.PrefetchScalarGridSpec(
            num_scalar_prefetch=3,
            grid=(pairs,),
            in_specs=[pair_spec(qkv.shape)] + [pl.BlockSpec(memory_space=pl.ANY)] * len(stamps),
            out_specs=[pair_spec(out_shape), pair_spec(total_shape)] + [sent_spec] * per_cell,
            scratch_shapes=[pltpu.VMEM((CELLS, CELL, HEAD), bf16)],
        ),
        compiler_params=pltpu.CompilerParams(vmem_limit_bytes=VMEM_LIMIT),
        cost_estimate=pl.CostEstimate(flops=10**10, bytes_accessed=8 << 20, transcendentals=0),
        name="self_forward",
    )(first, last, turned, qkv, *stamps)


def self_backward(qkv, grad, out, totals, first, last, valid, turned, stamps):
    pairs = qkv.shape[1]
    return pl.pallas_call(
        self_backward_kernel,
        out_shape=jax.ShapeDtypeStruct(qkv.shape, bf16),
        grid_spec=pltpu.PrefetchScalarGridSpec(
            num_scalar_prefetch=4,
            grid=(pairs,),
            in_specs=[
                pair_spec(qkv.shape),
                pair_spec(grad.shape)
                if grad.ndim == 4
                else pl.BlockSpec(
                    grad.shape[:2] + (1,) + grad.shape[3:], lambda pair, *_: (0, 0, pair, 0, 0)
                ),
                pair_spec(out.shape),
                pair_spec(totals.shape),
            ]
            + [pl.BlockSpec(memory_space=pl.ANY)] * len(stamps),
            out_specs=pair_spec(qkv.shape),
            scratch_shapes=[
                pltpu.VMEM((CELLS, CELL, HEAD), bf16),
                pltpu.VMEM((CELLS, CELL, HEAD), bf16),
                pltpu.VMEM((CELLS, HEAD, CELL), f32),
                pltpu.VMEM((CELLS, HEAD, CELL), f32),
            ],
        ),
        compiler_params=pltpu.CompilerParams(vmem_limit_bytes=VMEM_LIMIT),
        cost_estimate=pl.CostEstimate(flops=18 * 10**9, bytes_accessed=16 << 20, transcendentals=0),
        name="self_backward",
    )(first, last, valid, turned, qkv, grad, out, totals, *stamps)


def text_weights(key_block, query):
    scores = kernel_dot(flip(key_block), query) * SCALING
    present = lax.broadcasted_iota(jnp.int32, scores.shape, 0) < TEXT
    return jnp.where(present, jnp.exp(scores), 0.0)


def cross_forward_kernel(query_ref, key_ref, value_ref, out_ref, total_ref):
    for head in range(query_ref.shape[0]):
        weights = text_weights(key_ref[head], query_ref[head])
        totals = jnp.sum(weights, axis=0, keepdims=True)
        out_ref[head] = kernel_dot(value_ref[head], weights.astype(bf16)) / totals
        total_ref[head] = totals


def cross_backward_kernel(
    query_ref,
    key_ref,
    value_ref,
    grad_ref,
    out_ref,
    total_ref,
    query_grad_ref,
    key_grad_ref,
    value_grad_ref,
):
    for head in range(query_ref.shape[0]):
        query, keys = query_ref[head], key_ref[head]
        grad = grad_ref[head].astype(f32)
        inverse = 1.0 / total_ref[head]
        scaled = (grad * inverse).astype(bf16)
        total_grad = -jnp.sum(grad * out_ref[head], axis=0, keepdims=True) * inverse
        weights = text_weights(keys, query)
        weight_grad = kernel_dot(flip(value_ref[head]), scaled)
        score_grad = (weights * (weight_grad + total_grad)).astype(bf16)
        query_grad_ref[head] = kernel_dot(keys, score_grad) * SCALING
        key_grad_ref[head] = kernel_dot(query, score_grad, 1, 1) * SCALING
        value_grad_ref[head] = kernel_dot(scaled, weights.astype(bf16), 1, 1)


HEADS_STEP = 4


def head_spec(shape):
    return pl.BlockSpec((HEADS_STEP,) + shape[1:], lambda step: (step, 0, 0))


def cross_forward(queries, keys, values):
    count, _, rows = queries.shape
    out_shape = (count, HEAD, rows)
    total_shape = (count, 1, rows)
    return pl.pallas_call(
        cross_forward_kernel,
        out_shape=(
            jax.ShapeDtypeStruct(out_shape, f32),
            jax.ShapeDtypeStruct(total_shape, f32),
        ),
        grid=(count // HEADS_STEP,),
        in_specs=[head_spec(queries.shape), head_spec(keys.shape), head_spec(values.shape)],
        out_specs=[head_spec(out_shape), head_spec(total_shape)],
        compiler_params=pltpu.CompilerParams(vmem_limit_bytes=VMEM_LIMIT),
        name="cross_forward",
    )(queries, keys, values)


def cross_backward(queries, keys, values, grad, out, totals):
    inputs = (queries, keys, values, grad, out, totals)
    return pl.pallas_call(
        cross_backward_kernel,
        out_shape=(
            jax.ShapeDtypeStruct(queries.shape, f32),
            jax.ShapeDtypeStruct(keys.shape, f32),
            jax.ShapeDtypeStruct(values.shape, f32),
        ),
        grid=(queries.shape[0] // HEADS_STEP,),
        in_specs=[head_spec(member.shape) for member in inputs],
        out_specs=[head_spec(queries.shape), head_spec(keys.shape), head_spec(values.shape)],
        compiler_params=pltpu.CompilerParams(vmem_limit_bytes=VMEM_LIMIT),
        name="cross_backward",
    )(*inputs)


def unpack_kernel(width, text, bucket_ref, stamp_ref, *outs):
    whole = flip(bucket_ref[:, : 3 * width + -3 * width % 128])
    for part in range(3):
        outs[part][...] = whole[part * width : (part + 1) * width]
    rows = D * text // DT
    folded = 2 * width * DT // D
    for group in range(DT // text):
        block = bucket_ref[group * rows : (group + 1) * rows, 3 * width : 3 * width + folded]
        outs[3][group * text : (group + 1) * text, :] = unfold_rows(block)


def unpack_mid(bucket, width, text, stamp):
    part = jax.ShapeDtypeStruct((width, D), bf16)
    return pl.pallas_call(
        functools.partial(unpack_kernel, width, text),
        out_shape=(part, part, part, jax.ShapeDtypeStruct((DT, 2 * width), bf16)),
        in_specs=[VMEM_WHOLE, ANY_WHOLE],
        out_specs=[VMEM_WHOLE] * 4,
        compiler_params=pltpu.CompilerParams(vmem_limit_bytes=VMEM_LIMIT),
        cost_estimate=pl.CostEstimate(flops=1, bytes_accessed=12 << 20, transcendentals=0),
        name="unpack_mid",
    )(bucket, stamp)


def offer_kernel(count, which_ref, captions_ref, *refs):
    outputs = refs[-2 - count : -2]
    stage, sems = refs[-2:]
    copies = [
        pltpu.make_async_copy(captions_ref.at[0, which_ref[k]], stage.at[k], sems.at[k])
        for k in range(count)
    ]
    for copy in copies:
        copy.start()
    for k in range(count):
        copies[k].wait()
        rest = jnp.zeros((TEXT_PAD - TEXT, stage.shape[2]), f32)
        outputs[k][...] = jnp.concatenate([stage[k].astype(f32), rest], axis=0).astype(bf16)


def offer(which, captions, stamps):
    count = which.shape[0]
    shape = jax.ShapeDtypeStruct((TEXT_PAD, captions.shape[3]), bf16)
    return pl.pallas_call(
        functools.partial(offer_kernel, count),
        out_shape=(shape,) * count,
        in_specs=[SMEM_WHOLE] + [ANY_WHOLE] * (1 + len(stamps)),
        out_specs=[VMEM_WHOLE] * count,
        scratch_shapes=[
            pltpu.VMEM((count, TEXT, captions.shape[3]), bf16),
            pltpu.SemaphoreType.DMA((count,)),
        ],
        compiler_params=pltpu.CompilerParams(vmem_limit_bytes=VMEM_LIMIT),
        cost_estimate=pl.CostEstimate(flops=1, bytes_accessed=8 << 20, transcendentals=0),
        name="offer",
    )(which, captions, *stamps)


def gate(values, stamps):
    def kernel(*refs):
        pass

    return pl.pallas_call(
        kernel,
        out_shape=tuple(jax.ShapeDtypeStruct(value.shape, value.dtype) for value in values),
        in_specs=[ANY_WHOLE] * (len(values) + len(stamps)),
        out_specs=[ANY_WHOLE] * len(values),
        input_output_aliases={k: k for k in range(len(values))},
        cost_estimate=pl.CostEstimate(flops=1, bytes_accessed=1, transcendentals=0),
        name="gate",
    )(*values, *stamps)


def caption_kernel(count, null_ref, *refs):
    total = sum(refs[k][...].astype(f32) * null_ref[0, k] for k in range(count))
    refs[-1][...] = kernel_dot(refs[count][...], total.astype(bf16)).astype(bf16)


def caption_product(nulls, pairs, weight, stamp):
    count = len(pairs)
    return pl.pallas_call(
        functools.partial(caption_kernel, count),
        out_shape=jax.ShapeDtypeStruct((weight.shape[0], pairs[0].shape[1]), bf16),
        in_specs=[SMEM_WHOLE] + [VMEM_WHOLE] * (count + 1) + [ANY_WHOLE],
        out_specs=VMEM_WHOLE,
        compiler_params=pltpu.CompilerParams(vmem_limit_bytes=VMEM_LIMIT),
        cost_estimate=pl.CostEstimate(flops=10**9, bytes_accessed=5 << 20, transcendentals=0),
        name="caption_product",
    )(nulls, *pairs, weight, stamp)


def turn_over_kernel(value_ref, *refs):
    out_ref = refs[-1]
    out_ref[...] = flip(value_ref[...])


def turn_over(value, stamps):
    return pl.pallas_call(
        turn_over_kernel,
        out_shape=jax.ShapeDtypeStruct(value.shape[::-1], value.dtype),
        in_specs=[VMEM_WHOLE] + [ANY_WHOLE] * len(stamps),
        out_specs=VMEM_WHOLE,
        compiler_params=pltpu.CompilerParams(vmem_limit_bytes=VMEM_LIMIT),
        cost_estimate=pl.CostEstimate(flops=1, bytes_accessed=2 << 20, transcendentals=0),
        name="turn_over",
    )(value, *stamps)


def expand_grads_kernel(count, *refs):
    left = jnp.concatenate([ref[...] for ref in refs[:count]], axis=1)
    refs[-1][...] = kernel_dot(left, refs[count][...]).astype(bf16)


def expand_grads(pieces, right, stamps):
    steps = 2
    rows, width = D // steps, right.shape[1]
    return pl.pallas_call(
        functools.partial(expand_grads_kernel, len(pieces)),
        out_shape=jax.ShapeDtypeStruct((D, width), bf16),
        grid=(steps,),
        in_specs=[pl.BlockSpec((rows, pieces[0].shape[1]), lambda g: (g, 0))] * len(pieces)
        + [pl.BlockSpec(right.shape, lambda g: (0, 0))]
        + [ANY_WHOLE] * len(stamps),
        out_specs=pl.BlockSpec((rows, width), lambda g: (g, 0)),
        compiler_params=pltpu.CompilerParams(vmem_limit_bytes=VMEM_LIMIT),
        cost_estimate=pl.CostEstimate(
            flops=2 * D * right.shape[0] * width, bytes_accessed=12 << 20, transcendentals=0
        ),
        name="expand_grads",
    )(*pieces, right, *stamps)


def reduce_grads_kernel(count, group_ref, *refs):
    pieces, right_ref = refs[:count], refs[count]
    keep_ref, send_ref = refs[-2:]
    step, steps = pl.program_id(0), pl.num_programs(0)
    left = jnp.concatenate([ref[...] for ref in pieces], axis=1)
    product = kernel_dot(left, right_ref[...]).astype(bf16)

    @pl.when(step < steps // 2)
    def _():
        keep_ref[...] = product

    @pl.when(step >= steps // 2)
    def _():
        send_ref[...] = product


def reduce_grads(pieces, right, groups, stamps):
    steps, width = groups.shape[0], right.shape[1]
    rows, half = D // steps, steps // 2
    shape = jax.ShapeDtypeStruct((D // 2, width), bf16)
    return pl.pallas_call(
        functools.partial(reduce_grads_kernel, len(pieces)),
        out_shape=(shape, shape),
        grid_spec=pltpu.PrefetchScalarGridSpec(
            num_scalar_prefetch=1,
            grid=(steps,),
            in_specs=[
                pl.BlockSpec((rows, pieces[0].shape[1]), lambda g, group: (group[g], 0))
            ]
            * len(pieces)
            + [pl.BlockSpec(right.shape, lambda g, group: (0, 0))]
            + [ANY_WHOLE] * len(stamps),
            out_specs=[
                pl.BlockSpec((rows, width), lambda g, group: (jnp.minimum(g, half - 1), 0)),
                pl.BlockSpec((rows, width), lambda g, group: (jnp.maximum(g - half, 0), 0)),
            ],
        ),
        compiler_params=pltpu.CompilerParams(vmem_limit_bytes=VMEM_LIMIT),
        cost_estimate=pl.CostEstimate(
            flops=2 * D * right.shape[0] * width, bytes_accessed=12 << 20, transcendentals=0
        ),
        name="reduce_grads",
    )(groups, *pieces, right, *stamps)


def fold_rows(value):
    rows, columns = value.shape
    k, m = rows // 8, columns // 11
    over = value[:, 8 * m :]
    below = jnp.concatenate(
        [
            over[: 3 * k],
            over[3 * k : 6 * k],
            jnp.concatenate(
                [
                    over[6 * k :, : 2 * m],
                    jnp.concatenate([over[6 * k : 7 * k, 2 * m :], over[7 * k :, 2 * m :]], axis=1),
                ],
                axis=0,
            ),
        ],
        axis=1,
    )
    return jnp.concatenate([value[:, : 8 * m], below], axis=0)


def unfold_rows(value):
    rows, columns = value.shape
    k, m = rows // 11, columns // 8
    below = value[8 * k :]
    last = below[2 * k :, 6 * m :]
    over = jnp.concatenate(
        [
            below[:, : 3 * m],
            below[:, 3 * m : 6 * m],
            jnp.concatenate(
                [below[: 2 * k, 6 * m :], jnp.concatenate([last[:, :m], last[:, m:]], axis=0)],
                axis=1,
            ),
        ],
        axis=0,
    )
    return jnp.concatenate([value[: 8 * k], over], axis=1)


def mid_grads_kernel(count, width, groups, *refs):
    lefts, third, rights, texts, pairs = (refs[k * count : (k + 1) * count] for k in range(5))
    out_ref = refs[5 * count + 1]
    rows = out_ref.shape[0] // groups
    products = [
        sum(
            kernel_dot(left[part] if part < 2 else last[...], right[part], 1, 1)
            for left, last, right in zip(lefts, third, rights)
        )
        for part in range(3)
    ]
    text = texts[0].shape[0] // groups
    product = sum(kernel_dot(left[...], right[...], 1, 1) for left, right in zip(texts, pairs))
    for group in range(groups):
        here = slice(group * rows, (group + 1) * rows)
        block = [member[here] for member in products]
        block.append(fold_rows(product[group * text : (group + 1) * text]))
        rest = out_ref.shape[1] - sum(member.shape[1] for member in block)
        block.append(jnp.zeros((rows, rest), f32))
        out_ref[here, :] = jnp.concatenate(block, axis=1).astype(bf16)


def mid_grads_bucket(lefts, third, rights, texts, pairs, stamp, groups):
    count, width = len(lefts), rights[0].shape[1]
    steps = 2
    rows, text = D // steps, DT // steps
    columns = 3 * width + 2 * width * DT // D
    columns += -columns % 128
    return pl.pallas_call(
        functools.partial(mid_grads_kernel, count, width, groups // steps),
        out_shape=jax.ShapeDtypeStruct((D, columns), bf16),
        grid=(steps,),
        in_specs=[pl.BlockSpec((2, rows, lefts[0].shape[2]), lambda g: (0, g, 0))] * count
        + [pl.BlockSpec((rows, third[0].shape[1]), lambda g: (g, 0))] * count
        + [pl.BlockSpec(rights[0].shape, lambda g: (0, 0, 0))] * count
        + [pl.BlockSpec((text, texts[0].shape[1]), lambda g: (g, 0))] * count
        + [pl.BlockSpec(pairs[0].shape, lambda g: (0, 0))] * count
        + [ANY_WHOLE],
        out_specs=pl.BlockSpec((rows, columns), lambda g: (g, 0)),
        compiler_params=pltpu.CompilerParams(vmem_limit_bytes=VMEM_LIMIT),
        cost_estimate=pl.CostEstimate(
            flops=10 * D * D * width, bytes_accessed=24 << 20, transcendentals=0
        ),
        name="mid_grads",
    )(*lefts, *third, *rights, *texts, *pairs, stamp)


def skip_grads_kernel(count, width, *refs):
    rights, lefts = refs[:count], refs[count : 2 * count]
    input_ref, gain_ref, out_ref = refs[2 * count :]
    product = sum(kernel_dot(left[...], right[...]) for left, right in zip(lefts, rights))
    quarter = width // (2 * count)
    product = jnp.transpose(product)
    group_rows = count * quarter
    rest = out_ref.shape[1] - 5 * width - gain_ref.shape[1]
    for group in range(product.shape[0] // width):
        rows = slice(group * group_rows, (group + 1) * group_rows)
        halves = [
            jnp.concatenate(
                [
                    product[start : start + quarter]
                    for start in (
                        group * width + (2 * k + part) * quarter for k in range(count)
                    )
                ],
                axis=0,
            )
            for part in range(2)
        ]
        block = [input_ref[rows, :].astype(f32), *halves, gain_ref[rows, :]]
        block.append(jnp.zeros((group_rows, rest), f32))
        out_ref[rows, :] = jnp.concatenate(block, axis=1).astype(bf16)


def skip_grads_bucket(lefts, rights, inputs, gains):
    count, width = len(lefts), lefts[0].shape[0]
    columns = 5 * width + -5 * width % 128
    return pl.pallas_call(
        functools.partial(skip_grads_kernel, count, width),
        out_shape=jax.ShapeDtypeStruct((D, columns), bf16),
        grid=(2,),
        in_specs=[pl.BlockSpec((rights[0].shape[0], D), lambda g: (0, g))] * count
        + [pl.BlockSpec(lefts[0].shape, lambda g: (0, 0))] * count
        + [pl.BlockSpec((D // 2, member.shape[1]), lambda g: (g, 0)) for member in (inputs, gains)],
        out_specs=pl.BlockSpec((D // 2, columns), lambda g: (g, 0)),
        compiler_params=pltpu.CompilerParams(vmem_limit_bytes=VMEM_LIMIT),
        cost_estimate=pl.CostEstimate(
            flops=4 * D * width * count * 256, bytes_accessed=16 << 20, transcendentals=0
        ),
        name="skip_grads",
    )(*rights, *lefts, inputs, gains)


def finish_kernel(factor_ref, blocks_ref, skip_ref, input_ref, gain_ref):
    factor = factor_ref[0, 0]
    count, shard, _ = blocks_ref.shape
    width = skip_ref.shape[1] // count
    blocks = [blocks_ref[k].astype(f32) * factor for k in range(count)]
    for part in range(2):
        skip_ref[part * shard : (part + 1) * shard, :] = jnp.concatenate(
            [block[:, (3 + part) * width : (4 + part) * width] for block in blocks], axis=1
        )
    gain_ref[...] = sum(block[:, 5 * width : 5 * width + 4] for block in blocks)
    input_ref[...] = jnp.concatenate(
        [
            block[:, part * width : (part + 1) * width]
            for part in range(3)
            for block in blocks
        ],
        axis=1,
    )


def finish_head(blocks, factor):
    count, shard, _ = blocks.shape
    return pl.pallas_call(
        finish_kernel,
        out_shape=(
            jax.ShapeDtypeStruct((2 * shard, D), f32),
            jax.ShapeDtypeStruct((shard, 3 * D), f32),
            jax.ShapeDtypeStruct((shard, 4), f32),
        ),
        in_specs=[SMEM_WHOLE, VMEM_WHOLE],
        out_specs=[VMEM_WHOLE] * 3,
        compiler_params=pltpu.CompilerParams(vmem_limit_bytes=VMEM_LIMIT),
        cost_estimate=pl.CostEstimate(flops=1, bytes_accessed=2 << 20, transcendentals=0),
        name="finish_head",
    )(factor.reshape(1, 1), blocks)


def norm_rows(value):
    centred = value - jnp.mean(value, axis=0, keepdims=True)
    scale = lax.rsqrt(jnp.mean(centred * centred, axis=0, keepdims=True) + epsilon)
    return centred * scale, scale


def norm_rows_back(normed, scale, grad):
    return scale * (
        grad
        - jnp.mean(grad, axis=0, keepdims=True)
        - normed * jnp.mean(grad * normed, axis=0, keepdims=True)
    )


def fetch(sources, targets, sems, base):
    copies = [
        pltpu.make_async_copy(source, target, sems.at[base + k])
        for k, (source, target) in enumerate(zip(sources, targets))
    ]
    for copy in copies:
        copy.start()
    return copies


def mix_kernel(count, *refs):
    index_ref, bucket_ref = refs[:2]
    pieces = refs[2 : 2 + count]
    out_ref, weight = refs[-2:]
    width = weight.shape[1]
    half = width // 2
    for group in range(weight.shape[0] // width):
        for part in range(2):
            start = group * width + part * half
            weight[start : start + half, :] = bucket_ref[
                group * half : (group + 1) * half, (3 + part) * width : (4 + part) * width
            ]
    for piece in range(count):
        out_ref[piece ^ index_ref[0]] = kernel_dot(pieces[piece][...], weight[...]).astype(bf16)


def mix(index, bucket, pieces, width, stamps):
    count, rows = len(pieces), pieces[0].shape[0]
    return pl.pallas_call(
        functools.partial(mix_kernel, count),
        out_shape=jax.ShapeDtypeStruct((count, rows, width), bf16),
        grid=(1,),
        in_specs=[SMEM_WHOLE, pl.BlockSpec(bucket.shape, lambda g: (0, 0))]
        + [pl.BlockSpec(pieces[0].shape, lambda g: (0, 0))] * count
        + [ANY_WHOLE] * len(stamps),
        out_specs=pl.BlockSpec((count, rows, width), lambda g: (0, 0, 0)),
        scratch_shapes=[pltpu.VMEM((2 * D, width), bf16)],
        compiler_params=pltpu.CompilerParams(vmem_limit_bytes=VMEM_LIMIT),
        cost_estimate=pl.CostEstimate(
            flops=4 * D * width * count * rows, bytes_accessed=8 << 20, transcendentals=0
        ),
        name="mix",
    )(index, bucket, *pieces, *stamps)


def mixed_rows(blocks_ref, stage):
    width = blocks_ref.shape[2]
    for block in range(blocks_ref.shape[0]):
        turned = jnp.transpose(blocks_ref[block].astype(f32))
        stage[block * width : (block + 1) * width, :] = turned
    return stage[...]


def start_kernel(blocks_ref, gain_ref, shift_ref, base_ref, normed_ref, stage):
    base = norm_rows(mixed_rows(blocks_ref, stage))[0] * gain_ref[:, 0:1]
    base_ref[...] = base
    normed = norm_rows(base)[0] * gain_ref[:, 1:2] + shift_ref[...]
    normed_ref[...] = normed.astype(bf16)


def start_forward(blocks, gains, shift):
    tokens = blocks.shape[1]
    return pl.pallas_call(
        start_kernel,
        out_shape=(
            jax.ShapeDtypeStruct((D, tokens), f32),
            jax.ShapeDtypeStruct((D, tokens), bf16),
        ),
        in_specs=[VMEM_WHOLE] * 3,
        out_specs=[VMEM_WHOLE] * 2,
        scratch_shapes=[pltpu.VMEM((D, tokens), f32)],
        compiler_params=pltpu.CompilerParams(vmem_limit_bytes=VMEM_LIMIT),
        cost_estimate=pl.CostEstimate(flops=1, bytes_accessed=8 << 20, transcendentals=0),
        name="start_forward",
    )(blocks, gains, shift)


def start_back_kernel(
    blocks_ref, gain_ref, base_ref, mid_grad_ref, grad_ref, out_ref, sums_ref, stage
):
    normed, scale = norm_rows(base_ref[...])
    grad = grad_ref[...]
    sums_ref[:, 1:2] = jnp.sum(grad * normed, axis=1, keepdims=True)
    sums_ref[:, 2:3] = jnp.sum(grad, axis=1, keepdims=True)
    base_grad = mid_grad_ref[...] + norm_rows_back(normed, scale, grad * gain_ref[:, 1:2])
    normed, scale = norm_rows(mixed_rows(blocks_ref, stage))
    sums_ref[:, 0:1] = jnp.sum(base_grad * normed, axis=1, keepdims=True)
    mixed_grad = norm_rows_back(normed, scale, base_grad * gain_ref[:, 0:1]).astype(bf16)
    width = out_ref.shape[1]
    for block in range(out_ref.shape[0]):
        out_ref[block] = mixed_grad[block * width : (block + 1) * width]


def start_backward(blocks, gains, base, mid_grad, grad):
    count, tokens, width = blocks.shape
    return pl.pallas_call(
        start_back_kernel,
        out_shape=(
            jax.ShapeDtypeStruct((count, width, tokens), bf16),
            jax.ShapeDtypeStruct((D, 3), f32),
        ),
        in_specs=[VMEM_WHOLE] * 5,
        out_specs=[VMEM_WHOLE] * 2,
        scratch_shapes=[pltpu.VMEM((D, tokens), f32)],
        compiler_params=pltpu.CompilerParams(vmem_limit_bytes=VMEM_LIMIT),
        cost_estimate=pl.CostEstimate(flops=1, bytes_accessed=10 << 20, transcendentals=0),
        name="start_backward",
    )(blocks, gains, base, mid_grad, grad)


def middle_forward_kernel(count, *refs):
    index_ref, attended_ref, base_ref, gain_ref, key_ref, value_ref = refs[:6]
    sources = refs[6 : 6 + 3 * count]
    (
        mid_ref,
        late_ref,
        lefts_ref,
        raw_ref,
        query_ref,
        out_ref,
        total_ref,
        ffn_ref,
    ) = refs[6 + 3 * count : 14 + 3 * count]
    weights, sems = refs[14 + 3 * count :]
    copies = fetch(sources, [weights.at[k] for k in range(3 * count)], sems, 0)
    index = index_ref[0]
    width = D // count
    heads = HEADS // count

    def rows_of_piece(piece):
        return pl.ds(pl.multiple_of((piece ^ index) * width, 32), width)

    attended = attended_ref[...]
    for piece in range(count):
        copies[piece].wait()
        rows = rows_of_piece(piece)
        mid_ref[rows, :] = base_ref[rows, :] + kernel_dot(weights[piece], attended)
    normed = (norm_rows(mid_ref[...])[0] * gain_ref[:, 2:3]).astype(bf16)
    lefts_ref[0] = normed
    for piece in range(count):
        copies[count + piece].wait()
        product = kernel_dot(weights[count + piece], normed)
        for head in range(heads):
            raw_ref[(piece ^ index) * heads + head] = product[head * HEAD : (head + 1) * HEAD]
    for head in range(HEADS):
        query = norm_rows(raw_ref[head])[0].astype(bf16)
        query_ref[head] = query
        attention = text_weights(key_ref[head], query)
        totals = jnp.sum(attention, axis=0, keepdims=True)
        out = kernel_dot(value_ref[head], attention.astype(bf16)) / totals
        out_ref[head * HEAD : (head + 1) * HEAD, :] = out
        total_ref[head] = totals
    crossed = out_ref[...].astype(bf16)
    lefts_ref[1] = crossed
    for piece in range(count):
        copies[2 * count + piece].wait()
        rows = rows_of_piece(piece)
        late_ref[rows, :] = mid_ref[rows, :] + kernel_dot(weights[2 * count + piece], crossed)
    ffn_ref[...] = (norm_rows(late_ref[...])[0] * gain_ref[:, 3:4]).astype(bf16)


def middle_forward(index, attended, base, gains, keys, values, weights):
    count = len(weights) // 3
    tokens = attended.shape[1]
    stream = jax.ShapeDtypeStruct((D, tokens), f32)
    by_head = (HEADS, HEAD, tokens)
    return pl.pallas_call(
        functools.partial(middle_forward_kernel, count),
        out_shape=(
            stream,
            stream,
            jax.ShapeDtypeStruct((2, D, tokens), bf16),
            jax.ShapeDtypeStruct(by_head, f32),
            jax.ShapeDtypeStruct(by_head, bf16),
            stream,
            jax.ShapeDtypeStruct((HEADS, 1, tokens), f32),
            jax.ShapeDtypeStruct((D, tokens), bf16),
        ),
        in_specs=[SMEM_WHOLE] + [VMEM_WHOLE] * 5 + [ANY_WHOLE] * (3 * count),
        out_specs=[VMEM_WHOLE] * 8,
        scratch_shapes=[
            pltpu.VMEM((3 * count, D // count, D), bf16),
            pltpu.SemaphoreType.DMA((3 * count,)),
        ],
        compiler_params=pltpu.CompilerParams(vmem_limit_bytes=VMEM_LIMIT),
        cost_estimate=pl.CostEstimate(
            flops=10 * D * D * tokens, bytes_accessed=24 << 20, transcendentals=0
        ),
        name="middle_forward",
    )(index, attended, base, gains, keys, values, *weights)


def middle_backward_kernel(count, stamps, *refs):
    (
        index_ref,
        ffn_grad_ref,
        out_grad_ref,
        late_ref,
        mid_ref,
        gain_ref,
        query_ref,
        key_ref,
        value_ref,
        out_ref,
        total_ref,
        raw_ref,
        text_ref,
    ) = refs[:13]
    sources = refs[13 : 13 + 3 * count]
    (
        mid_grad_ref,
        attended_grad_ref,
        rights_ref,
        pairs_ref,
        gain_grad_ref,
    ) = refs[13 + stamps + 3 * count : 18 + stamps + 3 * count]
    weights, stage, rounded, sems = refs[18 + stamps + 3 * count :]
    order = [2, 1, 0]
    copies = []
    for place in order:
        copies += fetch(
            sources[place * count : (place + 1) * count],
            [weights.at[place * count + k] for k in range(count)],
            sems,
            place * count,
        )
    index = index_ref[0]
    width = D // count

    def through(place, turn, part):
        total = 0.0
        for piece in range(count):
            copies[turn * count + piece].wait()
            rows = pl.ds(pl.multiple_of((piece ^ index) * width, 32), width)
            value = rounded[rows, :]
            rights_ref[piece, part] = value
            total = total + kernel_dot(flip(value), weights[place * count + piece])
        return jnp.transpose(total)

    normed, scale = norm_rows(late_ref[...])
    grad = ffn_grad_ref[...]
    gain_grad_ref[:, 1:2] = jnp.sum(grad * normed, axis=1, keepdims=True)
    late_grad = out_grad_ref[...].astype(f32) + norm_rows_back(
        normed, scale, grad * gain_ref[:, 3:4]
    )
    mid_grad_ref[...] = late_grad
    rounded[...] = late_grad.astype(bf16)
    stage[...] = through(2, 0, 1).astype(bf16).astype(f32)
    key_grads, value_grads = [], []
    for head in range(HEADS):
        rows = slice(head * HEAD, (head + 1) * HEAD)
        query, keys = query_ref[head], key_ref[head]
        grad = stage[rows, :]
        inverse = 1.0 / total_ref[head]
        scaled = (grad * inverse).astype(bf16)
        total_grad = -jnp.sum(grad * out_ref[rows, :], axis=0, keepdims=True) * inverse
        attention = text_weights(keys, query)
        weight_grad = kernel_dot(flip(value_ref[head]), scaled)
        score_grad = (attention * (weight_grad + total_grad)).astype(bf16)
        query_grad = (kernel_dot(keys, score_grad) * SCALING).astype(bf16).astype(f32)
        key_grad = (kernel_dot(query, score_grad, 1, 1) * SCALING).astype(bf16).astype(f32)
        key_grads.append(norm_rows_back(*norm_rows(text_ref[head]), key_grad))
        value_grads.append(kernel_dot(scaled, attention.astype(bf16), 1, 1))
        normed, scale = norm_rows(raw_ref[head])
        stage[rows, :] = norm_rows_back(normed, scale, query_grad)
    per = 2 * HEADS // count
    grads = key_grads + value_grads
    for part in range(count):
        block = jnp.concatenate(grads[part * per : (part + 1) * per], axis=0)
        pairs_ref[part ^ index] = block.astype(bf16)
    rounded[...] = stage[...].astype(bf16)
    grad = through(1, 1, 0)
    normed, scale = norm_rows(mid_ref[...])
    gain_grad_ref[:, 0:1] = jnp.sum(grad * normed, axis=1, keepdims=True)
    mid_grad = mid_grad_ref[...] + norm_rows_back(normed, scale, grad * gain_ref[:, 2:3])
    mid_grad_ref[...] = mid_grad
    rounded[...] = mid_grad.astype(bf16)
    attended_grad_ref[...] = through(0, 2, 2).astype(bf16)


def middle_backward(index, arrays, weights, stamps):
    count = len(weights) // 3
    tokens = arrays[0].shape[1]
    rounded = jax.ShapeDtypeStruct((D, tokens), bf16)
    width = D // count
    return pl.pallas_call(
        functools.partial(middle_backward_kernel, count, len(stamps)),
        out_shape=(
            jax.ShapeDtypeStruct((D, tokens), f32),
            rounded,
            jax.ShapeDtypeStruct((count, 3, width, tokens), bf16),
            jax.ShapeDtypeStruct((count, 2 * width, TEXT_PAD), bf16),
            jax.ShapeDtypeStruct((D, 2), f32),
        ),
        in_specs=[SMEM_WHOLE]
        + [VMEM_WHOLE] * 12
        + [ANY_WHOLE] * (3 * count + len(stamps)),
        out_specs=[VMEM_WHOLE] * 5,
        scratch_shapes=[
            pltpu.VMEM((3 * count, D // count, D), bf16),
            pltpu.VMEM((D, tokens), f32),
            pltpu.VMEM((D, tokens), bf16),
            pltpu.SemaphoreType.DMA((3 * count,)),
        ],
        compiler_params=pltpu.CompilerParams(vmem_limit_bytes=VMEM_LIMIT),
        cost_estimate=pl.CostEstimate(
            flops=14 * D * D * tokens, bytes_accessed=30 << 20, transcendentals=0
        ),
        name="middle_backward",
    )(index, *arrays, *weights, *stamps)


GELU_SCALE = math.sqrt(2.0 / math.pi)


def ffn_kernel(count, stamps, *refs):
    inputs, grads = refs[:count], refs[count : 2 * count]
    expand_ref, reduce_ref = refs[2 * count : 2 * count + 2]
    hidden_ref, expand_in_ref, *outputs = refs[2 * count + 2 + stamps :]
    back_refs = outputs[:count]
    value_sc, grad_sc, back_sc = outputs[count:]
    step, steps = pl.program_id(0), pl.num_programs(0)
    tokens = inputs[0].shape[1]

    @pl.when(step == 0)
    def _():
        for piece in range(count):
            rows = slice(piece * tokens, (piece + 1) * tokens)
            value_sc[rows, :] = flip(inputs[piece][...])
            grad_sc[rows, :] = flip(grads[piece][...])

    weight = expand_ref[...]
    for half in range(2):
        rows = slice(half * count * tokens // 2, (half + 1) * count * tokens // 2)
        plain = kernel_dot(value_sc[rows, :], weight)
        square = plain * plain
        curve = jnp.tanh(plain * (GELU_SCALE + (GELU_SCALE * 0.044715) * square))
        above, half_plain = 1.0 + curve, 0.5 * plain
        hidden_ref[rows, :] = (half_plain * above).astype(bf16)
        steep = GELU_SCALE + (GELU_SCALE * 3.0 * 0.044715) * square
        slope = above * (0.5 + half_plain * (1.0 - curve) * steep)
        expand_in_ref[rows, :] = (kernel_dot(grad_sc[rows, :], reduce_ref[...]) * slope).astype(
            bf16
        )
    for piece in range(count):
        rows = slice(piece * tokens, (piece + 1) * tokens)
        part = kernel_dot(weight, expand_in_ref[rows, :], 1, 1)

        @pl.when(step == 0)
        def _():
            back_sc[piece] = part

        @pl.when((step > 0) & (step < steps - 1))
        def _():
            back_sc[piece] += part

        @pl.when(step == steps - 1)
        def _():
            back_refs[piece][...] = (back_sc[piece] + part).astype(bf16)


def feed_forward(inputs, grads, bucket, stamps):
    count = len(inputs)
    tokens, width = inputs[0].shape[1], bucket.shape[1] // 2
    steps = 3
    chunk = width // steps
    by_hidden = jax.ShapeDtypeStruct((count * tokens, width), bf16)
    by_piece = jax.ShapeDtypeStruct((D, tokens), bf16)
    whole = pl.BlockSpec((D, tokens), lambda step: (0, 0))
    hidden_spec = pl.BlockSpec((count * tokens, chunk), lambda step: (0, step))
    return pl.pallas_call(
        functools.partial(ffn_kernel, count, len(stamps)),
        out_shape=(by_hidden, by_hidden) + (by_piece,) * count,
        grid=(steps,),
        in_specs=[whole] * (2 * count)
        + [pl.BlockSpec((D, chunk), lambda step, k=k: (0, k * steps + step)) for k in range(2)]
        + [ANY_WHOLE] * len(stamps),
        out_specs=[hidden_spec, hidden_spec] + [whole] * count,
        scratch_shapes=[
            pltpu.VMEM((count * tokens, D), bf16),
            pltpu.VMEM((count * tokens, D), bf16),
            pltpu.VMEM((count, D, tokens), f32),
        ],
        compiler_params=pltpu.CompilerParams(vmem_limit_bytes=VMEM_LIMIT),
        cost_estimate=pl.CostEstimate(
            flops=6 * D * count * tokens * width,
            bytes_accessed=24 << 20,
            transcendentals=count * tokens * width,
        ),
        name="feed_forward",
    )(*inputs, *grads, bucket, bucket, *stamps)


def reduce_kernel(count, hidden_ref, reduce_ref, stamp_ref, *outputs):
    tokens = hidden_ref.shape[0] // count
    for piece in range(count):
        hidden = hidden_ref[piece * tokens : (piece + 1) * tokens, :]
        outputs[piece][...] = kernel_dot(reduce_ref[...], hidden, 1, 1).astype(bf16)


def reduce_parts(hidden, bucket, stamp, count):
    width = hidden.shape[1]
    tokens = hidden.shape[0] // count
    by_piece = jax.ShapeDtypeStruct((D, tokens), bf16)
    whole = pl.BlockSpec((D, tokens), lambda step: (0, 0))
    return pl.pallas_call(
        functools.partial(reduce_kernel, count),
        out_shape=(by_piece,) * count,
        grid=(1,),
        in_specs=[
            pl.BlockSpec(hidden.shape, lambda step: (0, 0)),
            pl.BlockSpec((D, width), lambda step: (0, 1)),
            ANY_WHOLE,
        ],
        out_specs=[whole] * count,
        compiler_params=pltpu.CompilerParams(vmem_limit_bytes=VMEM_LIMIT),
        cost_estimate=pl.CostEstimate(
            flops=2 * D * count * tokens * width, bytes_accessed=12 << 20, transcendentals=0
        ),
        name="reduce_parts",
    )(hidden, bucket, stamp)


def project_kernel(count, heads, *refs):
    values = refs[:count]
    weights = refs[count : count + 3]
    cos_ref, sin_ref = refs[count + 3 : count + 5]
    qkv_ref, raw_ref = refs[-2:]
    quarter = HEAD // 4
    rows = values[0].shape[1]
    for piece in range(count):
        lanes = pl.ds(piece * rows, rows)
        value = flip(values[piece][...])
        product = jnp.concatenate(
            [jnp.transpose(kernel_dot(value, weight[...])) for weight in weights], axis=0
        )
        cosine, sines = cos_ref[:, lanes], sin_ref[:, lanes]
        cos_row, cos_col = cosine[:quarter], cosine[quarter:]
        sin_row, sin_col = sines[:quarter], sines[quarter:]
        for part in range(3):
            for head in range(heads):
                start = (part * heads + head) * HEAD
                raw = product[start : start + HEAD]
                if part == 2:
                    qkv_ref[head, part, :, lanes] = raw.astype(bf16)
                    continue
                raw_ref[head, part, :, lanes] = raw
                normed = head_norm(raw)
                one, two, three, four = (
                    normed[k * quarter : (k + 1) * quarter] for k in range(4)
                )
                turned = jnp.concatenate(
                    [
                        one * cos_row - two * sin_row,
                        one * sin_row + two * cos_row,
                        three * cos_col - four * sin_col,
                        three * sin_col + four * cos_col,
                    ],
                    axis=0,
                )
                qkv_ref[head, part, :, lanes] = turned.astype(bf16)


def project(values, bucket, offset, heads, cosine, sines, stamps):
    count, rows = len(values), values[0].shape[1]
    third = (3 * heads * HEAD + 383) // 384 * 128
    columns = count * rows
    full = [pl.BlockSpec(member.shape, lambda g: (0, 0)) for member in (*values, cosine, sines)]
    return pl.pallas_call(
        functools.partial(project_kernel, count, heads),
        out_shape=(
            jax.ShapeDtypeStruct((heads, 3, HEAD, columns), bf16),
            jax.ShapeDtypeStruct((heads, 2, HEAD, columns), f32),
        ),
        grid=(1,),
        in_specs=full[:count]
        + [
            pl.BlockSpec((D, third), lambda g, k=k: (0, offset // third + k)) for k in range(3)
        ]
        + full[count:]
        + [ANY_WHOLE] * len(stamps),
        out_specs=[
            pl.BlockSpec((heads, 3, HEAD, columns), lambda g: (0, 0, 0, 0)),
            pl.BlockSpec((heads, 2, HEAD, columns), lambda g: (0, 0, 0, 0)),
        ],
        compiler_params=pltpu.CompilerParams(vmem_limit_bytes=VMEM_LIMIT),
        cost_estimate=pl.CostEstimate(
            flops=6 * columns * D * heads * HEAD, bytes_accessed=12 << 20, transcendentals=0
        ),
        name="project",
    )(*values, bucket, bucket, bucket, cosine, sines, *stamps)


def shards(
    tokens,
    skip_in,
    timestep,
    captions,
    null_mask,
    lengths,
    cotangent,
    skip_weight,
    shift_weight,
    self_input,
    self_output,
    cross_query,
    cross_pairs,
    cross_output,
    expand_weight,
    reduce_weight,
    null_caption,
    norm_gains,
):
    sp_count, cp_count = lax.axis_size("sp"), lax.axis_size("cp")
    dp_count = lax.axis_size("dp")
    dp_index, sp_index, cp_index = (lax.axis_index(name) for name in EVERY)
    place = (dp_index * sp_count + sp_index) * cp_count + cp_index
    packs, rows = tokens.shape[0], tokens.shape[1]
    held = packs * rows
    chunk = cp_count * rows
    group_heads = HEADS // cp_count
    pairs_dev = packs * group_heads // sp_count
    all_packs = lengths.shape[0]

    def lanes(value):
        spare = -value.shape[-1] % 128
        return jnp.pad(value, [(0, 0)] * (value.ndim - 1) + [(0, spare)])

    def split_columns(weight):
        columns = weight.shape[1] // cp_count
        blocks = jnp.swapaxes(weight.reshape(weight.shape[0], cp_count, columns), 0, 1)
        return trade_cp(blocks).reshape(cp_count * weight.shape[0], columns)

    def send_columns(weights):
        blocks = [
            jnp.concatenate(
                [jnp.split(weight, cp_count, axis=1)[k] for weight in weights], axis=1
            )
            for k in range(cp_count)
        ]
        return jnp.concatenate(send_cp(blocks), axis=0)

    def order_heads(weight):
        split = weight.reshape(weight.shape[0], 3, cp_count, -1)
        return jnp.swapaxes(split, 1, 2).reshape(weight.shape)

    def restore_heads(weight):
        split = weight.reshape(weight.shape[0], cp_count, 3, -1)
        return jnp.swapaxes(split, 1, 2).reshape(weight.shape)

    def pack(parts):
        return jnp.concatenate([lanes(part) for part in parts], axis=1)

    def unpack(bucket, widths):
        start, parts = 0, []
        for width in widths:
            parts.append(bucket[:, start : start + width])
            start += width + -width % 128
        return parts

    width = D // cp_count
    ff_width = expand_weight.shape[1] // cp_count
    group_rows = cp_count * self_output.shape[0]
    group_text = cp_count * cross_pairs.shape[0]
    head_widths = (width, width, 3 * width)
    mid_widths = (width, width, width, 2 * width)

    def gather_group(bucket):
        return lax.all_gather(bucket, GROUP, axis=0, tiled=True)

    skip_cols = split_columns(skip_weight)
    plain = rows == CELL and packs == 1 and group_rows % 16 == 0
    gain_columns = norm_gains.shape[1]
    shard = self_output.shape[0]
    fill = -3 * width % 128
    input_blocks = order_heads(self_input).reshape(shard, cp_count, 3 * width)
    input_blocks = jnp.swapaxes(jnp.pad(input_blocks, ((0, 0), (0, 0), (0, fill))), 0, 1)
    spare = jnp.pad(jnp.transpose(norm_gains), ((0, 0), (3 * width, fill - 4)))
    input_blocks = trade_cp(input_blocks + spare)
    input_blocks = input_blocks.reshape(group_rows, -1)
    if plain:
        tail = 3 * width + -5 * width % 128
        head_bucket = jnp.concatenate(
            [
                input_blocks[:, : 3 * width],
                skip_cols[:group_rows],
                skip_cols[group_rows:],
                input_blocks[:, 3 * width : tail],
            ],
            axis=1,
        )
    else:
        head_bucket = jnp.concatenate(
            [pack([skip_cols[:group_rows], skip_cols[group_rows:]]), input_blocks], axis=1
        )
    three = send_columns(
        tuple(after(member, head_bucket) for member in (self_output, cross_query, cross_output))
    )
    joined = jnp.concatenate([tokens.reshape(held, D), skip_in.reshape(held, D)], axis=1)
    joined_all = pieces_cp(after(joined, head_bucket))
    expand_weight = after(expand_weight, joined_all[-2])
    reduce_weight = after(reduce_weight, joined_all[-2])
    pairs_cols = send_columns((after(cross_pairs, head_bucket),))
    if plain:
        mid_bucket = lanes(jnp.concatenate([three, fold_rows(pairs_cols)], axis=1))
    else:
        pairs_cols = jnp.pad(pairs_cols, ((0, group_rows - group_text), (0, 0)))
        mid_bucket = pack(
            [three[:, :width], three[:, width : 2 * width], three[:, 2 * width :], pairs_cols]
        )
    mid_gathered = gather_group(mid_bucket)
    ff_bucket = send_columns((expand_weight, jnp.transpose(reduce_weight)))
    ff_gathered = gather_group(ff_bucket)
    expand_part, reduce_part = unpack(ff_gathered, (ff_width, ff_width))

    head_gathered = gather_group(head_bucket)
    if plain:
        input_part = head_gathered[:, : 3 * width]
        one = head_gathered[:, 3 * width : 4 * width]
        two = head_gathered[:, 4 * width : 5 * width]
        gain_start = 5 * width
    else:
        one, two, input_part = unpack(head_gathered, head_widths)
        gain_start = 2 * (width + -width % 128) + 3 * width
    skip_part = jnp.stack(
        [one.reshape(-1, group_rows, width), two.reshape(-1, group_rows, width)], axis=1
    ).reshape(2 * D, width)
    skip_part = after(skip_part, ff_bucket)
    gain_columns_t = head_gathered[:, gain_start : gain_start + 4].astype(f32)
    gain_rows = jnp.transpose(gain_columns_t)

    def times(left, full, left_dim):
        return jnp.concatenate(
            reorder_cp([dot(left, part, left_dim, 0) for part in full]), axis=1
        )

    def times_rows(full, right, right_dim):
        return jnp.concatenate(
            reorder_cp([dot(part, right, 0, right_dim) for part in full]), axis=0
        )

    def column_blocks(value):
        return jnp.split(value, cp_count, axis=1)

    def row_blocks(value):
        return jnp.split(value, cp_count, axis=0)

    def back_sum(left, full, left_dim):
        return sum(dot(block, part, left_dim, 1) for block, part in zip(left, full))

    def back_rows(full, right):
        return sum(dot(part, block, 1, 1) for part, block in zip(full, right))

    def traded(blocks):
        came = trade_cp(jnp.stack(blocks))
        return reorder_cp([came[k] for k in range(cp_count)])

    own_lengths = lax.dynamic_slice_in_dim(lengths, dp_index * packs, packs, 0)
    describe = jax.vmap(segment_info, in_axes=(0, None))
    chunk_block = jnp.arange(cp_count, dtype=jnp.int32) ^ cp_index
    chunk_pos = sp_index * chunk + (
        chunk_block[:, None] * rows + jnp.arange(rows, dtype=jnp.int32)[None, :]
    ).reshape(-1)
    turned = (cp_index * rows // CELL).reshape(1)
    _, chunk_row, chunk_col, _ = describe(own_lengths, chunk_pos)
    block_pos = jnp.arange(sp_count * cp_count, dtype=jnp.int32) * rows
    all_segments, _, _, all_valid = describe(lengths, block_pos)
    own_segments = lax.dynamic_slice_in_dim(all_segments, dp_index * packs, packs, 0)
    own_valid = lax.dynamic_slice_in_dim(all_valid, dp_index * packs, packs, 0)
    block = sp_index * cp_count + cp_index
    block_image = lax.dynamic_index_in_dim(own_segments, block, 1, keepdims=False)
    block_valid = lax.dynamic_index_in_dim(own_valid, block, 1, keepdims=False)
    token_valid = jnp.broadcast_to(block_valid[:, None], (packs, rows)).reshape(held, 1)
    pair_pack = (sp_index * pairs_dev + jnp.arange(pairs_dev, dtype=jnp.int32)) // group_heads
    first_cells, last_cells, valid_cells = jax.vmap(cell_ranges)(own_lengths)
    first_cells = jnp.take(first_cells, pair_pack, axis=0)
    last_cells = jnp.take(last_cells, pair_pack, axis=0)
    valid_cells = jnp.take(valid_cells, pair_pack, axis=0)

    times_all = after(timestep, head_bucket)
    for bit in bits_of("dp"):
        other = trade_bit(times_all, "dp", bit)
        times_all = jnp.where(
            has_bit("dp", bit),
            jnp.concatenate([other, times_all]),
            jnp.concatenate([times_all, other]),
        )
    silu_all = jax.nn.silu(times_all.astype(f32)).astype(bf16)
    shard_rows = shift_weight.shape[0]
    silu_own = lax.dynamic_slice_in_dim(silu_all, place * shard_rows, shard_rows, 2)
    slot_ids = jnp.arange(IMGS, dtype=jnp.int32)
    all_pick = (all_segments[:, :, None] == slot_ids).astype(f32)
    silu_blocks = jnp.einsum("pbi,pik->pbk", all_pick, silu_own.astype(f32), precision=highest)
    silu_blocks = jnp.swapaxes(
        silu_blocks.reshape(dp_count, packs, sp_count * cp_count, shard_rows), 1, 2
    ).reshape(-1, shard_rows)
    shifts = scatter_every(
        dot(silu_blocks.astype(bf16), shift_weight, 1, 0).reshape(-1, packs, D)
    )
    shift_rows = jnp.broadcast_to(shifts[:, None, :], (packs, rows, D)).reshape(held, D)

    image_dev = captions.shape[1]
    near = lax.dynamic_slice_in_dim(own_segments, sp_index * cp_count, cp_count, 1)
    local = jnp.clip(near - cp_index * image_dev, 0, image_dev - 1)
    caption_shard = jnp.pad(
        jnp.transpose(after(null_caption, head_bucket)), ((0, 0), (0, TEXT_PAD - TEXT))
    )
    caption_rows = caption_shard.shape[0]
    caption_full = jnp.transpose(gather_every(caption_shard).reshape(DT, TEXT_PAD))
    piece_index = cp_index.reshape(1)
    if plain:
        mixed_blocks = trade_cp(mix(piece_index, head_gathered, joined_all, width, ()))
        base_t, normed_self_t = start_forward(
            mixed_blocks, gain_columns_t, shifts.reshape(D, 1)
        )
        normed_all = pieces_cp(normed_self_t)
    else:
        mixed_all = [dot(piece, skip_part, 1, 0).astype(bf16) for piece in joined_all]
        mixed_blocks = trade_cp(jnp.stack(reorder_cp(mixed_all)))
        mixed = jnp.concatenate([mixed_blocks[k] for k in range(cp_count)], axis=1).astype(f32)
        base_stream = norm_gain(mixed, gain_rows[0])
        normed_self = (norm_gain(base_stream, gain_rows[1]) + shift_rows).astype(bf16)
        normed_all = pieces_cp(jnp.transpose(normed_self))
    cosine, sines = jax.vmap(rope_tables)(chunk_row, chunk_col)
    if plain:
        offset = 0
        qkv, raw = project(
            normed_all,
            head_gathered,
            offset,
            group_heads,
            cosine[0],
            sines[0],
            (caption_full,),
        )
        qkv, raw = qkv[None], raw[None]
        query_raw, key_raw = raw[:, :, 0], raw[:, :, 1]
    normed_all = jnp.concatenate(normed_all, axis=1)
    cosine, sines = cosine[:, None], sines[:, None]
    if not plain:
        projected = dot(input_part, normed_all, 0, 0)
        projected = jnp.transpose(
            projected.reshape(3, group_heads, HEAD, cp_count, packs, rows), (4, 1, 0, 2, 3, 5)
        ).reshape(packs, group_heads, 3, HEAD, chunk)
        query_raw, key_raw = projected[:, :, 0], projected[:, :, 1]
        queries = turn_norm(query_raw, cosine, sines).astype(bf16)
        key_rows = turn_norm(key_raw, cosine, sines).astype(bf16)
        value_rows = projected[:, :, 2].astype(bf16)
        qkv = jnp.stack([queries, key_rows, value_rows], axis=2)

    cp_ids = jnp.arange(cp_count, dtype=jnp.int32)
    turn_pick = (cp_ids[:, None] ^ cp_index) == cp_ids[None, :]
    near_turned = jnp.sum(jnp.where(turn_pick, near[0][None, :], 0), axis=1)
    near_null = jnp.sum(
        jnp.where(near_turned[:, None] == slot_ids[None, :], null_mask[0][None, :], 0), axis=1
    )
    near_null = near_null.astype(f32)[None, :]
    if plain:
        offered = offer(
            jnp.sum(jnp.where(turn_pick, local[0][None, :], 0), axis=1), captions, (qkv,)
        )
        arrived = jnp.stack(reorder_cp(exchange_cp(list(offered))))[:, None]
    else:
        offered = jnp.stack(
            [
                jnp.stack(
                    [
                        lax.dynamic_index_in_dim(captions[p], local[p, k], 0, keepdims=False)
                        for p in range(packs)
                    ]
                )
                for k in range(cp_count)
            ]
        )
        offered = jnp.pad(offered, ((0, 0), (0, 0), (0, TEXT_PAD - TEXT), (0, 0)))
        arrived = jnp.stack(send_cp([offered[k] for k in range(cp_count)]))
    own_null = jnp.take_along_axis(
        null_mask, block_image[:, None], axis=1
    )[:, 0]
    chosen = jnp.stack(
        [
            jnp.where(
                own_null[p] > 0,
                caption_full,
                lax.dynamic_index_in_dim(
                    arrived[:, p], block_image[p] // image_dev, 0, keepdims=False
                ),
            )
            for p in range(packs)
        ]
    )

    out_grad = cotangent.reshape(held, D).astype(f32) * token_valid
    out_turned = out_grad.astype(bf16)
    out_turned = turn_over(out_turned, (qkv,)) if plain else jnp.transpose(out_turned)
    out_grad = jnp.transpose(out_turned).astype(f32)
    reduce_pieces = pieces_cp(out_turned)

    def to_heads(value):
        value = value.reshape((sp_count, pairs_dev) + value.shape[2:])
        return lax.all_to_all(value, "sp", split_axis=0, concat_axis=0, tiled=True)

    def from_heads(value):
        value = lax.all_to_all(value, "sp", split_axis=0, concat_axis=0, tiled=True)
        return value.reshape((packs, group_heads) + value.shape[2:])

    if plain:
        *mid_parts, pairs_part = unpack_mid(
            mid_gathered, width, group_text, reduce_pieces[2]
        )
    else:
        output_part, query_part, cross_part, pairs_part = (
            after(part, qkv) for part in unpack(mid_gathered, mid_widths)
        )
        pairs_part = pairs_part.reshape(-1, group_rows, 2 * width)[:, :group_text].reshape(
            DT, 2 * width
        )
        mid_parts = (output_part, query_part, cross_part)
    pairs_full = pieces_cp(pairs_part)
    output_full, query_full, cross_full = (pieces_cp(part) for part in mid_parts)
    qkv = to_heads(qkv)
    out_self, totals_self, *sent = self_forward(
        qkv,
        first_cells,
        last_cells,
        turned,
        tuple(reduce_pieces) if plain else (),
        int(plain),
    )

    def to_tokens(value):
        value = value.reshape(sp_count, pairs_dev, HEAD, cp_count, rows)
        value = jnp.stack(reorder_cp([value[:, :, :, k] for k in range(cp_count)]))
        value = value.reshape(cp_count * sp_count, pairs_dev, HEAD, rows)
        value = lax.all_to_all(value, HEAD_ORDER, split_axis=0, concat_axis=0, tiled=True)
        value = value.reshape(cp_count, packs, group_heads, HEAD, rows)
        return jnp.transpose(value, (0, 2, 3, 1, 4)).reshape(D, held)

    def by_heads(value):
        value = value.reshape(cp_count, group_heads, HEAD, packs, rows)
        value = jnp.transpose(value, (0, 3, 1, 2, 4))
        value = value.reshape(cp_count * sp_count, pairs_dev, HEAD, rows)
        value = lax.all_to_all(value, HEAD_ORDER, split_axis=0, concat_axis=0, tiled=True)
        value = value.reshape(cp_count, sp_count, pairs_dev, HEAD, rows)
        value = reorder_cp([value[k] for k in range(cp_count)])
        return jnp.concatenate(value, axis=-1)

    def heads_of(value):
        value = value.reshape(HEADS, HEAD, packs, rows)
        return jnp.transpose(value, (2, 0, 1, 3)).reshape(packs * HEADS, HEAD, rows)

    def rows_of(value):
        value = value.reshape(packs, HEADS, HEAD, rows)
        return jnp.transpose(value, (1, 2, 0, 3)).reshape(D, held)

    if plain:
        attended = lax.all_to_all(
            sent[0].reshape(cp_count * sp_count, pairs_dev, HEAD, rows),
            HEAD_ORDER,
            split_axis=0,
            concat_axis=0,
            tiled=True,
        ).reshape(D, held)
    else:
        attended = to_tokens(out_self.astype(bf16))
    paired = times_rows(pairs_full, chosen.reshape(packs * TEXT_PAD, DT), 1)
    paired = jnp.moveaxis(paired.reshape(2, HEADS, HEAD, packs, TEXT_PAD), 3, 0)
    text_raw = paired[:, 0].reshape(packs * HEADS, HEAD, TEXT_PAD)
    text_keys = head_norm(text_raw).astype(bf16)
    text_values = paired[:, 1].reshape(packs * HEADS, HEAD, TEXT_PAD).astype(bf16)
    differences = jnp.array(group_differences(), jnp.int32)
    group_order = differences ^ (dp_index * sp_count + sp_index)
    if plain:
        mid_weights = (*output_full, *query_full, *cross_full)
        (
            mid_t,
            late_t,
            lefts,
            cross_raw,
            cross_queries,
            out_cross,
            totals_cross,
            normed_ffn_t,
        ) = middle_forward(
            piece_index,
            attended,
            base_t,
            gain_columns_t,
            text_keys,
            text_values,
            mid_weights,
        )
        attended_other = trade_bit(attended, "cp", 2)
        (normed_ffn_t,) = gate((normed_ffn_t,), (attended_other,))
        ffn_pieces = pieces_cp(normed_ffn_t)
        (lefts,) = gate((lefts,), (ffn_pieces[2],))
        lefts_other = trade_bit(lefts, "cp", 2)
        hidden, expand_in, *ffn_part = feed_forward(
            ffn_pieces, reduce_pieces, ff_gathered, ()
        )
    else:
        mid_stream = base_stream + times(attended, output_full, 0)
        normed_cross = norm_gain(mid_stream, gain_rows[2]).astype(bf16)
        cross_raw = heads_of(times_rows(query_full, normed_cross, 1))
        cross_queries = head_norm(cross_raw).astype(bf16)
        out_cross, totals_cross = cross_forward(cross_queries, text_keys, text_values)
        crossed = rows_of(out_cross.astype(bf16))
        late_stream = mid_stream + times(crossed, cross_full, 0)
        normed_ffn = norm_gain(late_stream, gain_rows[3]).astype(bf16)
        ffn_pieces = pieces_cp(jnp.transpose(normed_ffn))
        expanded = dot(jnp.concatenate(ffn_pieces, axis=1), expand_part, 0, 0)
        hidden = jax.nn.gelu(expanded, approximate=True).astype(bf16)

    def by_piece(value):
        value = value.astype(bf16).reshape(cp_count, held, D)
        return [value[k] for k in range(cp_count)]

    def sum_group(bucket):
        return lax.psum_scatter(bucket, GROUP, scatter_dimension=0, tiled=True)

    if not plain:
        gelu_back = jax.vjp(lambda preact: jax.nn.gelu(preact, approximate=True), expanded)[1]
        reduce_in = jnp.concatenate(reduce_pieces, axis=1)
        expand_in = gelu_back(dot(reduce_in, reduce_part, 0, 0))[0].astype(bf16)
        ffn_part = dot(expand_in, expand_part, 1, 1).astype(bf16)
        ffn_part = by_piece(ffn_part)
        block_part = by_piece(dot(hidden, reduce_part, 1, 1))
    if plain:
        keep, send = reduce_grads(reduce_pieces, hidden, group_order, ())
        first_half = trade_bit(send, *group_steps()[0][:2])
    ff_out = expand_grads(ffn_pieces, expand_in, (lefts_other,) if plain else ())
    if plain:
        ff_grads = sum_group(ff_out)
    else:
        reduce_out = dot(reduce_in, hidden, 1, 0).astype(bf16)
        ff_grads = sum_group(jnp.concatenate([ff_out, reduce_out], axis=1))
        ff_grads, reduce_sums = ff_grads[:, :ff_width], ff_grads[:, ff_width:]
    ffn_grad = scatter_cp(ffn_part)
    texts = jnp.transpose(chosen.reshape(packs * TEXT_PAD, DT))
    if plain:
        (texts,) = gate((texts,), (ff_out,))
        attended_all = [
            attended,
            trade_bit(attended, "cp", 1),
            attended_other,
            trade_bit(attended_other, "cp", 1),
        ]
        lefts = [lefts, trade_bit(lefts, "cp", 1), lefts_other, trade_bit(lefts_other, "cp", 1)]
    texts = pieces_cp(texts)
    if plain:
        mid_grad, attended_grad, rights, paired_rows, gain_pair = middle_backward(
            piece_index,
            (
                ffn_grad,
                out_turned,
                late_t,
                mid_t,
                gain_columns_t,
                cross_queries,
                text_keys,
                text_values,
                out_cross,
                totals_cross,
                cross_raw,
                text_raw,
            ),
            mid_weights,
            (ff_out, keep, send),
        )
        rights = exchange_cp([rights[k] for k in range(cp_count)])
        pairs = exchange_cp([paired_rows[k] for k in range(cp_count)])
    else:
        ffn_back = jax.vjp(norm_gain, late_stream, gain_rows[3])[1]
        late_part, gain_ffn = ffn_back(ffn_grad)
        late_grad = out_grad + late_part

        cout_in = column_blocks(late_grad.astype(bf16))
        cout_in = reorder_cp(cout_in)
        crossed_grad = heads_of(back_rows(cross_full, cout_in).astype(bf16))
        cq_grad, ck_grad, cv_grad = cross_backward(
            cross_queries, text_keys, text_values, crossed_grad, out_cross, totals_cross
        )
        cq_grad = cq_grad.astype(bf16).astype(f32)
        cross_raw_grad = rows_of(jax.vjp(head_norm, cross_raw)[1](cq_grad)[0].astype(bf16))
        cross_raw_grad = reorder_cp(row_blocks(cross_raw_grad))
        cross_norm_back = jax.vjp(norm_gain, mid_stream, gain_rows[2])[1]
        mid_part, gain_cross = cross_norm_back(
            back_sum(cross_raw_grad, query_full, 0)
        )
        mid_grad = late_grad + mid_part
        self_in = reorder_cp(column_blocks(mid_grad.astype(bf16)))
        attended_grad = back_rows(output_full, self_in).astype(bf16)
        normed_cross_t = jnp.transpose(normed_cross)
        cout_in = [jnp.transpose(member) for member in cout_in]
        self_in = [jnp.transpose(member) for member in self_in]
    if not plain:
        lefts = pieces_cp(jnp.stack([normed_cross_t, crossed]))
        attended_all = pieces_cp(attended)
    if not plain:
        rights = exchange_cp(
            [
                jnp.stack([cross, late, mid])
                for cross, late, mid in zip(cross_raw_grad, cout_in, self_in)
            ]
        )
    if plain:
        attended_grad = lax.all_to_all(
            attended_grad.reshape(cp_count * sp_count, pairs_dev, HEAD, rows),
            HEAD_ORDER,
            split_axis=0,
            concat_axis=0,
            tiled=True,
        ).reshape(cp_count, sp_count, pairs_dev, HEAD, rows)
    else:
        attended_grad = by_heads(attended_grad)
    qkv_grad = self_backward(
        qkv,
        attended_grad,
        out_self,
        totals_self,
        first_cells,
        last_cells,
        valid_cells,
        turned,
        (*rights[1:], *pairs[1:], texts[2], first_half) if plain else (),
    )
    stamp = qkv_grad
    qkv_grad = from_heads(qkv_grad)
    if not plain:
        block_out = (late_stream + scatter_cp(block_part)).astype(bf16)

    if not plain:
        ck_grad = ck_grad.astype(bf16).astype(f32)
        text_raw_grad = jax.vjp(head_norm, text_raw)[1](ck_grad)[0].astype(bf16)
        paired_grad = jnp.stack(
            [
                text_raw_grad.reshape(packs, D, TEXT_PAD),
                cv_grad.reshape(packs, D, TEXT_PAD).astype(bf16),
            ],
            axis=1,
        ).reshape(packs, 2 * D, TEXT_PAD)
        paired_rows = jnp.swapaxes(paired_grad, 0, 1).reshape(2 * D, packs * TEXT_PAD)
        paired_rows = reorder_cp(row_blocks(paired_rows))
        pairs = exchange_cp(paired_rows)
    if plain:
        mid_out = mid_grads_bucket(
            lefts, attended_all, rights, texts, pairs, stamp, dp_count * sp_count
        )
    else:
        lefts = jnp.concatenate(lefts, axis=2)
        lefts = [lefts[0], lefts[1], jnp.concatenate(attended_all, axis=1)]
        rights = jnp.concatenate(rights, axis=2)
        pairs_grad = dot(
            jnp.concatenate(texts, axis=1), jnp.concatenate(pairs, axis=1), 1, 1
        )
        pairs_grad = jnp.pad(
            pairs_grad.astype(bf16).reshape(-1, group_text, 2 * width),
            ((0, 0), (0, group_rows - group_text), (0, 0)),
        ).reshape(D, 2 * width)
        mid_out = pack(
            [dot(lefts[k], rights[k], 1, 1).astype(bf16) for k in range(3)] + [pairs_grad]
        )
    mid_grads = sum_group(mid_out)
    if plain:
        caption_grad = caption_product(near_null, pairs, pairs_part, mid_out)
    else:
        null_sum = jnp.einsum(
            "p,pnt->nt", own_null.astype(f32), paired_grad.astype(f32), precision=highest
        ).astype(bf16)
        caption_grad = sum(
            dot(part, block, 1, 0)
            for part, block in zip(pairs_full, reorder_cp(row_blocks(null_sum)))
        )
    caption_sum = caption_grad

    qkv_grad = after(qkv_grad, ff_grads)
    turn = functools.partial(turn_norm, cosine=cosine, sines=sines)
    query_raw_grad = jax.vjp(turn, query_raw)[1](qkv_grad[:, :, 0].astype(f32))[0].astype(bf16)
    key_raw_grad = jax.vjp(turn, key_raw)[1](qkv_grad[:, :, 1].astype(f32))[0].astype(bf16)
    projected_grad = jnp.stack([query_raw_grad, key_raw_grad, qkv_grad[:, :, 2]], axis=0)
    projected_grad = jnp.transpose(
        projected_grad.reshape(3, packs, group_heads, HEAD, cp_count, rows), (0, 2, 3, 4, 1, 5)
    ).reshape(3 * group_heads * HEAD, cp_count * held)
    if plain:
        normed_part = jnp.split(
            dot(input_part, projected_grad, 1, 0).astype(bf16), cp_count, axis=1
        )
    else:
        normed_part = dot(projected_grad, input_part, 0, 1).astype(bf16)
    self_input_grad = dot(normed_all, projected_grad, 1, 1).astype(bf16)
    if plain:
        block_part = reduce_parts(hidden, ff_gathered, normed_part[0], cp_count)
        block_out = jnp.transpose((late_t + scatter_cp(block_part)).astype(bf16))
    if plain:
        mixed_grad, sums = start_backward(
            mixed_blocks,
            gain_columns_t,
            base_t,
            mid_grad,
            scatter_cp([normed_part[k] for k in range(cp_count)]),
        )
        shift_grads = sums[:, 2][None]
        came = trade_cp(mixed_grad)
        mixed_pieces = reorder_cp([came[k] for k in range(cp_count)])
        head_out = skip_grads_bucket(
            mixed_pieces,
            joined_all,
            self_input_grad,
            jnp.concatenate([sums[:, :2], gain_pair], axis=1),
        )
        joined_part = [dot(piece, skip_part, 0, 1).astype(bf16) for piece in mixed_pieces]
    else:
        normed_self_grad = scatter_cp(by_piece(normed_part))
        self_norm_back = jax.vjp(norm_gain, base_stream, gain_rows[1])[1]
        base_part, gain_self = self_norm_back(normed_self_grad)
        shift_grads = jnp.sum(normed_self_grad.reshape(packs, rows, D), axis=1)
        base_grad = mid_grad + base_part
        skip_norm_back = jax.vjp(norm_gain, mixed, gain_rows[0])[1]
        mixed_grad, gain_skip = skip_norm_back(base_grad)
        mixed_pieces = traded(column_blocks(mixed_grad.astype(bf16)))
        mixed_in = jnp.concatenate(mixed_pieces, axis=0)
        skip_out = dot(jnp.concatenate(joined_all, axis=0), mixed_in, 0, 0).astype(bf16)
        skip_out = skip_out.reshape(-1, 2, shard, width)
        head_out = pack(
            [
                skip_out[:, 0].reshape(D, width),
                skip_out[:, 1].reshape(D, width),
                self_input_grad,
            ]
        )
        joined_part = dot(mixed_in, skip_part, 1, 1).astype(bf16).reshape(cp_count, held, 2 * D)
        joined_part = [joined_part[k] for k in range(cp_count)]
    head_grads = sum_group(head_out)
    if plain:
        reduce_sums = scatter_group_halves(
            keep, send, first_half, (stamp, normed_part[0], head_out)
        )
    caption_grad = scatter_every(
        after(caption_sum, head_out).astype(bf16).reshape(-1, caption_rows, TEXT_PAD)
    )
    joined_grad = scatter_cp(joined_part)

    shift_grads = after(shift_grads, head_out)
    if not plain:
        gains_part = jnp.stack([gain_skip, gain_self, gain_cross, gain_ffn])
        gains_grad = scatter_every(jnp.swapaxes(gains_part.reshape(4, -1, gain_columns), 0, 1))
    shift_weight_grad = lax.dot_general(
        silu_blocks,
        send_every(shift_grads).reshape(-1, D),
        (((0,), (0,)), ((), ())),
        precision=highest,
        preferred_element_type=f32,
    )

    factor = all_packs * PACK / jnp.sum(lengths).astype(f32)

    def join_columns(bucket, widths, tight=False):
        blocks = jnp.stack(send_cp(jnp.split(bucket, cp_count, axis=0)))
        start, parts = 0, []
        for size in widths:
            part = jnp.swapaxes(blocks[:, :, start : start + size], 0, 1)
            parts.append(part.astype(f32) * factor)
            start += size if tight else size + -size % 128
        return parts

    def whole(part):
        return part.reshape(part.shape[0], -1)

    mid_grads = after(mid_grads, head_out)
    (expand_out,) = join_columns(after(ff_grads, head_out), (ff_width,))
    (reduce_out,) = join_columns(reduce_sums, (ff_width,))
    if plain:
        cross_query_out, cross_out_out, self_out_out = join_columns(
            mid_grads[:, : 3 * width], (width, width, width), True
        )
        folded = 2 * width * DT // D
        (pairs_out,) = join_columns(
            unfold_rows(mid_grads[:, 3 * width : 3 * width + folded]), (2 * width,)
        )
    else:
        cross_query_out, cross_out_out, self_out_out = join_columns(
            mid_grads[:, : 3 * (width + -width % 128)], (width, width, width)
        )
        (pairs_out,) = join_columns(
            mid_grads[:group_text, 3 * (width + -width % 128) :], (2 * width,)
        )
    if plain:
        skip_out, input_out, gains_grad = finish_head(
            trade_cp(head_grads.reshape(cp_count, shard, -1)), factor
        )
        gains_grad = jnp.transpose(gains_grad)
    else:
        one, two, input_out = join_columns(head_grads, head_widths)
        skip_out = jnp.concatenate([whole(one), whole(two)], axis=0)
        input_out = restore_heads(whole(input_out))
        gains_grad = gains_grad * factor

    token_shape = (packs, rows, D)
    return (
        block_out.reshape(token_shape),
        (joined_grad[:, :D] * factor).astype(bf16).reshape(token_shape),
        (joined_grad[:, D:] * factor).astype(bf16).reshape(token_shape),
        skip_out,
        shift_weight_grad * factor,
        input_out,
        whole(self_out_out),
        whole(cross_query_out),
        whole(pairs_out),
        whole(cross_out_out),
        whole(expand_out),
        jnp.transpose(whole(reduce_out)),
        jnp.transpose(caption_grad)[:TEXT].astype(f32) * factor,
        gains_grad,
    )


def solution(mesh):
    token_spec = P("dp", ("sp", "cp"), None)
    by_rows = P(EVERY, None)
    by_columns = P(None, EVERY)
    return jax.shard_map(
        shards,
        mesh=mesh,
        in_specs=(
            token_spec,
            token_spec,
            P("dp", None, None),
            P("dp", "cp", None, None),
            P("dp", None),
            P(),
            token_spec,
            by_rows,
            by_rows,
            by_rows,
            by_rows,
            by_rows,
            by_rows,
            by_rows,
            by_rows,
            by_columns,
            by_columns,
            by_columns,
        ),
        out_specs=(
            token_spec,
            token_spec,
            token_spec,
            by_rows,
            by_rows,
            by_rows,
            by_rows,
            by_rows,
            by_rows,
            by_rows,
            by_rows,
            by_columns,
            by_columns,
            by_columns,
        ),
        check_vma=False,
    )
```

```python
import functools
import math

import jax
import jax.numpy as jnp
from jax import lax
from jax.experimental import pallas as pl
from jax.experimental.pallas import tpu as pltpu
from jax.sharding import PartitionSpec as P

D = 1408
HEADS = 16
HEAD = 88
DT = 1024
TEXT = 333
TEXT_PAD = 384
BIG_SIDE = 32
SMALL_SIDE = 16
PACK = 4096
IMGS = 16
CELL = 256
CELLS = PACK // CELL
SCALING = 1.0 / math.sqrt(HEAD)

epsilon = 1e-06
highest = lax.Precision.HIGHEST
bf16 = jnp.bfloat16
f32 = jnp.float32
GROUP = ("dp", "sp")
EVERY = ("dp", "sp", "cp")
HEAD_ORDER = ("cp", "sp")


def layer_norm(vector, axis=-1):
    centred = vector - jnp.mean(vector, axis=axis, keepdims=True)
    return centred * lax.rsqrt(jnp.mean(centred * centred, axis=axis, keepdims=True) + epsilon)


def head_norm(vector):
    return layer_norm(vector, -2)


def norm_gain(vector, gain):
    return layer_norm(vector) * gain


def dot(left, right, left_dim, right_dim):
    return lax.dot_general(
        left, right, (((left_dim,), (right_dim,)), ((), ())), preferred_element_type=f32
    )


def segment_info(lengths, positions):
    seg_ends = jnp.cumsum(lengths)
    starts = seg_ends - lengths
    present = lengths > 0
    slot_ids = jnp.arange(lengths.shape[0], dtype=jnp.int32)
    segment = jnp.sum(
        ((seg_ends[None, :] <= positions[:, None]) & present[None, :]).astype(jnp.int32), axis=1
    )
    onehot = segment[:, None] == slot_ids[None, :]
    seg_start = jnp.sum(jnp.where(onehot, starts[None, :], 0), axis=1)
    seg_size = jnp.sum(jnp.where(onehot, lengths[None, :], 0), axis=1)
    side_len = jnp.where(seg_size == BIG_SIDE * BIG_SIDE, BIG_SIDE, SMALL_SIDE).astype(jnp.int32)
    offset = positions - seg_start
    images = jnp.sum(present.astype(jnp.int32))
    return (segment, offset // side_len, offset % side_len, (segment < images).astype(f32))


def cell_ranges(lengths):
    positions = jnp.arange(CELLS, dtype=jnp.int32) * CELL
    seg_ends = jnp.cumsum(lengths)
    present = lengths > 0
    segment = jnp.sum(
        ((seg_ends[None, :] <= positions[:, None]) & present[None, :]).astype(jnp.int32), axis=1
    )
    same = segment[:, None] == segment[None, :]
    cells = jnp.arange(CELLS, dtype=jnp.int32)
    first = jnp.min(jnp.where(same, cells[None, :], CELLS), axis=1)
    last = jnp.max(jnp.where(same, cells[None, :] + 1, 0), axis=1)
    return (first, last, jnp.sum(lengths) // CELL)


def rope_tables(grid_row, grid_col):
    quarter = HEAD // 4
    frequency = jnp.exp(jnp.arange(quarter, dtype=f32) * (-math.log(10000.0) / quarter))
    angles = jnp.concatenate(
        [
            frequency[:, None] * grid_row.astype(f32)[None, :],
            frequency[:, None] * grid_col.astype(f32)[None, :],
        ],
        axis=0,
    )
    return (jnp.cos(angles), jnp.sin(angles))


def rotate(vector, cosine, sines):
    quarter = HEAD // 4
    one, two, three, four = (
        vector[..., k * quarter : (k + 1) * quarter, :] for k in range(4)
    )
    cos_row, cos_col = cosine[..., :quarter, :], cosine[..., quarter:, :]
    sin_row, sin_col = sines[..., :quarter, :], sines[..., quarter:, :]
    return jnp.concatenate(
        [
            one * cos_row - two * sin_row,
            one * sin_row + two * cos_row,
            three * cos_col - four * sin_col,
            three * sin_col + four * cos_col,
        ],
        axis=-2,
    )


def turn_norm(vector, cosine, sines):
    return rotate(head_norm(vector), cosine, sines)


def trade_bit(value, axis, bit):
    count = lax.axis_size(axis)
    return lax.ppermute(value, axis, [(k, k ^ bit) for k in range(count)])


def bits_of(axis):
    count = lax.axis_size(axis)
    return [1 << k for k in range(count.bit_length() - 1)]


def has_bit(axis, bit):
    return (lax.axis_index(axis) // bit) % 2 == 1


def pieces_cp(value):
    pieces = [value]
    found = {0: value}
    for bit in reversed(bits_of("cp")):
        for key in list(found):
            found[key | bit] = trade_bit(found[key], "cp", bit)
    pieces = [found[key] for key in range(lax.axis_size("cp"))]
    return pieces


def reorder_cp(pieces):
    for bit in bits_of("cp"):
        high = has_bit("cp", bit)
        pieces = [
            jnp.where(high, pieces[key ^ bit], pieces[key]) for key in range(len(pieces))
        ]
    return pieces


def gather_cp(value):
    return jnp.stack(reorder_cp(pieces_cp(value)))


def scatter_cp(pieces):
    pieces = [piece.astype(bf16) for piece in pieces]
    for bit in bits_of("cp"):
        pieces = [
            (
                pieces[key].astype(f32) + trade_bit(pieces[key + 1], "cp", bit).astype(f32)
            ).astype(f32 if len(pieces) == 2 else bf16)
            for key in range(0, len(pieces), 2)
        ]
    return pieces[0]


def after(value, *others):
    for other in others:
        value = value + (other[(0,) * other.ndim].astype(f32) * 0.0).astype(value.dtype)
    return value


def exchange_cp(pieces):
    count = lax.axis_size("cp")
    return [pieces[0]] + [
        lax.ppermute(pieces[key], "cp", [(k, k ^ key) for k in range(count)])
        for key in range(1, count)
    ]


def trade_cp(blocks):
    return lax.all_to_all(blocks, "cp", split_axis=0, concat_axis=0, tiled=True)


def send_cp(blocks):
    return reorder_cp(exchange_cp(reorder_cp(blocks)))


def group_steps():
    steps = [("dp", bit, bit * lax.axis_size("sp")) for bit in bits_of("dp")]
    return steps + [("sp", bit, bit) for bit in bits_of("sp")]


def group_differences():
    differences = [0]
    for _, _, weight in reversed(group_steps()):
        differences = differences + [key ^ weight for key in differences]
    return differences


def scatter_group_halves(keep, send, first, waits):
    for step, (axis, bit, _) in enumerate(group_steps()):
        came = (trade_bit(send, axis, bit) if step else first).astype(f32)
        total = after(keep.astype(f32) + came, waits[step]).astype(bf16)
        half = total.shape[0] // 2
        keep, send = total[:half], total[half:]
        if step == len(group_steps()) - 1:
            return total
    return None


def gather_every(value):
    dims = []
    for axis in ("dp", "sp", "cp"):
        for bit in reversed(bits_of(axis)):
            other = trade_bit(value, axis, bit)
            value = jnp.where(
                has_bit(axis, bit), jnp.stack([other, value]), jnp.stack([value, other])
            )
            dims.append((axis, bit))
    depth = len(dims)
    value = jnp.transpose(
        value, tuple(reversed(range(depth))) + tuple(range(depth, value.ndim))
    )
    return value.reshape((-1,) + value.shape[depth:])


def scatter_every(value):
    cp_count = lax.axis_size("cp")
    value = jnp.swapaxes(value.reshape((-1, cp_count) + value.shape[1:]), 0, 1)
    for axis in ("cp", "dp", "sp"):
        for bit in reversed(bits_of(axis)) if axis != "cp" else bits_of(axis):
            if axis == "cp":
                halves = value.reshape((-1, 2) + value.shape[1:])
                first, second = halves[:, 0], halves[:, 1]
            else:
                halves = value.reshape((2, -1) + value.shape[1:])
                first, second = halves[0], halves[1]
            high = has_bit(axis, bit)
            keep = jnp.where(high, second, first)
            send = jnp.where(high, first, second)
            value = keep + trade_bit(send, axis, bit)
        if axis == "cp":
            value = value[0]
    return value[0]


def send_every(value):
    count = lax.axis_size("dp") * lax.axis_size("sp") * lax.axis_size("cp")
    value = jnp.broadcast_to(value[None], (count,) + value.shape)
    return lax.all_to_all(value, EVERY, split_axis=0, concat_axis=0, tiled=True)


def sum_every(value):
    came = lax.all_to_all(value, EVERY, split_axis=0, concat_axis=0, tiled=True)
    return jnp.sum(came.astype(f32), axis=0)


def flip(block):
    if block.shape[0] % 128 == 0 and block.shape[1] % 128 == 0:
        return jnp.transpose(block)
    return jnp.transpose(block.astype(f32)).astype(bf16)


def kernel_dot(left, right, left_dim=1, right_dim=0):
    return lax.dot_general(
        left, right, (((left_dim,), (right_dim,)), ((), ())), preferred_element_type=f32
    )


def over_cells(first, last, step, carry):
    count = last - first
    fours = count // 4

    def four(turn, current):
        for k in range(4):
            current = step(first + turn * 4 + k, current)
        return current

    carry = lax.fori_loop(0, fours, four, carry)
    return lax.fori_loop(first + fours * 4, last, step, carry)


def self_forward_kernel(per_cell, first_ref, last_ref, turned_ref, qkv_ref, *refs):
    out_ref, total_ref, *sent_ref, keys = refs[-4:] if per_cell else refs[-3:]
    pair = pl.program_id(0)
    per = qkv_ref.shape[-1] // CELL

    def where(cell):
        lanes = ((cell % per) ^ turned_ref[0]) * CELL
        return cell // per, pl.ds(pl.multiple_of(lanes, CELL), CELL)

    def turn_keys(cell, carry):
        chunk, lanes = where(cell)
        keys[cell] = flip(qkv_ref[chunk, 0, 1, :, lanes])
        return carry

    lax.fori_loop(0, CELLS, turn_keys, 0)

    def one_cell(cell, carry):
        chunk, lanes = where(cell)
        query = qkv_ref[chunk, 0, 0, :, lanes]

        def step(other, current):
            summed, totals = current
            key_chunk, key_lanes = where(other)
            weights = jnp.exp(kernel_dot(keys[other], query) * SCALING)
            totals = totals + jnp.sum(weights, axis=0, keepdims=True)
            summed = summed + kernel_dot(
                qkv_ref[key_chunk, 0, 2, :, key_lanes], weights.astype(bf16)
            )
            return (summed, totals)

        summed, totals = over_cells(
            first_ref[pair, cell],
            last_ref[pair, cell],
            step,
            (jnp.zeros((HEAD, CELL), f32), jnp.zeros((1, CELL), f32)),
        )
        out = summed / totals
        out_ref[chunk, 0, :, lanes] = out
        if per_cell:
            sent_ref[0][cell % per, chunk, 0] = out.astype(bf16)
        total_ref[chunk, 0, :, lanes] = totals
        return carry

    lax.fori_loop(0, CELLS, one_cell, 0)


def self_backward_kernel(
    first_ref,
    last_ref,
    valid_ref,
    turned_ref,
    qkv_ref,
    grad_ref,
    out_ref,
    total_ref,
    *refs,
):
    result_ref, keys, values, key_sums, value_sums = refs[-5:]
    pair = pl.program_id(0)
    per = qkv_ref.shape[-1] // CELL

    def where(cell):
        lanes = ((cell % per) ^ turned_ref[0]) * CELL
        return cell // per, pl.ds(pl.multiple_of(lanes, CELL), CELL)

    def prepare(cell, carry):
        chunk, lanes = where(cell)
        keys[cell] = flip(qkv_ref[chunk, 0, 1, :, lanes])
        values[cell] = flip(qkv_ref[chunk, 0, 2, :, lanes])
        key_sums[cell] = jnp.zeros((HEAD, CELL), f32)
        value_sums[cell] = jnp.zeros((HEAD, CELL), f32)
        result_ref[chunk, 0, 0, :, lanes] = jnp.zeros((HEAD, CELL), bf16)
        return carry

    lax.fori_loop(0, CELLS, prepare, 0)

    def one_cell(cell, carry):
        chunk, lanes = where(cell)
        query = qkv_ref[chunk, 0, 0, :, lanes]
        if len(grad_ref.shape) == 5:
            grad = grad_ref[cell % per, chunk, 0].astype(f32)
        else:
            grad = grad_ref[chunk, 0, :, lanes].astype(f32)
        inverse = 1.0 / total_ref[chunk, 0, :, lanes]
        scaled = (grad * inverse).astype(bf16)
        total_grad = (
            -jnp.sum(grad * out_ref[chunk, 0, :, lanes], axis=0, keepdims=True) * inverse
        )

        def step(other, query_sum):
            key_chunk, key_lanes = where(other)
            weights = jnp.exp(kernel_dot(keys[other], query) * SCALING)
            weight_grad = kernel_dot(values[other], scaled)
            score_grad = (weights * (weight_grad + total_grad)).astype(bf16)
            value_sums[other] += kernel_dot(scaled, weights.astype(bf16), 1, 1)
            key_sums[other] += kernel_dot(query, score_grad, 1, 1)
            return query_sum + kernel_dot(qkv_ref[key_chunk, 0, 1, :, key_lanes], score_grad)

        query_sum = over_cells(
            first_ref[pair, cell], last_ref[pair, cell], step, jnp.zeros((HEAD, CELL), f32)
        )
        result_ref[chunk, 0, 0, :, lanes] = (query_sum * SCALING).astype(bf16)
        return carry

    lax.fori_loop(0, valid_ref[pair], one_cell, 0)

    def finish(cell, carry):
        chunk, lanes = where(cell)
        result_ref[chunk, 0, 1, :, lanes] = (key_sums[cell] * SCALING).astype(bf16)
        result_ref[chunk, 0, 2, :, lanes] = value_sums[cell].astype(bf16)
        return carry

    lax.fori_loop(0, CELLS, finish, 0)


def pair_spec(shape):
    block = (shape[0], 1) + shape[2:]
    rest = (0,) * (len(shape) - 2)
    return pl.BlockSpec(block, lambda pair, *_: (0, pair) + rest)


VMEM_WHOLE = pl.BlockSpec(memory_space=pltpu.VMEM)
SMEM_WHOLE = pl.BlockSpec(memory_space=pltpu.SMEM)
ANY_WHOLE = pl.BlockSpec(memory_space=pl.ANY)
VMEM_LIMIT = 48 * 1024 * 1024


def self_forward(qkv, first, last, turned, stamps, per_cell):
    chunks, pairs, _, _, columns = qkv.shape
    out_shape = (chunks, pairs, HEAD, columns)
    total_shape = (chunks, pairs, 1, columns)
    sent_shape = (columns // CELL, chunks, pairs, HEAD, CELL)
    sent_spec = pl.BlockSpec(
        sent_shape[:2] + (1,) + sent_shape[3:], lambda pair, *_: (0, 0, pair, 0, 0)
    )
    return pl.pallas_call(
        functools.partial(self_forward_kernel, per_cell),
        out_shape=(
            jax.ShapeDtypeStruct(out_shape, f32),
            jax.ShapeDtypeStruct(total_shape, f32),
        )
        + (jax.ShapeDtypeStruct(sent_shape, bf16),) * per_cell,
        grid_spec=pltpu.PrefetchScalarGridSpec(
            num_scalar_prefetch=3,
            grid=(pairs,),
            in_specs=[pair_spec(qkv.shape)] + [pl.BlockSpec(memory_space=pl.ANY)] * len(stamps),
            out_specs=[pair_spec(out_shape), pair_spec(total_shape)] + [sent_spec] * per_cell,
            scratch_shapes=[pltpu.VMEM((CELLS, CELL, HEAD), bf16)],
        ),
        compiler_params=pltpu.CompilerParams(vmem_limit_bytes=VMEM_LIMIT),
        cost_estimate=pl.CostEstimate(flops=10**10, bytes_accessed=8 << 20, transcendentals=0),
        name="self_forward",
    )(first, last, turned, qkv, *stamps)


def self_backward(qkv, grad, out, totals, first, last, valid, turned, stamps):
    pairs = qkv.shape[1]
    return pl.pallas_call(
        self_backward_kernel,
        out_shape=jax.ShapeDtypeStruct(qkv.shape, bf16),
        grid_spec=pltpu.PrefetchScalarGridSpec(
            num_scalar_prefetch=4,
            grid=(pairs,),
            in_specs=[
                pair_spec(qkv.shape),
                pair_spec(grad.shape)
                if grad.ndim == 4
                else pl.BlockSpec(
                    grad.shape[:2] + (1,) + grad.shape[3:], lambda pair, *_: (0, 0, pair, 0, 0)
                ),
                pair_spec(out.shape),
                pair_spec(totals.shape),
            ]
            + [pl.BlockSpec(memory_space=pl.ANY)] * len(stamps),
            out_specs=pair_spec(qkv.shape),
            scratch_shapes=[
                pltpu.VMEM((CELLS, CELL, HEAD), bf16),
                pltpu.VMEM((CELLS, CELL, HEAD), bf16),
                pltpu.VMEM((CELLS, HEAD, CELL), f32),
                pltpu.VMEM((CELLS, HEAD, CELL), f32),
            ],
        ),
        compiler_params=pltpu.CompilerParams(vmem_limit_bytes=VMEM_LIMIT),
        cost_estimate=pl.CostEstimate(flops=18 * 10**9, bytes_accessed=16 << 20, transcendentals=0),
        name="self_backward",
    )(first, last, valid, turned, qkv, grad, out, totals, *stamps)


def text_weights(key_block, query):
    scores = kernel_dot(flip(key_block), query) * SCALING
    present = lax.broadcasted_iota(jnp.int32, scores.shape, 0) < TEXT
    return jnp.where(present, jnp.exp(scores), 0.0)


def cross_forward_kernel(query_ref, key_ref, value_ref, out_ref, total_ref):
    for head in range(query_ref.shape[0]):
        weights = text_weights(key_ref[head], query_ref[head])
        totals = jnp.sum(weights, axis=0, keepdims=True)
        out_ref[head] = kernel_dot(value_ref[head], weights.astype(bf16)) / totals
        total_ref[head] = totals


def cross_backward_kernel(
    query_ref,
    key_ref,
    value_ref,
    grad_ref,
    out_ref,
    total_ref,
    query_grad_ref,
    key_grad_ref,
    value_grad_ref,
):
    for head in range(query_ref.shape[0]):
        query, keys = query_ref[head], key_ref[head]
        grad = grad_ref[head].astype(f32)
        inverse = 1.0 / total_ref[head]
        scaled = (grad * inverse).astype(bf16)
        total_grad = -jnp.sum(grad * out_ref[head], axis=0, keepdims=True) * inverse
        weights = text_weights(keys, query)
        weight_grad = kernel_dot(flip(value_ref[head]), scaled)
        score_grad = (weights * (weight_grad + total_grad)).astype(bf16)
        query_grad_ref[head] = kernel_dot(keys, score_grad) * SCALING
        key_grad_ref[head] = kernel_dot(query, score_grad, 1, 1) * SCALING
        value_grad_ref[head] = kernel_dot(scaled, weights.astype(bf16), 1, 1)


HEADS_STEP = 4


def head_spec(shape):
    return pl.BlockSpec((HEADS_STEP,) + shape[1:], lambda step: (step, 0, 0))


def cross_forward(queries, keys, values):
    count, _, rows = queries.shape
    out_shape = (count, HEAD, rows)
    total_shape = (count, 1, rows)
    return pl.pallas_call(
        cross_forward_kernel,
        out_shape=(
            jax.ShapeDtypeStruct(out_shape, f32),
            jax.ShapeDtypeStruct(total_shape, f32),
        ),
        grid=(count // HEADS_STEP,),
        in_specs=[head_spec(queries.shape), head_spec(keys.shape), head_spec(values.shape)],
        out_specs=[head_spec(out_shape), head_spec(total_shape)],
        compiler_params=pltpu.CompilerParams(vmem_limit_bytes=VMEM_LIMIT),
        name="cross_forward",
    )(queries, keys, values)


def cross_backward(queries, keys, values, grad, out, totals):
    inputs = (queries, keys, values, grad, out, totals)
    return pl.pallas_call(
        cross_backward_kernel,
        out_shape=(
            jax.ShapeDtypeStruct(queries.shape, f32),
            jax.ShapeDtypeStruct(keys.shape, f32),
            jax.ShapeDtypeStruct(values.shape, f32),
        ),
        grid=(queries.shape[0] // HEADS_STEP,),
        in_specs=[head_spec(member.shape) for member in inputs],
        out_specs=[head_spec(queries.shape), head_spec(keys.shape), head_spec(values.shape)],
        compiler_params=pltpu.CompilerParams(vmem_limit_bytes=VMEM_LIMIT),
        name="cross_backward",
    )(*inputs)


def unpack_kernel(width, text, bucket_ref, stamp_ref, *outs):
    whole = flip(bucket_ref[:, : 3 * width + -3 * width % 128])
    for part in range(3):
        outs[part][...] = whole[part * width : (part + 1) * width]
    rows = D * text // DT
    folded = 2 * width * DT // D
    for group in range(DT // text):
        block = bucket_ref[group * rows : (group + 1) * rows, 3 * width : 3 * width + folded]
        outs[3][group * text : (group + 1) * text, :] = unfold_rows(block)


def unpack_mid(bucket, width, text, stamp):
    part = jax.ShapeDtypeStruct((width, D), bf16)
    return pl.pallas_call(
        functools.partial(unpack_kernel, width, text),
        out_shape=(part, part, part, jax.ShapeDtypeStruct((DT, 2 * width), bf16)),
        in_specs=[VMEM_WHOLE, ANY_WHOLE],
        out_specs=[VMEM_WHOLE] * 4,
        compiler_params=pltpu.CompilerParams(vmem_limit_bytes=VMEM_LIMIT),
        cost_estimate=pl.CostEstimate(flops=1, bytes_accessed=12 << 20, transcendentals=0),
        name="unpack_mid",
    )(bucket, stamp)


def offer_kernel(count, which_ref, captions_ref, *refs):
    outputs = refs[-2 - count : -2]
    stage, sems = refs[-2:]
    copies = [
        pltpu.make_async_copy(captions_ref.at[0, which_ref[k]], stage.at[k], sems.at[k])
        for k in range(count)
    ]
    for copy in copies:
        copy.start()
    for k in range(count):
        copies[k].wait()
        rest = jnp.zeros((TEXT_PAD - TEXT, stage.shape[2]), f32)
        outputs[k][...] = jnp.concatenate([stage[k].astype(f32), rest], axis=0).astype(bf16)


def offer(which, captions, stamps):
    count = which.shape[0]
    shape = jax.ShapeDtypeStruct((TEXT_PAD, captions.shape[3]), bf16)
    return pl.pallas_call(
        functools.partial(offer_kernel, count),
        out_shape=(shape,) * count,
        in_specs=[SMEM_WHOLE] + [ANY_WHOLE] * (1 + len(stamps)),
        out_specs=[VMEM_WHOLE] * count,
        scratch_shapes=[
            pltpu.VMEM((count, TEXT, captions.shape[3]), bf16),
            pltpu.SemaphoreType.DMA((count,)),
        ],
        compiler_params=pltpu.CompilerParams(vmem_limit_bytes=VMEM_LIMIT),
        cost_estimate=pl.CostEstimate(flops=1, bytes_accessed=8 << 20, transcendentals=0),
        name="offer",
    )(which, captions, *stamps)


def gate(values, stamps):
    def kernel(*refs):
        pass

    return pl.pallas_call(
        kernel,
        out_shape=tuple(jax.ShapeDtypeStruct(value.shape, value.dtype) for value in values),
        in_specs=[ANY_WHOLE] * (len(values) + len(stamps)),
        out_specs=[ANY_WHOLE] * len(values),
        input_output_aliases={k: k for k in range(len(values))},
        cost_estimate=pl.CostEstimate(flops=1, bytes_accessed=1, transcendentals=0),
        name="gate",
    )(*values, *stamps)


def caption_kernel(count, null_ref, *refs):
    total = sum(refs[k][...].astype(f32) * null_ref[0, k] for k in range(count))
    refs[-1][...] = kernel_dot(refs[count][...], total.astype(bf16)).astype(bf16)


def caption_product(nulls, pairs, weight, stamp):
    count = len(pairs)
    return pl.pallas_call(
        functools.partial(caption_kernel, count),
        out_shape=jax.ShapeDtypeStruct((weight.shape[0], pairs[0].shape[1]), bf16),
        in_specs=[SMEM_WHOLE] + [VMEM_WHOLE] * (count + 1) + [ANY_WHOLE],
        out_specs=VMEM_WHOLE,
        compiler_params=pltpu.CompilerParams(vmem_limit_bytes=VMEM_LIMIT),
        cost_estimate=pl.CostEstimate(flops=10**9, bytes_accessed=5 << 20, transcendentals=0),
        name="caption_product",
    )(nulls, *pairs, weight, stamp)


def turn_over_kernel(value_ref, *refs):
    out_ref = refs[-1]
    out_ref[...] = flip(value_ref[...])


def turn_over(value, stamps):
    return pl.pallas_call(
        turn_over_kernel,
        out_shape=jax.ShapeDtypeStruct(value.shape[::-1], value.dtype),
        in_specs=[VMEM_WHOLE] + [ANY_WHOLE] * len(stamps),
        out_specs=VMEM_WHOLE,
        compiler_params=pltpu.CompilerParams(vmem_limit_bytes=VMEM_LIMIT),
        cost_estimate=pl.CostEstimate(flops=1, bytes_accessed=2 << 20, transcendentals=0),
        name="turn_over",
    )(value, *stamps)


def expand_grads_kernel(count, *refs):
    left = jnp.concatenate([ref[...] for ref in refs[:count]], axis=1)
    refs[-1][...] = kernel_dot(left, refs[count][...]).astype(bf16)


def expand_grads(pieces, right, stamps):
    steps = 2
    rows, width = D // steps, right.shape[1]
    return pl.pallas_call(
        functools.partial(expand_grads_kernel, len(pieces)),
        out_shape=jax.ShapeDtypeStruct((D, width), bf16),
        grid=(steps,),
        in_specs=[pl.BlockSpec((rows, pieces[0].shape[1]), lambda g: (g, 0))] * len(pieces)
        + [pl.BlockSpec(right.shape, lambda g: (0, 0))]
        + [ANY_WHOLE] * len(stamps),
        out_specs=pl.BlockSpec((rows, width), lambda g: (g, 0)),
        compiler_params=pltpu.CompilerParams(vmem_limit_bytes=VMEM_LIMIT),
        cost_estimate=pl.CostEstimate(
            flops=2 * D * right.shape[0] * width, bytes_accessed=12 << 20, transcendentals=0
        ),
        name="expand_grads",
    )(*pieces, right, *stamps)


def reduce_grads_kernel(count, group_ref, *refs):
    pieces, right_ref = refs[:count], refs[count]
    keep_ref, send_ref = refs[-2:]
    step, steps = pl.program_id(0), pl.num_programs(0)
    left = jnp.concatenate([ref[...] for ref in pieces], axis=1)
    product = kernel_dot(left, right_ref[...]).astype(bf16)

    @pl.when(step < steps // 2)
    def _():
        keep_ref[...] = product

    @pl.when(step >= steps // 2)
    def _():
        send_ref[...] = product


def reduce_grads(pieces, right, groups, stamps):
    steps, width = groups.shape[0], right.shape[1]
    rows, half = D // steps, steps // 2
    shape = jax.ShapeDtypeStruct((D // 2, width), bf16)
    return pl.pallas_call(
        functools.partial(reduce_grads_kernel, len(pieces)),
        out_shape=(shape, shape),
        grid_spec=pltpu.PrefetchScalarGridSpec(
            num_scalar_prefetch=1,
            grid=(steps,),
            in_specs=[
                pl.BlockSpec((rows, pieces[0].shape[1]), lambda g, group: (group[g], 0))
            ]
            * len(pieces)
            + [pl.BlockSpec(right.shape, lambda g, group: (0, 0))]
            + [ANY_WHOLE] * len(stamps),
            out_specs=[
                pl.BlockSpec((rows, width), lambda g, group: (jnp.minimum(g, half - 1), 0)),
                pl.BlockSpec((rows, width), lambda g, group: (jnp.maximum(g - half, 0), 0)),
            ],
        ),
        compiler_params=pltpu.CompilerParams(vmem_limit_bytes=VMEM_LIMIT),
        cost_estimate=pl.CostEstimate(
            flops=2 * D * right.shape[0] * width, bytes_accessed=12 << 20, transcendentals=0
        ),
        name="reduce_grads",
    )(groups, *pieces, right, *stamps)


def fold_rows(value):
    rows, columns = value.shape
    k, m = rows // 8, columns // 11
    over = value[:, 8 * m :]
    below = jnp.concatenate(
        [
            over[: 3 * k],
            over[3 * k : 6 * k],
            jnp.concatenate(
                [
                    over[6 * k :, : 2 * m],
                    jnp.concatenate([over[6 * k : 7 * k, 2 * m :], over[7 * k :, 2 * m :]], axis=1),
                ],
                axis=0,
            ),
        ],
        axis=1,
    )
    return jnp.concatenate([value[:, : 8 * m], below], axis=0)


def unfold_rows(value):
    rows, columns = value.shape
    k, m = rows // 11, columns // 8
    below = value[8 * k :]
    last = below[2 * k :, 6 * m :]
    over = jnp.concatenate(
        [
            below[:, : 3 * m],
            below[:, 3 * m : 6 * m],
            jnp.concatenate(
                [below[: 2 * k, 6 * m :], jnp.concatenate([last[:, :m], last[:, m:]], axis=0)],
                axis=1,
            ),
        ],
        axis=0,
    )
    return jnp.concatenate([value[: 8 * k], over], axis=1)


def mid_grads_kernel(count, width, groups, *refs):
    lefts, third, rights, texts, pairs = (refs[k * count : (k + 1) * count] for k in range(5))
    out_ref = refs[5 * count + 1]
    rows = out_ref.shape[0] // groups
    products = [
        sum(
            kernel_dot(left[part] if part < 2 else last[...], right[part], 1, 1)
            for left, last, right in zip(lefts, third, rights)
        )
        for part in range(3)
    ]
    text = texts[0].shape[0] // groups
    product = sum(kernel_dot(left[...], right[...], 1, 1) for left, right in zip(texts, pairs))
    for group in range(groups):
        here = slice(group * rows, (group + 1) * rows)
        block = [member[here] for member in products]
        block.append(fold_rows(product[group * text : (group + 1) * text]))
        rest = out_ref.shape[1] - sum(member.shape[1] for member in block)
        block.append(jnp.zeros((rows, rest), f32))
        out_ref[here, :] = jnp.concatenate(block, axis=1).astype(bf16)


def mid_grads_bucket(lefts, third, rights, texts, pairs, stamp, groups):
    count, width = len(lefts), rights[0].shape[1]
    steps = 2
    rows, text = D // steps, DT // steps
    columns = 3 * width + 2 * width * DT // D
    columns += -columns % 128
    return pl.pallas_call(
        functools.partial(mid_grads_kernel, count, width, groups // steps),
        out_shape=jax.ShapeDtypeStruct((D, columns), bf16),
        grid=(steps,),
        in_specs=[pl.BlockSpec((2, rows, lefts[0].shape[2]), lambda g: (0, g, 0))] * count
        + [pl.BlockSpec((rows, third[0].shape[1]), lambda g: (g, 0))] * count
        + [pl.BlockSpec(rights[0].shape, lambda g: (0, 0, 0))] * count
        + [pl.BlockSpec((text, texts[0].shape[1]), lambda g: (g, 0))] * count
        + [pl.BlockSpec(pairs[0].shape, lambda g: (0, 0))] * count
        + [ANY_WHOLE],
        out_specs=pl.BlockSpec((rows, columns), lambda g: (g, 0)),
        compiler_params=pltpu.CompilerParams(vmem_limit_bytes=VMEM_LIMIT),
        cost_estimate=pl.CostEstimate(
            flops=10 * D * D * width, bytes_accessed=24 << 20, transcendentals=0
        ),
        name="mid_grads",
    )(*lefts, *third, *rights, *texts, *pairs, stamp)


def skip_grads_kernel(count, width, *refs):
    rights, lefts = refs[:count], refs[count : 2 * count]
    input_ref, gain_ref, out_ref = refs[2 * count :]
    product = sum(kernel_dot(left[...], right[...]) for left, right in zip(lefts, rights))
    quarter = width // (2 * count)
    product = jnp.transpose(product)
    group_rows = count * quarter
    rest = out_ref.shape[1] - 5 * width - gain_ref.shape[1]
    for group in range(product.shape[0] // width):
        rows = slice(group * group_rows, (group + 1) * group_rows)
        halves = [
            jnp.concatenate(
                [
                    product[start : start + quarter]
                    for start in (
                        group * width + (2 * k + part) * quarter for k in range(count)
                    )
                ],
                axis=0,
            )
            for part in range(2)
        ]
        block = [input_ref[rows, :].astype(f32), *halves, gain_ref[rows, :]]
        block.append(jnp.zeros((group_rows, rest), f32))
        out_ref[rows, :] = jnp.concatenate(block, axis=1).astype(bf16)


def skip_grads_bucket(lefts, rights, inputs, gains):
    count, width = len(lefts), lefts[0].shape[0]
    columns = 5 * width + -5 * width % 128
    return pl.pallas_call(
        functools.partial(skip_grads_kernel, count, width),
        out_shape=jax.ShapeDtypeStruct((D, columns), bf16),
        grid=(2,),
        in_specs=[pl.BlockSpec((rights[0].shape[0], D), lambda g: (0, g))] * count
        + [pl.BlockSpec(lefts[0].shape, lambda g: (0, 0))] * count
        + [pl.BlockSpec((D // 2, member.shape[1]), lambda g: (g, 0)) for member in (inputs, gains)],
        out_specs=pl.BlockSpec((D // 2, columns), lambda g: (g, 0)),
        compiler_params=pltpu.CompilerParams(vmem_limit_bytes=VMEM_LIMIT),
        cost_estimate=pl.CostEstimate(
            flops=4 * D * width * count * 256, bytes_accessed=16 << 20, transcendentals=0
        ),
        name="skip_grads",
    )(*rights, *lefts, inputs, gains)


def finish_kernel(factor_ref, blocks_ref, skip_ref, input_ref, gain_ref):
    factor = factor_ref[0, 0]
    count, shard, _ = blocks_ref.shape
    width = skip_ref.shape[1] // count
    blocks = [blocks_ref[k].astype(f32) * factor for k in range(count)]
    for part in range(2):
        skip_ref[part * shard : (part + 1) * shard, :] = jnp.concatenate(
            [block[:, (3 + part) * width : (4 + part) * width] for block in blocks], axis=1
        )
    gain_ref[...] = sum(block[:, 5 * width : 5 * width + 4] for block in blocks)
    input_ref[...] = jnp.concatenate(
        [
            block[:, part * width : (part + 1) * width]
            for part in range(3)
            for block in blocks
        ],
        axis=1,
    )


def finish_head(blocks, factor):
    count, shard, _ = blocks.shape
    return pl.pallas_call(
        finish_kernel,
        out_shape=(
            jax.ShapeDtypeStruct((2 * shard, D), f32),
            jax.ShapeDtypeStruct((shard, 3 * D), f32),
            jax.ShapeDtypeStruct((shard, 4), f32),
        ),
        in_specs=[SMEM_WHOLE, VMEM_WHOLE],
        out_specs=[VMEM_WHOLE] * 3,
        compiler_params=pltpu.CompilerParams(vmem_limit_bytes=VMEM_LIMIT),
        cost_estimate=pl.CostEstimate(flops=1, bytes_accessed=2 << 20, transcendentals=0),
        name="finish_head",
    )(factor.reshape(1, 1), blocks)


def norm_rows(value):
    centred = value - jnp.mean(value, axis=0, keepdims=True)
    scale = lax.rsqrt(jnp.mean(centred * centred, axis=0, keepdims=True) + epsilon)
    return centred * scale, scale


def norm_rows_back(normed, scale, grad):
    return scale * (
        grad
        - jnp.mean(grad, axis=0, keepdims=True)
        - normed * jnp.mean(grad * normed, axis=0, keepdims=True)
    )


def fetch(sources, targets, sems, base):
    copies = [
        pltpu.make_async_copy(source, target, sems.at[base + k])
        for k, (source, target) in enumerate(zip(sources, targets))
    ]
    for copy in copies:
        copy.start()
    return copies


def mix_kernel(count, *refs):
    index_ref, bucket_ref = refs[:2]
    pieces = refs[2 : 2 + count]
    out_ref, weight = refs[-2:]
    width = weight.shape[1]
    half = width // 2
    for group in range(weight.shape[0] // width):
        for part in range(2):
            start = group * width + part * half
            weight[start : start + half, :] = bucket_ref[
                group * half : (group + 1) * half, (3 + part) * width : (4 + part) * width
            ]
    for piece in range(count):
        out_ref[piece ^ index_ref[0]] = kernel_dot(pieces[piece][...], weight[...]).astype(bf16)


def mix(index, bucket, pieces, width, stamps):
    count, rows = len(pieces), pieces[0].shape[0]
    return pl.pallas_call(
        functools.partial(mix_kernel, count),
        out_shape=jax.ShapeDtypeStruct((count, rows, width), bf16),
        grid=(1,),
        in_specs=[SMEM_WHOLE, pl.BlockSpec(bucket.shape, lambda g: (0, 0))]
        + [pl.BlockSpec(pieces[0].shape, lambda g: (0, 0))] * count
        + [ANY_WHOLE] * len(stamps),
        out_specs=pl.BlockSpec((count, rows, width), lambda g: (0, 0, 0)),
        scratch_shapes=[pltpu.VMEM((2 * D, width), bf16)],
        compiler_params=pltpu.CompilerParams(vmem_limit_bytes=VMEM_LIMIT),
        cost_estimate=pl.CostEstimate(
            flops=4 * D * width * count * rows, bytes_accessed=8 << 20, transcendentals=0
        ),
        name="mix",
    )(index, bucket, *pieces, *stamps)


def mixed_rows(blocks_ref, stage):
    width = blocks_ref.shape[2]
    for block in range(blocks_ref.shape[0]):
        turned = jnp.transpose(blocks_ref[block].astype(f32))
        stage[block * width : (block + 1) * width, :] = turned
    return stage[...]


def start_kernel(blocks_ref, gain_ref, shift_ref, base_ref, normed_ref, stage):
    base = norm_rows(mixed_rows(blocks_ref, stage))[0] * gain_ref[:, 0:1]
    base_ref[...] = base
    normed = norm_rows(base)[0] * gain_ref[:, 1:2] + shift_ref[...]
    normed_ref[...] = normed.astype(bf16)


def start_forward(blocks, gains, shift):
    tokens = blocks.shape[1]
    return pl.pallas_call(
        start_kernel,
        out_shape=(
            jax.ShapeDtypeStruct((D, tokens), f32),
            jax.ShapeDtypeStruct((D, tokens), bf16),
        ),
        in_specs=[VMEM_WHOLE] * 3,
        out_specs=[VMEM_WHOLE] * 2,
        scratch_shapes=[pltpu.VMEM((D, tokens), f32)],
        compiler_params=pltpu.CompilerParams(vmem_limit_bytes=VMEM_LIMIT),
        cost_estimate=pl.CostEstimate(flops=1, bytes_accessed=8 << 20, transcendentals=0),
        name="start_forward",
    )(blocks, gains, shift)


def start_back_kernel(
    blocks_ref, gain_ref, base_ref, mid_grad_ref, grad_ref, out_ref, sums_ref, stage
):
    normed, scale = norm_rows(base_ref[...])
    grad = grad_ref[...]
    sums_ref[:, 1:2] = jnp.sum(grad * normed, axis=1, keepdims=True)
    sums_ref[:, 2:3] = jnp.sum(grad, axis=1, keepdims=True)
    base_grad = mid_grad_ref[...] + norm_rows_back(normed, scale, grad * gain_ref[:, 1:2])
    normed, scale = norm_rows(mixed_rows(blocks_ref, stage))
    sums_ref[:, 0:1] = jnp.sum(base_grad * normed, axis=1, keepdims=True)
    mixed_grad = norm_rows_back(normed, scale, base_grad * gain_ref[:, 0:1]).astype(bf16)
    width = out_ref.shape[1]
    for block in range(out_ref.shape[0]):
        out_ref[block] = mixed_grad[block * width : (block + 1) * width]


def start_backward(blocks, gains, base, mid_grad, grad):
    count, tokens, width = blocks.shape
    return pl.pallas_call(
        start_back_kernel,
        out_shape=(
            jax.ShapeDtypeStruct((count, width, tokens), bf16),
            jax.ShapeDtypeStruct((D, 3), f32),
        ),
        in_specs=[VMEM_WHOLE] * 5,
        out_specs=[VMEM_WHOLE] * 2,
        scratch_shapes=[pltpu.VMEM((D, tokens), f32)],
        compiler_params=pltpu.CompilerParams(vmem_limit_bytes=VMEM_LIMIT),
        cost_estimate=pl.CostEstimate(flops=1, bytes_accessed=10 << 20, transcendentals=0),
        name="start_backward",
    )(blocks, gains, base, mid_grad, grad)


def middle_forward_kernel(count, *refs):
    index_ref, attended_ref, base_ref, gain_ref, key_ref, value_ref = refs[:6]
    sources = refs[6 : 6 + 3 * count]
    (
        mid_ref,
        late_ref,
        lefts_ref,
        raw_ref,
        query_ref,
        out_ref,
        total_ref,
        ffn_ref,
    ) = refs[6 + 3 * count : 14 + 3 * count]
    weights, sems = refs[14 + 3 * count :]
    copies = fetch(sources, [weights.at[k] for k in range(3 * count)], sems, 0)
    index = index_ref[0]
    width = D // count
    heads = HEADS // count

    def rows_of_piece(piece):
        return pl.ds(pl.multiple_of((piece ^ index) * width, 32), width)

    attended = attended_ref[...]
    for piece in range(count):
        copies[piece].wait()
        rows = rows_of_piece(piece)
        mid_ref[rows, :] = base_ref[rows, :] + kernel_dot(weights[piece], attended)
    normed = (norm_rows(mid_ref[...])[0] * gain_ref[:, 2:3]).astype(bf16)
    lefts_ref[0] = normed
    for piece in range(count):
        copies[count + piece].wait()
        product = kernel_dot(weights[count + piece], normed)
        for head in range(heads):
            raw_ref[(piece ^ index) * heads + head] = product[head * HEAD : (head + 1) * HEAD]
    for head in range(HEADS):
        query = norm_rows(raw_ref[head])[0].astype(bf16)
        query_ref[head] = query
        attention = text_weights(key_ref[head], query)
        totals = jnp.sum(attention, axis=0, keepdims=True)
        out = kernel_dot(value_ref[head], attention.astype(bf16)) / totals
        out_ref[head * HEAD : (head + 1) * HEAD, :] = out
        total_ref[head] = totals
    crossed = out_ref[...].astype(bf16)
    lefts_ref[1] = crossed
    for piece in range(count):
        copies[2 * count + piece].wait()
        rows = rows_of_piece(piece)
        late_ref[rows, :] = mid_ref[rows, :] + kernel_dot(weights[2 * count + piece], crossed)
    ffn_ref[...] = (norm_rows(late_ref[...])[0] * gain_ref[:, 3:4]).astype(bf16)


def middle_forward(index, attended, base, gains, keys, values, weights):
    count = len(weights) // 3
    tokens = attended.shape[1]
    stream = jax.ShapeDtypeStruct((D, tokens), f32)
    by_head = (HEADS, HEAD, tokens)
    return pl.pallas_call(
        functools.partial(middle_forward_kernel, count),
        out_shape=(
            stream,
            stream,
            jax.ShapeDtypeStruct((2, D, tokens), bf16),
            jax.ShapeDtypeStruct(by_head, f32),
            jax.ShapeDtypeStruct(by_head, bf16),
            stream,
            jax.ShapeDtypeStruct((HEADS, 1, tokens), f32),
            jax.ShapeDtypeStruct((D, tokens), bf16),
        ),
        in_specs=[SMEM_WHOLE] + [VMEM_WHOLE] * 5 + [ANY_WHOLE] * (3 * count),
        out_specs=[VMEM_WHOLE] * 8,
        scratch_shapes=[
            pltpu.VMEM((3 * count, D // count, D), bf16),
            pltpu.SemaphoreType.DMA((3 * count,)),
        ],
        compiler_params=pltpu.CompilerParams(vmem_limit_bytes=VMEM_LIMIT),
        cost_estimate=pl.CostEstimate(
            flops=10 * D * D * tokens, bytes_accessed=24 << 20, transcendentals=0
        ),
        name="middle_forward",
    )(index, attended, base, gains, keys, values, *weights)


def middle_backward_kernel(count, stamps, *refs):
    (
        index_ref,
        ffn_grad_ref,
        out_grad_ref,
        late_ref,
        mid_ref,
        gain_ref,
        query_ref,
        key_ref,
        value_ref,
        out_ref,
        total_ref,
        raw_ref,
        text_ref,
    ) = refs[:13]
    sources = refs[13 : 13 + 3 * count]
    (
        mid_grad_ref,
        attended_grad_ref,
        rights_ref,
        pairs_ref,
        gain_grad_ref,
    ) = refs[13 + stamps + 3 * count : 18 + stamps + 3 * count]
    weights, stage, rounded, sems = refs[18 + stamps + 3 * count :]
    order = [2, 1, 0]
    copies = []
    for place in order:
        copies += fetch(
            sources[place * count : (place + 1) * count],
            [weights.at[place * count + k] for k in range(count)],
            sems,
            place * count,
        )
    index = index_ref[0]
    width = D // count

    def through(place, turn, part):
        total = 0.0
        for piece in range(count):
            copies[turn * count + piece].wait()
            rows = pl.ds(pl.multiple_of((piece ^ index) * width, 32), width)
            value = rounded[rows, :]
            rights_ref[piece, part] = value
            total = total + kernel_dot(flip(value), weights[place * count + piece])
        return jnp.transpose(total)

    normed, scale = norm_rows(late_ref[...])
    grad = ffn_grad_ref[...]
    gain_grad_ref[:, 1:2] = jnp.sum(grad * normed, axis=1, keepdims=True)
    late_grad = out_grad_ref[...].astype(f32) + norm_rows_back(
        normed, scale, grad * gain_ref[:, 3:4]
    )
    mid_grad_ref[...] = late_grad
    rounded[...] = late_grad.astype(bf16)
    stage[...] = through(2, 0, 1).astype(bf16).astype(f32)
    key_grads, value_grads = [], []
    for head in range(HEADS):
        rows = slice(head * HEAD, (head + 1) * HEAD)
        query, keys = query_ref[head], key_ref[head]
        grad = stage[rows, :]
        inverse = 1.0 / total_ref[head]
        scaled = (grad * inverse).astype(bf16)
        total_grad = -jnp.sum(grad * out_ref[rows, :], axis=0, keepdims=True) * inverse
        attention = text_weights(keys, query)
        weight_grad = kernel_dot(flip(value_ref[head]), scaled)
        score_grad = (attention * (weight_grad + total_grad)).astype(bf16)
        query_grad = (kernel_dot(keys, score_grad) * SCALING).astype(bf16).astype(f32)
        key_grad = (kernel_dot(query, score_grad, 1, 1) * SCALING).astype(bf16).astype(f32)
        key_grads.append(norm_rows_back(*norm_rows(text_ref[head]), key_grad))
        value_grads.append(kernel_dot(scaled, attention.astype(bf16), 1, 1))
        normed, scale = norm_rows(raw_ref[head])
        stage[rows, :] = norm_rows_back(normed, scale, query_grad)
    per = 2 * HEADS // count
    grads = key_grads + value_grads
    for part in range(count):
        block = jnp.concatenate(grads[part * per : (part + 1) * per], axis=0)
        pairs_ref[part ^ index] = block.astype(bf16)
    rounded[...] = stage[...].astype(bf16)
    grad = through(1, 1, 0)
    normed, scale = norm_rows(mid_ref[...])
    gain_grad_ref[:, 0:1] = jnp.sum(grad * normed, axis=1, keepdims=True)
    mid_grad = mid_grad_ref[...] + norm_rows_back(normed, scale, grad * gain_ref[:, 2:3])
    mid_grad_ref[...] = mid_grad
    rounded[...] = mid_grad.astype(bf16)
    attended_grad_ref[...] = through(0, 2, 2).astype(bf16)


def middle_backward(index, arrays, weights, stamps):
    count = len(weights) // 3
    tokens = arrays[0].shape[1]
    rounded = jax.ShapeDtypeStruct((D, tokens), bf16)
    width = D // count
    return pl.pallas_call(
        functools.partial(middle_backward_kernel, count, len(stamps)),
        out_shape=(
            jax.ShapeDtypeStruct((D, tokens), f32),
            rounded,
            jax.ShapeDtypeStruct((count, 3, width, tokens), bf16),
            jax.ShapeDtypeStruct((count, 2 * width, TEXT_PAD), bf16),
            jax.ShapeDtypeStruct((D, 2), f32),
        ),
        in_specs=[SMEM_WHOLE]
        + [VMEM_WHOLE] * 12
        + [ANY_WHOLE] * (3 * count + len(stamps)),
        out_specs=[VMEM_WHOLE] * 5,
        scratch_shapes=[
            pltpu.VMEM((3 * count, D // count, D), bf16),
            pltpu.VMEM((D, tokens), f32),
            pltpu.VMEM((D, tokens), bf16),
            pltpu.SemaphoreType.DMA((3 * count,)),
        ],
        compiler_params=pltpu.CompilerParams(vmem_limit_bytes=VMEM_LIMIT),
        cost_estimate=pl.CostEstimate(
            flops=14 * D * D * tokens, bytes_accessed=30 << 20, transcendentals=0
        ),
        name="middle_backward",
    )(index, *arrays, *weights, *stamps)


GELU_SCALE = math.sqrt(2.0 / math.pi)


def ffn_kernel(count, stamps, *refs):
    inputs, grads = refs[:count], refs[count : 2 * count]
    expand_ref, reduce_ref = refs[2 * count : 2 * count + 2]
    hidden_ref, expand_in_ref, *outputs = refs[2 * count + 2 + stamps :]
    back_refs = outputs[:count]
    value_sc, grad_sc, back_sc = outputs[count:]
    step, steps = pl.program_id(0), pl.num_programs(0)
    tokens = inputs[0].shape[1]

    @pl.when(step == 0)
    def _():
        for piece in range(count):
            rows = slice(piece * tokens, (piece + 1) * tokens)
            value_sc[rows, :] = flip(inputs[piece][...])
            grad_sc[rows, :] = flip(grads[piece][...])

    weight = expand_ref[...]
    for half in range(2):
        rows = slice(half * count * tokens // 2, (half + 1) * count * tokens // 2)
        plain = kernel_dot(value_sc[rows, :], weight)
        square = plain * plain
        curve = jnp.tanh(plain * (GELU_SCALE + (GELU_SCALE * 0.044715) * square))
        above, half_plain = 1.0 + curve, 0.5 * plain
        hidden_ref[rows, :] = (half_plain * above).astype(bf16)
        steep = GELU_SCALE + (GELU_SCALE * 3.0 * 0.044715) * square
        slope = above * (0.5 + half_plain * (1.0 - curve) * steep)
        expand_in_ref[rows, :] = (kernel_dot(grad_sc[rows, :], reduce_ref[...]) * slope).astype(
            bf16
        )
    for piece in range(count):
        rows = slice(piece * tokens, (piece + 1) * tokens)
        part = kernel_dot(weight, expand_in_ref[rows, :], 1, 1)

        @pl.when(step == 0)
        def _():
            back_sc[piece] = part

        @pl.when((step > 0) & (step < steps - 1))
        def _():
            back_sc[piece] += part

        @pl.when(step == steps - 1)
        def _():
            back_refs[piece][...] = (back_sc[piece] + part).astype(bf16)


def feed_forward(inputs, grads, bucket, stamps):
    count = len(inputs)
    tokens, width = inputs[0].shape[1], bucket.shape[1] // 2
    steps = 3
    chunk = width // steps
    by_hidden = jax.ShapeDtypeStruct((count * tokens, width), bf16)
    by_piece = jax.ShapeDtypeStruct((D, tokens), bf16)
    whole = pl.BlockSpec((D, tokens), lambda step: (0, 0))
    hidden_spec = pl.BlockSpec((count * tokens, chunk), lambda step: (0, step))
    return pl.pallas_call(
        functools.partial(ffn_kernel, count, len(stamps)),
        out_shape=(by_hidden, by_hidden) + (by_piece,) * count,
        grid=(steps,),
        in_specs=[whole] * (2 * count)
        + [pl.BlockSpec((D, chunk), lambda step, k=k: (0, k * steps + step)) for k in range(2)]
        + [ANY_WHOLE] * len(stamps),
        out_specs=[hidden_spec, hidden_spec] + [whole] * count,
        scratch_shapes=[
            pltpu.VMEM((count * tokens, D), bf16),
            pltpu.VMEM((count * tokens, D), bf16),
            pltpu.VMEM((count, D, tokens), f32),
        ],
        compiler_params=pltpu.CompilerParams(vmem_limit_bytes=VMEM_LIMIT),
        cost_estimate=pl.CostEstimate(
            flops=6 * D * count * tokens * width,
            bytes_accessed=24 << 20,
            transcendentals=count * tokens * width,
        ),
        name="feed_forward",
    )(*inputs, *grads, bucket, bucket, *stamps)


def reduce_kernel(count, hidden_ref, reduce_ref, stamp_ref, *outputs):
    tokens = hidden_ref.shape[0] // count
    for piece in range(count):
        hidden = hidden_ref[piece * tokens : (piece + 1) * tokens, :]
        outputs[piece][...] = kernel_dot(reduce_ref[...], hidden, 1, 1).astype(bf16)


def reduce_parts(hidden, bucket, stamp, count):
    width = hidden.shape[1]
    tokens = hidden.shape[0] // count
    by_piece = jax.ShapeDtypeStruct((D, tokens), bf16)
    whole = pl.BlockSpec((D, tokens), lambda step: (0, 0))
    return pl.pallas_call(
        functools.partial(reduce_kernel, count),
        out_shape=(by_piece,) * count,
        grid=(1,),
        in_specs=[
            pl.BlockSpec(hidden.shape, lambda step: (0, 0)),
            pl.BlockSpec((D, width), lambda step: (0, 1)),
            ANY_WHOLE,
        ],
        out_specs=[whole] * count,
        compiler_params=pltpu.CompilerParams(vmem_limit_bytes=VMEM_LIMIT),
        cost_estimate=pl.CostEstimate(
            flops=2 * D * count * tokens * width, bytes_accessed=12 << 20, transcendentals=0
        ),
        name="reduce_parts",
    )(hidden, bucket, stamp)


def project_kernel(count, heads, *refs):
    values = refs[:count]
    weights = refs[count : count + 3]
    cos_ref, sin_ref = refs[count + 3 : count + 5]
    qkv_ref, raw_ref = refs[-2:]
    quarter = HEAD // 4
    rows = values[0].shape[1]
    for piece in range(count):
        lanes = pl.ds(piece * rows, rows)
        value = flip(values[piece][...])
        product = jnp.concatenate(
            [jnp.transpose(kernel_dot(value, weight[...])) for weight in weights], axis=0
        )
        cosine, sines = cos_ref[:, lanes], sin_ref[:, lanes]
        cos_row, cos_col = cosine[:quarter], cosine[quarter:]
        sin_row, sin_col = sines[:quarter], sines[quarter:]
        for part in range(3):
            for head in range(heads):
                start = (part * heads + head) * HEAD
                raw = product[start : start + HEAD]
                if part == 2:
                    qkv_ref[head, part, :, lanes] = raw.astype(bf16)
                    continue
                raw_ref[head, part, :, lanes] = raw
                normed = head_norm(raw)
                one, two, three, four = (
                    normed[k * quarter : (k + 1) * quarter] for k in range(4)
                )
                turned = jnp.concatenate(
                    [
                        one * cos_row - two * sin_row,
                        one * sin_row + two * cos_row,
                        three * cos_col - four * sin_col,
                        three * sin_col + four * cos_col,
                    ],
                    axis=0,
                )
                qkv_ref[head, part, :, lanes] = turned.astype(bf16)


def project(values, bucket, offset, heads, cosine, sines, stamps):
    count, rows = len(values), values[0].shape[1]
    third = (3 * heads * HEAD + 383) // 384 * 128
    columns = count * rows
    full = [pl.BlockSpec(member.shape, lambda g: (0, 0)) for member in (*values, cosine, sines)]
    return pl.pallas_call(
        functools.partial(project_kernel, count, heads),
        out_shape=(
            jax.ShapeDtypeStruct((heads, 3, HEAD, columns), bf16),
            jax.ShapeDtypeStruct((heads, 2, HEAD, columns), f32),
        ),
        grid=(1,),
        in_specs=full[:count]
        + [
            pl.BlockSpec((D, third), lambda g, k=k: (0, offset // third + k)) for k in range(3)
        ]
        + full[count:]
        + [ANY_WHOLE] * len(stamps),
        out_specs=[
            pl.BlockSpec((heads, 3, HEAD, columns), lambda g: (0, 0, 0, 0)),
            pl.BlockSpec((heads, 2, HEAD, columns), lambda g: (0, 0, 0, 0)),
        ],
        compiler_params=pltpu.CompilerParams(vmem_limit_bytes=VMEM_LIMIT),
        cost_estimate=pl.CostEstimate(
            flops=6 * columns * D * heads * HEAD, bytes_accessed=12 << 20, transcendentals=0
        ),
        name="project",
    )(*values, bucket, bucket, bucket, cosine, sines, *stamps)


def shards(
    tokens,
    skip_in,
    timestep,
    captions,
    null_mask,
    lengths,
    cotangent,
    skip_weight,
    shift_weight,
    self_input,
    self_output,
    cross_query,
    cross_pairs,
    cross_output,
    expand_weight,
    reduce_weight,
    null_caption,
    norm_gains,
):
    sp_count, cp_count = lax.axis_size("sp"), lax.axis_size("cp")
    dp_count = lax.axis_size("dp")
    dp_index, sp_index, cp_index = (lax.axis_index(name) for name in EVERY)
    place = (dp_index * sp_count + sp_index) * cp_count + cp_index
    packs, rows = tokens.shape[0], tokens.shape[1]
    held = packs * rows
    chunk = cp_count * rows
    group_heads = HEADS // cp_count
    pairs_dev = packs * group_heads // sp_count
    all_packs = lengths.shape[0]

    def lanes(value):
        spare = -value.shape[-1] % 128
        return jnp.pad(value, [(0, 0)] * (value.ndim - 1) + [(0, spare)])

    def split_columns(weight):
        columns = weight.shape[1] // cp_count
        blocks = jnp.swapaxes(weight.reshape(weight.shape[0], cp_count, columns), 0, 1)
        return trade_cp(blocks).reshape(cp_count * weight.shape[0], columns)

    def send_columns(weights):
        blocks = [
            jnp.concatenate(
                [jnp.split(weight, cp_count, axis=1)[k] for weight in weights], axis=1
            )
            for k in range(cp_count)
        ]
        return jnp.concatenate(send_cp(blocks), axis=0)

    def order_heads(weight):
        split = weight.reshape(weight.shape[0], 3, cp_count, -1)
        return jnp.swapaxes(split, 1, 2).reshape(weight.shape)

    def restore_heads(weight):
        split = weight.reshape(weight.shape[0], cp_count, 3, -1)
        return jnp.swapaxes(split, 1, 2).reshape(weight.shape)

    def pack(parts):
        return jnp.concatenate([lanes(part) for part in parts], axis=1)

    def unpack(bucket, widths):
        start, parts = 0, []
        for width in widths:
            parts.append(bucket[:, start : start + width])
            start += width + -width % 128
        return parts

    width = D // cp_count
    ff_width = expand_weight.shape[1] // cp_count
    group_rows = cp_count * self_output.shape[0]
    group_text = cp_count * cross_pairs.shape[0]
    head_widths = (width, width, 3 * width)
    mid_widths = (width, width, width, 2 * width)

    def gather_group(bucket):
        return lax.all_gather(bucket, GROUP, axis=0, tiled=True)

    skip_cols = split_columns(skip_weight)
    plain = rows == CELL and packs == 1 and group_rows % 16 == 0
    gain_columns = norm_gains.shape[1]
    shard = self_output.shape[0]
    fill = -3 * width % 128
    input_blocks = order_heads(self_input).reshape(shard, cp_count, 3 * width)
    input_blocks = jnp.swapaxes(jnp.pad(input_blocks, ((0, 0), (0, 0), (0, fill))), 0, 1)
    spare = jnp.pad(jnp.transpose(norm_gains), ((0, 0), (3 * width, fill - 4)))
    input_blocks = trade_cp(input_blocks + spare)
    input_blocks = input_blocks.reshape(group_rows, -1)
    if plain:
        tail = 3 * width + -5 * width % 128
        head_bucket = jnp.concatenate(
            [
                input_blocks[:, : 3 * width],
                skip_cols[:group_rows],
                skip_cols[group_rows:],
                input_blocks[:, 3 * width : tail],
            ],
            axis=1,
        )
    else:
        head_bucket = jnp.concatenate(
            [pack([skip_cols[:group_rows], skip_cols[group_rows:]]), input_blocks], axis=1
        )
    three = send_columns(
        tuple(after(member, head_bucket) for member in (self_output, cross_query, cross_output))
    )
    joined = jnp.concatenate([tokens.reshape(held, D), skip_in.reshape(held, D)], axis=1)
    joined_all = pieces_cp(after(joined, head_bucket))
    expand_weight = after(expand_weight, joined_all[-2])
    reduce_weight = after(reduce_weight, joined_all[-2])
    pairs_cols = send_columns((after(cross_pairs, head_bucket),))
    if plain:
        mid_bucket = lanes(jnp.concatenate([three, fold_rows(pairs_cols)], axis=1))
    else:
        pairs_cols = jnp.pad(pairs_cols, ((0, group_rows - group_text), (0, 0)))
        mid_bucket = pack(
            [three[:, :width], three[:, width : 2 * width], three[:, 2 * width :], pairs_cols]
        )
    mid_gathered = gather_group(mid_bucket)
    ff_bucket = send_columns((expand_weight, jnp.transpose(reduce_weight)))
    ff_gathered = gather_group(ff_bucket)
    expand_part, reduce_part = unpack(ff_gathered, (ff_width, ff_width))

    head_gathered = gather_group(head_bucket)
    if plain:
        input_part = head_gathered[:, : 3 * width]
        one = head_gathered[:, 3 * width : 4 * width]
        two = head_gathered[:, 4 * width : 5 * width]
        gain_start = 5 * width
    else:
        one, two, input_part = unpack(head_gathered, head_widths)
        gain_start = 2 * (width + -width % 128) + 3 * width
    skip_part = jnp.stack(
        [one.reshape(-1, group_rows, width), two.reshape(-1, group_rows, width)], axis=1
    ).reshape(2 * D, width)
    skip_part = after(skip_part, ff_bucket)
    gain_columns_t = head_gathered[:, gain_start : gain_start + 4].astype(f32)
    gain_rows = jnp.transpose(gain_columns_t)

    def times(left, full, left_dim):
        return jnp.concatenate(
            reorder_cp([dot(left, part, left_dim, 0) for part in full]), axis=1
        )

    def times_rows(full, right, right_dim):
        return jnp.concatenate(
            reorder_cp([dot(part, right, 0, right_dim) for part in full]), axis=0
        )

    def column_blocks(value):
        return jnp.split(value, cp_count, axis=1)

    def row_blocks(value):
        return jnp.split(value, cp_count, axis=0)

    def back_sum(left, full, left_dim):
        return sum(dot(block, part, left_dim, 1) for block, part in zip(left, full))

    def back_rows(full, right):
        return sum(dot(part, block, 1, 1) for part, block in zip(full, right))

    def traded(blocks):
        came = trade_cp(jnp.stack(blocks))
        return reorder_cp([came[k] for k in range(cp_count)])

    own_lengths = lax.dynamic_slice_in_dim(lengths, dp_index * packs, packs, 0)
    describe = jax.vmap(segment_info, in_axes=(0, None))
    chunk_block = jnp.arange(cp_count, dtype=jnp.int32) ^ cp_index
    chunk_pos = sp_index * chunk + (
        chunk_block[:, None] * rows + jnp.arange(rows, dtype=jnp.int32)[None, :]
    ).reshape(-1)
    turned = (cp_index * rows // CELL).reshape(1)
    _, chunk_row, chunk_col, _ = describe(own_lengths, chunk_pos)
    block_pos = jnp.arange(sp_count * cp_count, dtype=jnp.int32) * rows
    all_segments, _, _, all_valid = describe(lengths, block_pos)
    own_segments = lax.dynamic_slice_in_dim(all_segments, dp_index * packs, packs, 0)
    own_valid = lax.dynamic_slice_in_dim(all_valid, dp_index * packs, packs, 0)
    block = sp_index * cp_count + cp_index
    block_image = lax.dynamic_index_in_dim(own_segments, block, 1, keepdims=False)
    block_valid = lax.dynamic_index_in_dim(own_valid, block, 1, keepdims=False)
    token_valid = jnp.broadcast_to(block_valid[:, None], (packs, rows)).reshape(held, 1)
    pair_pack = (sp_index * pairs_dev + jnp.arange(pairs_dev, dtype=jnp.int32)) // group_heads
    first_cells, last_cells, valid_cells = jax.vmap(cell_ranges)(own_lengths)
    first_cells = jnp.take(first_cells, pair_pack, axis=0)
    last_cells = jnp.take(last_cells, pair_pack, axis=0)
    valid_cells = jnp.take(valid_cells, pair_pack, axis=0)

    times_all = after(timestep, head_bucket)
    for bit in bits_of("dp"):
        other = trade_bit(times_all, "dp", bit)
        times_all = jnp.where(
            has_bit("dp", bit),
            jnp.concatenate([other, times_all]),
            jnp.concatenate([times_all, other]),
        )
    silu_all = jax.nn.silu(times_all.astype(f32)).astype(bf16)
    shard_rows = shift_weight.shape[0]
    silu_own = lax.dynamic_slice_in_dim(silu_all, place * shard_rows, shard_rows, 2)
    slot_ids = jnp.arange(IMGS, dtype=jnp.int32)
    all_pick = (all_segments[:, :, None] == slot_ids).astype(f32)
    silu_blocks = jnp.einsum("pbi,pik->pbk", all_pick, silu_own.astype(f32), precision=highest)
    silu_blocks = jnp.swapaxes(
        silu_blocks.reshape(dp_count, packs, sp_count * cp_count, shard_rows), 1, 2
    ).reshape(-1, shard_rows)
    shifts = scatter_every(
        dot(silu_blocks.astype(bf16), shift_weight, 1, 0).reshape(-1, packs, D)
    )
    shift_rows = jnp.broadcast_to(shifts[:, None, :], (packs, rows, D)).reshape(held, D)

    image_dev = captions.shape[1]
    near = lax.dynamic_slice_in_dim(own_segments, sp_index * cp_count, cp_count, 1)
    local = jnp.clip(near - cp_index * image_dev, 0, image_dev - 1)
    caption_shard = jnp.pad(
        jnp.transpose(after(null_caption, head_bucket)), ((0, 0), (0, TEXT_PAD - TEXT))
    )
    caption_rows = caption_shard.shape[0]
    caption_full = jnp.transpose(gather_every(caption_shard).reshape(DT, TEXT_PAD))
    piece_index = cp_index.reshape(1)
    if plain:
        mixed_blocks = trade_cp(mix(piece_index, head_gathered, joined_all, width, ()))
        base_t, normed_self_t = start_forward(
            mixed_blocks, gain_columns_t, shifts.reshape(D, 1)
        )
        normed_all = pieces_cp(normed_self_t)
    else:
        mixed_all = [dot(piece, skip_part, 1, 0).astype(bf16) for piece in joined_all]
        mixed_blocks = trade_cp(jnp.stack(reorder_cp(mixed_all)))
        mixed = jnp.concatenate([mixed_blocks[k] for k in range(cp_count)], axis=1).astype(f32)
        base_stream = norm_gain(mixed, gain_rows[0])
        normed_self = (norm_gain(base_stream, gain_rows[1]) + shift_rows).astype(bf16)
        normed_all = pieces_cp(jnp.transpose(normed_self))
    cosine, sines = jax.vmap(rope_tables)(chunk_row, chunk_col)
    if plain:
        offset = 0
        qkv, raw = project(
            normed_all,
            head_gathered,
            offset,
            group_heads,
            cosine[0],
            sines[0],
            (caption_full,),
        )
        qkv, raw = qkv[None], raw[None]
        query_raw, key_raw = raw[:, :, 0], raw[:, :, 1]
    normed_all = jnp.concatenate(normed_all, axis=1)
    cosine, sines = cosine[:, None], sines[:, None]
    if not plain:
        projected = dot(input_part, normed_all, 0, 0)
        projected = jnp.transpose(
            projected.reshape(3, group_heads, HEAD, cp_count, packs, rows), (4, 1, 0, 2, 3, 5)
        ).reshape(packs, group_heads, 3, HEAD, chunk)
        query_raw, key_raw = projected[:, :, 0], projected[:, :, 1]
        queries = turn_norm(query_raw, cosine, sines).astype(bf16)
        key_rows = turn_norm(key_raw, cosine, sines).astype(bf16)
        value_rows = projected[:, :, 2].astype(bf16)
        qkv = jnp.stack([queries, key_rows, value_rows], axis=2)

    cp_ids = jnp.arange(cp_count, dtype=jnp.int32)
    turn_pick = (cp_ids[:, None] ^ cp_index) == cp_ids[None, :]
    near_turned = jnp.sum(jnp.where(turn_pick, near[0][None, :], 0), axis=1)
    near_null = jnp.sum(
        jnp.where(near_turned[:, None] == slot_ids[None, :], null_mask[0][None, :], 0), axis=1
    )
    near_null = near_null.astype(f32)[None, :]
    if plain:
        offered = offer(
            jnp.sum(jnp.where(turn_pick, local[0][None, :], 0), axis=1), captions, (qkv,)
        )
        arrived = jnp.stack(reorder_cp(exchange_cp(list(offered))))[:, None]
    else:
        offered = jnp.stack(
            [
                jnp.stack(
                    [
                        lax.dynamic_index_in_dim(captions[p], local[p, k], 0, keepdims=False)
                        for p in range(packs)
                    ]
                )
                for k in range(cp_count)
            ]
        )
        offered = jnp.pad(offered, ((0, 0), (0, 0), (0, TEXT_PAD - TEXT), (0, 0)))
        arrived = jnp.stack(send_cp([offered[k] for k in range(cp_count)]))
    own_null = jnp.take_along_axis(
        null_mask, block_image[:, None], axis=1
    )[:, 0]
    chosen = jnp.stack(
        [
            jnp.where(
                own_null[p] > 0,
                caption_full,
                lax.dynamic_index_in_dim(
                    arrived[:, p], block_image[p] // image_dev, 0, keepdims=False
                ),
            )
            for p in range(packs)
        ]
    )

    out_grad = cotangent.reshape(held, D).astype(f32) * token_valid
    out_turned = out_grad.astype(bf16)
    out_turned = turn_over(out_turned, (qkv,)) if plain else jnp.transpose(out_turned)
    out_grad = jnp.transpose(out_turned).astype(f32)
    reduce_pieces = pieces_cp(out_turned)

    def to_heads(value):
        value = value.reshape((sp_count, pairs_dev) + value.shape[2:])
        return lax.all_to_all(value, "sp", split_axis=0, concat_axis=0, tiled=True)

    def from_heads(value):
        value = lax.all_to_all(value, "sp", split_axis=0, concat_axis=0, tiled=True)
        return value.reshape((packs, group_heads) + value.shape[2:])

    if plain:
        *mid_parts, pairs_part = unpack_mid(
            mid_gathered, width, group_text, reduce_pieces[2]
        )
    else:
        output_part, query_part, cross_part, pairs_part = (
            after(part, qkv) for part in unpack(mid_gathered, mid_widths)
        )
        pairs_part = pairs_part.reshape(-1, group_rows, 2 * width)[:, :group_text].reshape(
            DT, 2 * width
        )
        mid_parts = (output_part, query_part, cross_part)
    pairs_full = pieces_cp(pairs_part)
    output_full, query_full, cross_full = (pieces_cp(part) for part in mid_parts)
    qkv = to_heads(qkv)
    out_self, totals_self, *sent = self_forward(
        qkv,
        first_cells,
        last_cells,
        turned,
        tuple(reduce_pieces) if plain else (),
        int(plain),
    )

    def to_tokens(value):
        value = value.reshape(sp_count, pairs_dev, HEAD, cp_count, rows)
        value = jnp.stack(reorder_cp([value[:, :, :, k] for k in range(cp_count)]))
        value = value.reshape(cp_count * sp_count, pairs_dev, HEAD, rows)
        value = lax.all_to_all(value, HEAD_ORDER, split_axis=0, concat_axis=0, tiled=True)
        value = value.reshape(cp_count, packs, group_heads, HEAD, rows)
        return jnp.transpose(value, (0, 2, 3, 1, 4)).reshape(D, held)

    def by_heads(value):
        value = value.reshape(cp_count, group_heads, HEAD, packs, rows)
        value = jnp.transpose(value, (0, 3, 1, 2, 4))
        value = value.reshape(cp_count * sp_count, pairs_dev, HEAD, rows)
        value = lax.all_to_all(value, HEAD_ORDER, split_axis=0, concat_axis=0, tiled=True)
        value = value.reshape(cp_count, sp_count, pairs_dev, HEAD, rows)
        value = reorder_cp([value[k] for k in range(cp_count)])
        return jnp.concatenate(value, axis=-1)

    def heads_of(value):
        value = value.reshape(HEADS, HEAD, packs, rows)
        return jnp.transpose(value, (2, 0, 1, 3)).reshape(packs * HEADS, HEAD, rows)

    def rows_of(value):
        value = value.reshape(packs, HEADS, HEAD, rows)
        return jnp.transpose(value, (1, 2, 0, 3)).reshape(D, held)

    if plain:
        attended = lax.all_to_all(
            sent[0].reshape(cp_count * sp_count, pairs_dev, HEAD, rows),
            HEAD_ORDER,
            split_axis=0,
            concat_axis=0,
            tiled=True,
        ).reshape(D, held)
    else:
        attended = to_tokens(out_self.astype(bf16))
    paired = times_rows(pairs_full, chosen.reshape(packs * TEXT_PAD, DT), 1)
    paired = jnp.moveaxis(paired.reshape(2, HEADS, HEAD, packs, TEXT_PAD), 3, 0)
    text_raw = paired[:, 0].reshape(packs * HEADS, HEAD, TEXT_PAD)
    text_keys = head_norm(text_raw).astype(bf16)
    text_values = paired[:, 1].reshape(packs * HEADS, HEAD, TEXT_PAD).astype(bf16)
    differences = jnp.array(group_differences(), jnp.int32)
    group_order = differences ^ (dp_index * sp_count + sp_index)
    if plain:
        mid_weights = (*output_full, *query_full, *cross_full)
        (
            mid_t,
            late_t,
            lefts,
            cross_raw,
            cross_queries,
            out_cross,
            totals_cross,
            normed_ffn_t,
        ) = middle_forward(
            piece_index,
            attended,
            base_t,
            gain_columns_t,
            text_keys,
            text_values,
            mid_weights,
        )
        attended_other = trade_bit(attended, "cp", 2)
        (normed_ffn_t,) = gate((normed_ffn_t,), (attended_other,))
        ffn_pieces = pieces_cp(normed_ffn_t)
        (lefts,) = gate((lefts,), (ffn_pieces[2],))
        lefts_other = trade_bit(lefts, "cp", 2)
        hidden, expand_in, *ffn_part = feed_forward(
            ffn_pieces, reduce_pieces, ff_gathered, ()
        )
    else:
        mid_stream = base_stream + times(attended, output_full, 0)
        normed_cross = norm_gain(mid_stream, gain_rows[2]).astype(bf16)
        cross_raw = heads_of(times_rows(query_full, normed_cross, 1))
        cross_queries = head_norm(cross_raw).astype(bf16)
        out_cross, totals_cross = cross_forward(cross_queries, text_keys, text_values)
        crossed = rows_of(out_cross.astype(bf16))
        late_stream = mid_stream + times(crossed, cross_full, 0)
        normed_ffn = norm_gain(late_stream, gain_rows[3]).astype(bf16)
        ffn_pieces = pieces_cp(jnp.transpose(normed_ffn))
        expanded = dot(jnp.concatenate(ffn_pieces, axis=1), expand_part, 0, 0)
        hidden = jax.nn.gelu(expanded, approximate=True).astype(bf16)

    def by_piece(value):
        value = value.astype(bf16).reshape(cp_count, held, D)
        return [value[k] for k in range(cp_count)]

    def sum_group(bucket):
        return lax.psum_scatter(bucket, GROUP, scatter_dimension=0, tiled=True)

    if not plain:
        gelu_back = jax.vjp(lambda preact: jax.nn.gelu(preact, approximate=True), expanded)[1]
        reduce_in = jnp.concatenate(reduce_pieces, axis=1)
        expand_in = gelu_back(dot(reduce_in, reduce_part, 0, 0))[0].astype(bf16)
        ffn_part = dot(expand_in, expand_part, 1, 1).astype(bf16)
        ffn_part = by_piece(ffn_part)
        block_part = by_piece(dot(hidden, reduce_part, 1, 1))
    if plain:
        keep, send = reduce_grads(reduce_pieces, hidden, group_order, ())
        first_half = trade_bit(send, *group_steps()[0][:2])
    ff_out = expand_grads(ffn_pieces, expand_in, (lefts_other,) if plain else ())
    if plain:
        ff_grads = sum_group(ff_out)
    else:
        reduce_out = dot(reduce_in, hidden, 1, 0).astype(bf16)
        ff_grads = sum_group(jnp.concatenate([ff_out, reduce_out], axis=1))
        ff_grads, reduce_sums = ff_grads[:, :ff_width], ff_grads[:, ff_width:]
    ffn_grad = scatter_cp(ffn_part)
    texts = jnp.transpose(chosen.reshape(packs * TEXT_PAD, DT))
    if plain:
        (texts,) = gate((texts,), (ff_out,))
        attended_all = [
            attended,
            trade_bit(attended, "cp", 1),
            attended_other,
            trade_bit(attended_other, "cp", 1),
        ]
        lefts = [lefts, trade_bit(lefts, "cp", 1), lefts_other, trade_bit(lefts_other, "cp", 1)]
    texts = pieces_cp(texts)
    if plain:
        mid_grad, attended_grad, rights, paired_rows, gain_pair = middle_backward(
            piece_index,
            (
                ffn_grad,
                out_turned,
                late_t,
                mid_t,
                gain_columns_t,
                cross_queries,
                text_keys,
                text_values,
                out_cross,
                totals_cross,
                cross_raw,
                text_raw,
            ),
            mid_weights,
            (ff_out, keep, send),
        )
        rights = exchange_cp([rights[k] for k in range(cp_count)])
        pairs = exchange_cp([paired_rows[k] for k in range(cp_count)])
    else:
        ffn_back = jax.vjp(norm_gain, late_stream, gain_rows[3])[1]
        late_part, gain_ffn = ffn_back(ffn_grad)
        late_grad = out_grad + late_part

        cout_in = column_blocks(late_grad.astype(bf16))
        cout_in = reorder_cp(cout_in)
        crossed_grad = heads_of(back_rows(cross_full, cout_in).astype(bf16))
        cq_grad, ck_grad, cv_grad = cross_backward(
            cross_queries, text_keys, text_values, crossed_grad, out_cross, totals_cross
        )
        cq_grad = cq_grad.astype(bf16).astype(f32)
        cross_raw_grad = rows_of(jax.vjp(head_norm, cross_raw)[1](cq_grad)[0].astype(bf16))
        cross_raw_grad = reorder_cp(row_blocks(cross_raw_grad))
        cross_norm_back = jax.vjp(norm_gain, mid_stream, gain_rows[2])[1]
        mid_part, gain_cross = cross_norm_back(
            back_sum(cross_raw_grad, query_full, 0)
        )
        mid_grad = late_grad + mid_part
        self_in = reorder_cp(column_blocks(mid_grad.astype(bf16)))
        attended_grad = back_rows(output_full, self_in).astype(bf16)
        normed_cross_t = jnp.transpose(normed_cross)
        cout_in = [jnp.transpose(member) for member in cout_in]
        self_in = [jnp.transpose(member) for member in self_in]
    if not plain:
        lefts = pieces_cp(jnp.stack([normed_cross_t, crossed]))
        attended_all = pieces_cp(attended)
    if not plain:
        rights = exchange_cp(
            [
                jnp.stack([cross, late, mid])
                for cross, late, mid in zip(cross_raw_grad, cout_in, self_in)
            ]
        )
    if plain:
        attended_grad = lax.all_to_all(
            attended_grad.reshape(cp_count * sp_count, pairs_dev, HEAD, rows),
            HEAD_ORDER,
            split_axis=0,
            concat_axis=0,
            tiled=True,
        ).reshape(cp_count, sp_count, pairs_dev, HEAD, rows)
    else:
        attended_grad = by_heads(attended_grad)
    qkv_grad = self_backward(
        qkv,
        attended_grad,
        out_self,
        totals_self,
        first_cells,
        last_cells,
        valid_cells,
        turned,
        (*pairs[1:], first_half) if plain else (),
    )
    stamp = qkv_grad
    qkv_grad = from_heads(qkv_grad)
    if not plain:
        block_out = (late_stream + scatter_cp(block_part)).astype(bf16)

    if not plain:
        ck_grad = ck_grad.astype(bf16).astype(f32)
        text_raw_grad = jax.vjp(head_norm, text_raw)[1](ck_grad)[0].astype(bf16)
        paired_grad = jnp.stack(
            [
                text_raw_grad.reshape(packs, D, TEXT_PAD),
                cv_grad.reshape(packs, D, TEXT_PAD).astype(bf16),
            ],
            axis=1,
        ).reshape(packs, 2 * D, TEXT_PAD)
        paired_rows = jnp.swapaxes(paired_grad, 0, 1).reshape(2 * D, packs * TEXT_PAD)
        paired_rows = reorder_cp(row_blocks(paired_rows))
        pairs = exchange_cp(paired_rows)
    if plain:
        mid_out = mid_grads_bucket(
            lefts, attended_all, rights, texts, pairs, stamp, dp_count * sp_count
        )
    else:
        lefts = jnp.concatenate(lefts, axis=2)
        lefts = [lefts[0], lefts[1], jnp.concatenate(attended_all, axis=1)]
        rights = jnp.concatenate(rights, axis=2)
        pairs_grad = dot(
            jnp.concatenate(texts, axis=1), jnp.concatenate(pairs, axis=1), 1, 1
        )
        pairs_grad = jnp.pad(
            pairs_grad.astype(bf16).reshape(-1, group_text, 2 * width),
            ((0, 0), (0, group_rows - group_text), (0, 0)),
        ).reshape(D, 2 * width)
        mid_out = pack(
            [dot(lefts[k], rights[k], 1, 1).astype(bf16) for k in range(3)] + [pairs_grad]
        )
    mid_grads = sum_group(mid_out)
    if plain:
        caption_grad = caption_product(near_null, pairs, pairs_part, mid_out)
    else:
        null_sum = jnp.einsum(
            "p,pnt->nt", own_null.astype(f32), paired_grad.astype(f32), precision=highest
        ).astype(bf16)
        caption_grad = sum(
            dot(part, block, 1, 0)
            for part, block in zip(pairs_full, reorder_cp(row_blocks(null_sum)))
        )
    caption_sum = caption_grad

    qkv_grad = after(qkv_grad, ff_grads)
    turn = functools.partial(turn_norm, cosine=cosine, sines=sines)
    query_raw_grad = jax.vjp(turn, query_raw)[1](qkv_grad[:, :, 0].astype(f32))[0].astype(bf16)
    key_raw_grad = jax.vjp(turn, key_raw)[1](qkv_grad[:, :, 1].astype(f32))[0].astype(bf16)
    projected_grad = jnp.stack([query_raw_grad, key_raw_grad, qkv_grad[:, :, 2]], axis=0)
    projected_grad = jnp.transpose(
        projected_grad.reshape(3, packs, group_heads, HEAD, cp_count, rows), (0, 2, 3, 4, 1, 5)
    ).reshape(3 * group_heads * HEAD, cp_count * held)
    if plain:
        normed_part = jnp.split(
            dot(input_part, projected_grad, 1, 0).astype(bf16), cp_count, axis=1
        )
    else:
        normed_part = dot(projected_grad, input_part, 0, 1).astype(bf16)
    self_input_grad = dot(normed_all, projected_grad, 1, 1).astype(bf16)
    if plain:
        block_part = reduce_parts(hidden, ff_gathered, normed_part[0], cp_count)
        block_out = jnp.transpose((late_t + scatter_cp(block_part)).astype(bf16))
    if plain:
        mixed_grad, sums = start_backward(
            mixed_blocks,
            gain_columns_t,
            base_t,
            mid_grad,
            scatter_cp([normed_part[k] for k in range(cp_count)]),
        )
        shift_grads = sums[:, 2][None]
        came = trade_cp(mixed_grad)
        mixed_pieces = reorder_cp([came[k] for k in range(cp_count)])
        head_out = skip_grads_bucket(
            mixed_pieces,
            joined_all,
            self_input_grad,
            jnp.concatenate([sums[:, :2], gain_pair], axis=1),
        )
        joined_part = [dot(piece, skip_part, 0, 1).astype(bf16) for piece in mixed_pieces]
    else:
        normed_self_grad = scatter_cp(by_piece(normed_part))
        self_norm_back = jax.vjp(norm_gain, base_stream, gain_rows[1])[1]
        base_part, gain_self = self_norm_back(normed_self_grad)
        shift_grads = jnp.sum(normed_self_grad.reshape(packs, rows, D), axis=1)
        base_grad = mid_grad + base_part
        skip_norm_back = jax.vjp(norm_gain, mixed, gain_rows[0])[1]
        mixed_grad, gain_skip = skip_norm_back(base_grad)
        mixed_pieces = traded(column_blocks(mixed_grad.astype(bf16)))
        mixed_in = jnp.concatenate(mixed_pieces, axis=0)
        skip_out = dot(jnp.concatenate(joined_all, axis=0), mixed_in, 0, 0).astype(bf16)
        skip_out = skip_out.reshape(-1, 2, shard, width)
        head_out = pack(
            [
                skip_out[:, 0].reshape(D, width),
                skip_out[:, 1].reshape(D, width),
                self_input_grad,
            ]
        )
        joined_part = dot(mixed_in, skip_part, 1, 1).astype(bf16).reshape(cp_count, held, 2 * D)
        joined_part = [joined_part[k] for k in range(cp_count)]
    head_grads = sum_group(head_out)
    if plain:
        reduce_sums = scatter_group_halves(
            keep, send, first_half, (mid_out, normed_part[0], head_out)
        )
    caption_grad = scatter_every(
        after(caption_sum, head_out).astype(bf16).reshape(-1, caption_rows, TEXT_PAD)
    )
    joined_grad = scatter_cp(joined_part)

    shift_grads = after(shift_grads, head_out)
    if not plain:
        gains_part = jnp.stack([gain_skip, gain_self, gain_cross, gain_ffn])
        gains_grad = scatter_every(jnp.swapaxes(gains_part.reshape(4, -1, gain_columns), 0, 1))
    shift_weight_grad = lax.dot_general(
        silu_blocks,
        send_every(shift_grads).reshape(-1, D),
        (((0,), (0,)), ((), ())),
        precision=highest,
        preferred_element_type=f32,
    )

    factor = all_packs * PACK / jnp.sum(lengths).astype(f32)

    def join_columns(bucket, widths, tight=False):
        blocks = jnp.stack(send_cp(jnp.split(bucket, cp_count, axis=0)))
        start, parts = 0, []
        for size in widths:
            part = jnp.swapaxes(blocks[:, :, start : start + size], 0, 1)
            parts.append(part.astype(f32) * factor)
            start += size if tight else size + -size % 128
        return parts

    def whole(part):
        return part.reshape(part.shape[0], -1)

    mid_grads = after(mid_grads, head_out)
    (expand_out,) = join_columns(after(ff_grads, head_out), (ff_width,))
    (reduce_out,) = join_columns(reduce_sums, (ff_width,))
    if plain:
        cross_query_out, cross_out_out, self_out_out = join_columns(
            mid_grads[:, : 3 * width], (width, width, width), True
        )
        folded = 2 * width * DT // D
        (pairs_out,) = join_columns(
            unfold_rows(mid_grads[:, 3 * width : 3 * width + folded]), (2 * width,)
        )
    else:
        cross_query_out, cross_out_out, self_out_out = join_columns(
            mid_grads[:, : 3 * (width + -width % 128)], (width, width, width)
        )
        (pairs_out,) = join_columns(
            mid_grads[:group_text, 3 * (width + -width % 128) :], (2 * width,)
        )
    if plain:
        skip_out, input_out, gains_grad = finish_head(
            trade_cp(head_grads.reshape(cp_count, shard, -1)), factor
        )
        gains_grad = jnp.transpose(gains_grad)
    else:
        one, two, input_out = join_columns(head_grads, head_widths)
        skip_out = jnp.concatenate([whole(one), whole(two)], axis=0)
        input_out = restore_heads(whole(input_out))
        gains_grad = gains_grad * factor

    token_shape = (packs, rows, D)
    return (
        block_out.reshape(token_shape),
        (joined_grad[:, :D] * factor).astype(bf16).reshape(token_shape),
        (joined_grad[:, D:] * factor).astype(bf16).reshape(token_shape),
        skip_out,
        shift_weight_grad * factor,
        input_out,
        whole(self_out_out),
        whole(cross_query_out),
        whole(pairs_out),
        whole(cross_out_out),
        whole(expand_out),
        jnp.transpose(whole(reduce_out)),
        jnp.transpose(caption_grad)[:TEXT].astype(f32) * factor,
        gains_grad,
    )


def solution(mesh):
    token_spec = P("dp", ("sp", "cp"), None)
    by_rows = P(EVERY, None)
    by_columns = P(None, EVERY)
    return jax.shard_map(
        shards,
        mesh=mesh,
        in_specs=(
            token_spec,
            token_spec,
            P("dp", None, None),
            P("dp", "cp", None, None),
            P("dp", None),
            P(),
            token_spec,
            by_rows,
            by_rows,
            by_rows,
            by_rows,
            by_rows,
            by_rows,
            by_rows,
            by_rows,
            by_columns,
            by_columns,
            by_columns,
        ),
        out_specs=(
            token_spec,
            token_spec,
            token_spec,
            by_rows,
            by_rows,
            by_rows,
            by_rows,
            by_rows,
            by_rows,
            by_rows,
            by_rows,
            by_columns,
            by_columns,
            by_columns,
        ),
        check_vma=False,
    )
```
